32 devices in a mesh: dp: 4 (over z), ctx: 2 (over x), expert: 4 (over y, core).
Axes of the slice: x: 2, y: 2, z: 4, core: 2. Of those that a mesh axis runs over, the one named last changes fastest.
Arguments:
- layer_input: bfloat16 [16384, 1024], P(('dp', 'ctx', 'expert')), may hold values from -6 to 6
- attn_gain: float32 [1024], replicated, may hold values from 0.5 to 1.5
- qkv_weight: bfloat16 [1024, 3072], replicated, may hold values from -0.1875 to 0.1875
- out_weight: bfloat16 [1024, 1024], replicated, may hold values from -1.5 to 1.5
- bias_table: float32 [32, 16], P(None, 'expert'), may hold values from -4 to 4
- moe_gain: float32 [1024], replicated, may hold values from 0.5 to 1.5
- router_weight: bfloat16 [1024, 4], replicated, may hold values from -0.125 to 0.125
- expert_in: bfloat16 [4, 1024, 5632], P('expert'), may hold values from -0.1875 to 0.1875
- expert_down: bfloat16 [4, 2816, 1024], P('expert'), may hold values from -0.625 to 0.625
- expert_ids: int32 [16384, 2], P(('dp', 'ctx', 'expert')), may hold values from 0 to 3, all different within a row
- fill_order: int32 [32, 1024], P(('dp', 'ctx', 'expert')), may hold values from 0 to 1023, each once within a row
- block_ids: int32 [4, 4096], P('dp'), may hold values from 0 to 15, never falling along the last dimension, each value on 1 to 512 neighbouring positions
- bucket_ids: int32 [8191], replicated, may hold values from 0 to 31
- cotangent: bfloat16 [16384, 1024], P(('dp', 'ctx', 'expert')), may hold values from -6 to 6
Outputs:
- layer_output: bfloat16 [16384, 1024], P(('dp', 'ctx', 'expert'))
- input_grad: float32 [16384, 1024], P(('dp', 'ctx', 'expert'))
- attn_gain_grad: float32 [1024], P(('dp', 'ctx', 'expert'))
- qkv_grad: float32 [1024, 3072], P(('dp', 'ctx', 'expert'))
- out_grad: float32 [1024, 1024], P(('dp', 'ctx', 'expert'))
- bias_grad: float32 [32, 16], P(('dp', 'ctx'), 'expert')
- moe_gain_grad: float32 [1024], P(('dp', 'ctx', 'expert'))
- router_grad: float32 [1024, 4], P(('dp', 'ctx', 'expert'))
- expert_in_grad: float32 [4, 1024, 5632], P('expert', ('dp', 'ctx'))
- expert_down_grad: float32 [4, 2816, 1024], P('expert', None, ('dp', 'ctx'))
The draws below stay inside these ranges and needn't reach their ends.
Inputs may be any that keep to these rules, and one draw needn't show every extreme that they name: `expert_ids`: each token's 2 expert ids differ. `fill_order`: each row is a permutation of the numbers 0 to 1023. `block_ids`: along each sequence the block number never falls and each block holds 1 to 512 positions, one exactly 512.
All inputs are finite; a program needn't handle non-finite values.
Results may differ from the reference program's by a relative error of at most 0.029.
Values may be sent and summed in bfloat16 or wider, within the bound.
A program may use at most 640 MiB of HBM per device.

```python
import math
import jax
import jax.numpy as jnp
import numpy as np
from jax import lax

D = 1024
HEADS = 16
HEAD_DIM = 64
FF = 2816
TOP = 2
NB = 32
BLOCK = 256
SEQ_LEN = 4096
SEQS = 1
EXPERTS = 4
TOK_DEV = 512
TOKENS = 16384
CAP = 320
N_DP = 4
N_CTX = 2
N_EXPERT = 4
DEVICES = 32


def plant(values, rng, least, high):
    longest = values.shape.index(max(values.shape))
    spots = []
    for shift in (0, 1):
        where = [jax.random.randint(jax.random.fold_in(rng, axis), (), 0, length) for axis, length in enumerate(values.shape)]
        where[longest] = (where[longest] + shift) % values.shape[longest]
        spots.append(tuple(where))
    return values.at[spots[0]].set(least).at[spots[1]].set(high)


def shard_levels(key, extent, pieces, low, high):
    def one(position, blocks):
        heights = jax.random.uniform(jax.random.fold_in(jax.random.fold_in(key, 6), position), (blocks,), jnp.float32, low / len(pieces), high / len(pieces))
        return jnp.repeat(jnp.exp(heights), extent[position] // blocks).reshape((-1,) + (1,) * (len(extent) - position - 1))

    gain = one(*pieces[0])
    for cut in pieces[1:]:
        gain = gain * one(*cut)
    return gain


def choose_distinct(stream_key, rows, amount, top, lift):
    sequence = jax.random.permutation(jax.random.fold_in(stream_key, 1), amount)
    favour = sequence
    for power in range(3):
        favour = favour * favour // amount
    favour = favour * lift // amount
    lots = jax.random.randint(jax.random.fold_in(stream_key, 2), (rows, amount), 0, 4096) + favour
    sure = jax.random.permutation(jax.random.fold_in(stream_key, 3), rows)[jnp.arange(amount) % rows]
    lots = jnp.where(jnp.arange(rows)[:, None] == sure[None, :], 1 << 14, lots)
    merit = lots * amount + jnp.arange(amount)
    return lax.top_k(merit.astype(jnp.int32), top)[1].astype(jnp.int32)


def length_profile(amount, total, reach, lean):
    portions = [(1 << 20) // math.isqrt(standing ** lean) + 1 for standing in range(2, amount + 1)]
    spare, holding = total - reach - (amount - 1), [1] * (amount - 1)
    while spare > 0:
        candidates = [i for i in range(amount - 1) if holding[i] < reach]
        mass, remaining = sum([portions[i] for i in candidates]), spare
        for i in candidates:
            extra = min(reach - holding[i], max(1, remaining * portions[i] // mass), spare)
            holding[i] = holding[i] + extra
            spare = spare - extra
    return np.array([reach] + holding)


def ragged_sizes(stream_key, amount, total, most, skew):
    if amount == 2:
        one = jax.random.randint(stream_key, (), max(1, total - most), min(most, total - 1) + 1)
        return jnp.stack([one, total - one])
    sizes = jnp.asarray(length_profile(amount, total, most, skew), jnp.int32)
    pairs = (amount - 1) // 2
    donor, taker = sizes[1:1 + 2 * pairs:2], sizes[2:2 + 2 * pairs:2]
    slack = jnp.minimum(donor - 1, most - taker)
    passed = jax.random.randint(jax.random.fold_in(stream_key, 1), (pairs,), 0, 1 << 20) % (slack + 1)
    sizes = sizes.at[1:1 + 2 * pairs:2].set(donor - passed).at[2:2 + 2 * pairs:2].set(taker + passed)
    return sizes[jax.random.permutation(jax.random.fold_in(stream_key, 2), amount)]


def scatter_about(stream_key, dims, scale, reach, cuts=(), dtype=jnp.bfloat16):
    array = jax.random.normal(stream_key, dims, jnp.float32) * scale
    if len(cuts) > 0:
        array = shard_levels(stream_key, dims, cuts, -0.22, 0.18) * array
    return jnp.clip(array, min=-reach, max=reach).astype(dtype)


def setup_inputs(seed: int = 0) -> dict:
    streams_of = jax.random.split(jax.random.key(seed), 15)
    layer_input = scatter_about(streams_of[0], (TOKENS, D), 1.0, 6.0, ((0, 32),))
    attn_gain = jnp.clip(1.0 + 0.1 * jax.random.normal(streams_of[1], (D,), jnp.float32), 0.5, 1.5)
    qkv_weight = scatter_about(streams_of[2], (D, 3 * D), D ** -0.5, 0.1875)
    out_weight = scatter_about(streams_of[3], (D, D), (D // 64) ** -0.5, 1.5)
    bias_table = scatter_about(streams_of[4], (NB, HEADS), 1.0, 4.0, ((1, 4),), jnp.float32)
    moe_gain = jnp.clip(1.0 + 0.1 * jax.random.normal(streams_of[5], (D,), jnp.float32), 0.5, 1.5)
    router_weight = scatter_about(streams_of[6], (D, EXPERTS), (2 * D) ** -0.5, 0.125)
    expert_in = scatter_about(streams_of[7], (EXPERTS, D, 2 * FF), D ** -0.5, 0.1875, ((0, 4),))
    expert_down = scatter_about(streams_of[8], (EXPERTS, FF, D), (FF // 32) ** -0.5, 0.625, ((0, 4),))
    expert_ids = choose_distinct(streams_of[9], TOKENS, EXPERTS, TOP, 4096)
    fill_order = jax.vmap(lambda own: jax.random.permutation(own, TOP * TOK_DEV))(jax.random.split(streams_of[10], (N_DP * N_CTX * N_EXPERT))).reshape((N_DP * N_CTX * N_EXPERT, TOP * TOK_DEV)).astype(jnp.int32)
    block_ids = jax.vmap(lambda own: jnp.searchsorted(jnp.cumsum(ragged_sizes(own, SEQ_LEN // BLOCK, SEQ_LEN, 2 * BLOCK, 0)), jnp.arange(SEQ_LEN), side="right"))(jax.random.split(streams_of[11], (N_DP * SEQS))).reshape((N_DP * SEQS, SEQ_LEN)).astype(jnp.int32)
    bucket_ids = plant(jax.random.randint(streams_of[12], (2 * SEQ_LEN - 1,), 0, NB), jax.random.fold_in(streams_of[12], 1), 0, NB - 1).astype(jnp.int32)
    cotangent = scatter_about(streams_of[13], (TOKENS, D), 1.0, 6.0, ((0, 32),))
    return dict(layer_input=layer_input, attn_gain=attn_gain, qkv_weight=qkv_weight, out_weight=out_weight, bias_table=bias_table, moe_gain=moe_gain, router_weight=router_weight, expert_in=expert_in, expert_down=expert_down, expert_ids=expert_ids, fill_order=fill_order, block_ids=block_ids, bucket_ids=bucket_ids, cotangent=cotangent)


@jax.custom_vjp
def low(v):
    return lax.optimization_barrier(v.astype(jnp.bfloat16)).astype(jnp.float32)

@jax.custom_vjp
def low_back(v):
    return v

def low_keep(v):
    return (low(v), None)

def low_pass(kept, grad):
    return (grad,)

def back_keep(v):
    return (v, None)

def back_low(kept, grad):
    return (low(grad),)
low.defvjp(low_keep, low_pass)
low_back.defvjp(back_keep, back_low)
highest = lax.Precision.HIGHEST

def rms_scale(values, gain_vec):
    return values * lax.rsqrt(lax.optimization_barrier(jnp.mean(values * values, axis=-1, keepdims=True)) + 1e-06) * gain_vec

def slot_numbers(seq_pair):
    ids_row, order_row = seq_pair
    same_expert = ids_row[:, None] == ids_row[None, :]
    before = order_row[None, :] < order_row[:, None]
    return lax.optimization_barrier(jnp.sum((same_expert & before).astype(jnp.int32), axis=1))

def attend_head(head_in, allowed, bucket_grid):
    queries, keys_head, values_head, column = head_in
    bias_vals = column[bucket_grid]
    scores = jnp.dot(queries, keys_head.T, precision=highest) * 0.125 + bias_vals
    scores = low_back(scores)
    scores = jnp.where(allowed, scores, -1e+30)
    attention = low(jax.nn.softmax(scores, axis=-1))
    return jnp.dot(attention, values_head, precision=highest)

def attend_sequence(qkv_seq, blk_seq, table, bucket_ids):
    length = qkv_seq.shape[0]
    offsets = (jnp.arange(length)[None, :] - jnp.arange(length)[:, None] + length - 1).astype(jnp.int32)
    bucket_grid = bucket_ids[offsets]
    allowed = blk_seq[None, :] <= blk_seq[:, None]
    checked_head = jax.checkpoint(attend_head)
    head_inputs = (jnp.transpose(qkv_seq[:, 0], (1, 0, 2)), jnp.transpose(qkv_seq[:, 1], (1, 0, 2)), jnp.transpose(qkv_seq[:, 2], (1, 0, 2)), table.T)

    def one_head(head_in):
        return checked_head(head_in, allowed, bucket_grid)
    outputs = lax.map(one_head, head_inputs)
    return jnp.transpose(outputs, (1, 0, 2))

def expert_rows(triple):
    slot_rows, weight_in, weight_down = triple
    ff_width = weight_down.shape[0]
    gate_up = low_back(jnp.dot(slot_rows, weight_in, precision=highest))
    hidden = low(jax.nn.gelu(gate_up[:, :ff_width]) * gate_up[:, ff_width:])
    return low_back(low(jnp.dot(hidden, weight_down, precision=highest)))

def reference(layer_input, attn_gain, qkv_weight, out_weight, bias_table, moe_gain, router_weight, expert_in, expert_down, expert_ids, fill_order, block_ids, bucket_ids, cotangent):
    half_len = SEQ_LEN // 2
    slot_nums = lax.map(slot_numbers, (expert_ids.reshape(DEVICES, TOP * TOK_DEV), fill_order))
    slot_nums = slot_nums.reshape(TOKENS, TOP).astype(jnp.int32)
    kept_mask = slot_nums < CAP
    slot_safe = jnp.minimum(slot_nums, CAP - 1).astype(jnp.int32)
    slot_write = jnp.where(kept_mask, slot_nums, CAP).astype(jnp.int32)
    device_of = jnp.broadcast_to((jnp.arange(TOKENS) // TOK_DEV)[:, None], (TOKENS, TOP)).astype(jnp.int32)
    checked_expert = jax.checkpoint(expert_rows)

    def forward(inputs, gain_attn, qkv_w, out_w, table, gain_moe, router_w, in_w, down_w):
        normed = low(rms_scale(inputs, gain_attn))
        qkv_all = low_back(low(jnp.dot(normed, qkv_w, precision=highest)))
        qkv_all = qkv_all.reshape(N_DP, N_CTX, SEQS, half_len, 3, HEADS, HEAD_DIM)
        qkv_all = jnp.transpose(qkv_all, (0, 2, 1, 3, 4, 5, 6)).reshape(N_DP * SEQS, SEQ_LEN, 3, HEADS, HEAD_DIM)

        def attend_one(seq_pair):
            return attend_sequence(seq_pair[0], seq_pair[1], table, bucket_ids)
        mixed_out = lax.map(attend_one, (qkv_all, block_ids))
        mixed_out = mixed_out.reshape(N_DP, SEQS, N_CTX, half_len, D)
        mixed_out = jnp.transpose(mixed_out, (0, 2, 1, 3, 4)).reshape(TOKENS, D)
        mixed_out = low_back(low(mixed_out))
        branch = low_back(jnp.dot(mixed_out, out_w, precision=highest))
        middle = inputs + branch
        normed_moe = low(rms_scale(middle, gain_moe))
        logits = jnp.dot(normed_moe, router_w, precision=highest)
        probs_all = jax.nn.softmax(logits, axis=-1)
        gate_vals = jnp.take_along_axis(probs_all, expert_ids, axis=1)
        spread = jnp.broadcast_to(normed_moe[:, None, :], (TOKENS, TOP, D))
        buffer = jnp.zeros((EXPERTS, DEVICES, CAP, D), jnp.float32)
        buffer = buffer.at[expert_ids, device_of, slot_write].set(spread, mode='drop')
        buffer = low_back(buffer.reshape(EXPERTS, DEVICES * CAP, D))
        outputs = lax.map(checked_expert, (buffer, in_w, down_w))
        outputs = outputs.reshape(EXPERTS, DEVICES, CAP, D)
        picked = outputs[expert_ids, device_of, slot_safe] * kept_mask.astype(jnp.float32)[:, :, None]
        moe_sum = lax.optimization_barrier(jnp.sum(gate_vals[:, :, None] * picked, axis=1))
        return middle + moe_sum
    result, pullback = jax.vjp(forward, layer_input.astype(jnp.float32), attn_gain, qkv_weight.astype(jnp.float32), out_weight.astype(jnp.float32), bias_table, moe_gain, router_weight.astype(jnp.float32), expert_in.astype(jnp.float32), expert_down.astype(jnp.float32))
    all_grads = pullback(cotangent.astype(jnp.float32))
    return (result.astype(jnp.bfloat16), all_grads[0], all_grads[1], all_grads[2], all_grads[3], all_grads[4], all_grads[5], all_grads[6], all_grads[7], all_grads[8])
```

```python
import functools

import jax
import jax.numpy as jnp
from jax import lax
from jax.experimental import pallas as pl
from jax.experimental.pallas import tpu as pltpu
from jax.sharding import PartitionSpec as P


HEAD_DIM = 64
TOP = 2
LOG2E = 1.4426950408889634
SCALE = 0.125 * LOG2E
HIDE = -(2.0**100)
f32 = jnp.float32
bf16 = jnp.bfloat16
highest = lax.Precision.HIGHEST
NN = (((1,), (0,)), ((), ()))
NT = (((1,), (1,)), ((), ()))
TN = (((0,), (0,)), ((), ()))


def mm(left, right, dims):
    return lax.dot_general(left, right, dims, preferred_element_type=f32)


def cost(flops, bytes_accessed, transcendentals=0):
    return pl.CostEstimate(
        flops=int(flops), bytes_accessed=int(bytes_accessed), transcendentals=int(transcendentals)
    )


def fill_table(tab_ref, buck_ref, tb_ref, width, mul):
    buck = buck_ref[...]
    row = jnp.zeros(buck.shape, f32)
    for b in range(tab_ref.shape[0]):
        row = jnp.where(buck == b, tab_ref[b] * mul, row)
    for m in range(16):
        rolled = pltpu.roll(row, 8 * m, 1, stride=1, stride_axis=0)
        for c in range(width // 128 - 1):
            lo = width - 128 - 128 * c
            tb_ref[16 * c + m] = rolled[:, lo : lo + 128]


def bias_tile(tb_ref, start, rows, cols):
    parts = [
        tb_ref[pl.ds(start - 16 * c, rows // 8)].reshape(rows, 128) for c in range(cols // 128)
    ]
    return jnp.concatenate(parts, axis=1)


def attention_fwd_kernel(
    bk, order, nch_ref, tab_ref, buck_ref, kmask_ref, qmask_ref, q_ref, k_ref, v_ref,
    o_ref, lse_ref, kaug, vaug, tb,
):
    qi = pl.program_id(0)
    blocks, _, _, tok = k_ref.shape
    length = blocks * tok

    @pl.when(qi == 0)
    def _():
        fill_table(tab_ref, buck_ref, tb, 2 * length, LOG2E)
        first = lax.broadcasted_iota(jnp.int32, (16, length), 0) == 0
        vaug[HEAD_DIM:, :] = first.astype(f32).astype(bf16)
        for p in range(blocks):
            rows = slice(p * tok, (p + 1) * tok)
            kaug[rows, :] = jnp.concatenate([k_ref[order(p), 0].T, kmask_ref[rows, :]], axis=1)
            vaug[0:HEAD_DIM, rows] = v_ref[order(p), 0]

    qaug = jnp.concatenate([q_ref[0, 0], qmask_ref[...]], axis=0)
    base = (length - 128) // 8 - qi * (tok // 8)

    def step(j, carry):
        peak, acc = carry
        ks = pl.ds(pl.multiple_of(j * bk, bk), bk)
        scores = mm(kaug[ks, :], qaug, NN) * SCALE + bias_tile(tb, base + j * (bk // 8), bk, tok)
        now = jnp.maximum(peak, jnp.max(scores, axis=0, keepdims=True))
        weights = jnp.exp2(scores - now).astype(bf16)
        return now, acc * jnp.exp2(peak - now) + mm(vaug[:, ks], weights, NN)

    start = (jnp.full((1, tok), -1e37, f32), jnp.zeros((HEAD_DIM + 16, tok), f32))
    peak, acc = lax.fori_loop(0, nch_ref[qi], step, start)
    total = acc[HEAD_DIM : HEAD_DIM + 1]
    o_ref[0] = (acc[0:HEAD_DIM] / total).astype(bf16)
    lse_ref[0] = peak + jnp.log2(total)


def attention_fwd(order, chunks, table, buck, kmask, qmask, qkv, bk):
    blocks, _, dim, tok = qkv.shape
    length = blocks * tok
    return pl.pallas_call(
        functools.partial(attention_fwd_kernel, bk, order),
        grid_spec=pltpu.PrefetchScalarGridSpec(
            num_scalar_prefetch=2,
            grid=(blocks,),
            in_specs=[
                pl.BlockSpec((8, 2 * length), lambda i, *_: (0, 0)),
                pl.BlockSpec((length, 64), lambda i, *_: (0, 0)),
                pl.BlockSpec((64, tok), lambda i, *_: (0, i)),
                pl.BlockSpec((1, 1, dim, tok), lambda i, *_: (order(i), 0, 0, 0)),
                pl.BlockSpec((blocks, 1, dim, tok), lambda i, *_: (0, 1, 0, 0)),
                pl.BlockSpec((blocks, 1, dim, tok), lambda i, *_: (0, 2, 0, 0)),
            ],
            out_specs=[
                pl.BlockSpec((1, dim, tok), lambda i, *_: (order(i), 0, 0)),
                pl.BlockSpec((1, 1, tok), lambda i, *_: (i, 0, 0)),
            ],
            scratch_shapes=[
                pltpu.VMEM((length, 128), bf16),
                pltpu.VMEM((dim + 16, length), bf16),
                pltpu.VMEM((2 * length // 8 - 16, 8, 128), f32),
            ],
        ),
        out_shape=[
            jax.ShapeDtypeStruct((blocks, dim, tok), bf16),
            jax.ShapeDtypeStruct((blocks, 1, tok), f32),
        ],
        compiler_params=pltpu.CompilerParams(vmem_limit_bytes=48 << 20),
        cost_estimate=cost(2000 * length * length // 2, 4 * length * 2 * dim, length * length // 2),
        name="attention_fwd",
    )(chunks, table, buck, kmask, qmask, qkv, qkv, qkv)


def three_rows(values, rows):
    high = values.astype(bf16).astype(f32)
    mid = (values - high).astype(bf16).astype(f32)
    row = lax.broadcasted_iota(jnp.int32, (rows, values.shape[1]), 0)
    out = jnp.where(row == 0, high, jnp.where(row == 1, mid, jnp.where(row == 2, values - high - mid, 0.0)))
    return out.astype(bf16)


def attention_bwd_kernel(
    bk, order, nch_ref, tab_ref, buck_ref, kmask_ref, qmask_ref, q_ref, k_ref, v_ref, o_ref,
    do_ref, lse_ref, out_ref, off_ref, knat, kaug, vaug, tb, gb, dkacc, dvacc,
):
    qi = pl.program_id(0)
    blocks, _, _, tok = k_ref.shape
    length = blocks * tok

    @pl.when(qi == 0)
    def _():
        fill_table(tab_ref, buck_ref, tb, 2 * length, LOG2E)
        gb[...] = jnp.zeros_like(gb)
        dkacc[...] = jnp.zeros_like(dkacc)
        dvacc[...] = jnp.zeros_like(dvacc)
        three = lax.broadcasted_iota(jnp.int32, (64, length), 0) < 3
        vaug[64:128, :] = three.astype(f32).astype(bf16)
        kaug[64:128, :] = kmask_ref[...]
        for p in range(blocks):
            rows = slice(p * tok, (p + 1) * tok)
            knat[rows, :] = k_ref[order(p), 0].T
            kaug[0:64, rows] = k_ref[order(p), 0]
            vaug[0:64, rows] = v_ref[order(p), 0]

    q_t = q_ref[0, 0]
    do_t = do_ref[0]
    delta = jnp.sum(do_t.astype(f32) * o_ref[0].astype(f32), axis=0, keepdims=True)
    lse = lse_ref[0] * (1.0 / SCALE)
    blank = jnp.zeros((32, tok), bf16)
    qaug = jnp.concatenate([q_t, qmask_ref[...], three_rows(-lse, 16), blank], axis=0).T
    doaug = jnp.concatenate([do_t, three_rows(-delta, 32), blank], axis=0).T
    base = (length - 128) // 8 + qi * (tok // 8)

    def step(j, dq):
        ks = pl.ds(pl.multiple_of(j * bk, bk), bk)
        start = base - j * (bk // 8)
        probs = jnp.exp2(mm(qaug, kaug[:, ks], NN) * SCALE + bias_tile(tb, start, tok, bk))
        ds = probs * mm(doaug, vaug[:, ks], NN)
        for c in range(bk // 128):
            at = pl.ds(start - 16 * c, tok // 8)
            gb[at] += ds[:, 128 * c : 128 * c + 128].reshape(tok // 8, 8, 128)
        low = ds.astype(bf16)
        dvacc[:, ks] += mm(do_t, probs.astype(bf16), NN)
        dkacc[:, ks] += mm(q_t, low, NN)
        return dq + mm(low, knat[ks, :], NN)

    dq = lax.fori_loop(0, nch_ref[qi], step, jnp.zeros((tok, 64), f32))
    out_ref[order(qi), 0] = (dq * 0.125).T.astype(bf16)

    @pl.when(qi == blocks - 1)
    def _():
        for p in range(blocks):
            rows = slice(p * tok, (p + 1) * tok)
            out_ref[order(p), 1] = (dkacc[:, rows] * 0.125).astype(bf16)
            out_ref[order(p), 2] = dvacc[:, rows].astype(bf16)
        width = 2 * length
        total = jnp.zeros((8, width), f32)
        for m in range(16):
            tiles = [gb[16 * c + m] for c in range(width // 128 - 2, -1, -1)]
            skewed = jnp.concatenate([jnp.zeros((8, 128), f32)] + tiles, axis=1)
            total = total + (pltpu.roll(skewed, width - 8 * m, 1) if m else skewed)
        row = total[0:1]
        for s in range(1, 8):
            row = row + pltpu.roll(total[s : s + 1], width - s, 1)
        buck = buck_ref[0:1, :]
        for b in range(off_ref.shape[0]):
            mine = jnp.where(buck == b, row, 0.0)
            parts = [mine[:, 128 * c : 128 * c + 128] for c in range(width // 128)]
            while len(parts) > 1:
                parts = [x + y for x, y in zip(parts[::2], parts[1::2])]
            off_ref[b : b + 1, :] = parts[0]


def attention_bwd(order, chunks, table, buck, kmask, qmask, qkv, mixed, mixed_grad, lse, bk):
    blocks, _, dim, tok = qkv.shape
    length = blocks * tok
    one = pl.BlockSpec((1, dim, tok), lambda i, *_: (order(i), 0, 0))
    return pl.pallas_call(
        functools.partial(attention_bwd_kernel, bk, order),
        grid_spec=pltpu.PrefetchScalarGridSpec(
            num_scalar_prefetch=2,
            grid=(blocks,),
            in_specs=[
                pl.BlockSpec((8, 2 * length), lambda i, *_: (0, 0)),
                pl.BlockSpec((64, length), lambda i, *_: (0, 0)),
                pl.BlockSpec((16, tok), lambda i, *_: (0, i)),
                pl.BlockSpec((1, 1, dim, tok), lambda i, *_: (order(i), 0, 0, 0)),
                pl.BlockSpec((blocks, 1, dim, tok), lambda i, *_: (0, 1, 0, 0)),
                pl.BlockSpec((blocks, 1, dim, tok), lambda i, *_: (0, 2, 0, 0)),
                one,
                one,
                pl.BlockSpec((1, 1, tok), lambda i, *_: (i, 0, 0)),
            ],
            out_specs=[
                pl.BlockSpec((blocks, 3, dim, tok), lambda i, *_: (0, 0, 0, 0)),
                pl.BlockSpec((table.shape[0], 128), lambda i, *_: (0, 0)),
            ],
            scratch_shapes=[
                pltpu.VMEM((length, dim), bf16),
                pltpu.VMEM((128, length), bf16),
                pltpu.VMEM((128, length), bf16),
                pltpu.VMEM((2 * length // 8 - 16, 8, 128), f32),
                pltpu.VMEM((2 * length // 8 - 16, 8, 128), f32),
                pltpu.VMEM((dim, length), f32),
                pltpu.VMEM((dim, length), f32),
            ],
        ),
        out_shape=[
            jax.ShapeDtypeStruct((blocks, 3, dim, tok), bf16),
            jax.ShapeDtypeStruct((table.shape[0], 128), f32),
        ],
        compiler_params=pltpu.CompilerParams(vmem_limit_bytes=48 << 20),
        cost_estimate=cost(5000 * length * length // 2, 8 * length * 2 * dim, length * length // 2),
        name="attention_bwd",
    )(chunks, table, buck, kmask, qmask, qkv, qkv, qkv, mixed, mixed_grad, lse)


def write_groups(acc, refs):
    rows = refs[0].shape[0]
    for d, ref in enumerate(refs):
        ref[...] = acc[d * rows : (d + 1) * rows, :].astype(bf16)


def expert_fwd_kernel(
    steps, x_ref, wg_ref, wu_ref, wd_ref, h_ref, act_ref, slope_ref, *refs
):
    outs, acc = refs[:-1], refs[-1]
    f = pl.program_id(0)

    @pl.when(f == 0)
    def _():
        acc[...] = jnp.zeros_like(acc)

    x = x_ref[...]
    gate = mm(x, wg_ref[0], NN)
    up = mm(x, wu_ref[0], NN)
    square = gate * gate
    t = jnp.tanh(gate * (0.7978845608028654 + 0.035677408136300125 * square))
    half = 0.5 + 0.5 * t
    act = gate * half
    slope = half + (gate * (0.5 - 0.5 * t * t)) * (
        0.7978845608028654 + 0.10703222440890037 * square
    )
    hidden = (act * up).astype(bf16)
    h_ref[...] = hidden
    act_ref[...] = act.astype(bf16)
    slope_ref[...] = (slope * up).astype(bf16)
    acc[...] += mm(hidden, wd_ref[0], NN)

    @pl.when(f == steps - 1)
    def _():
        write_groups(acc, outs)


def expert_fwd(x, w_in, w_down, groups, tile=256):
    rows, width = x.shape
    ff = w_down.shape[1]
    steps = ff // tile
    whole = pl.BlockSpec((rows, width), lambda f: (0, 0))
    part = pl.BlockSpec((rows, tile), lambda f: (0, f))
    inner = jax.ShapeDtypeStruct((rows, ff), bf16)
    one = pl.BlockSpec((rows // groups, width), lambda f: (0, 0))
    return pl.pallas_call(
        functools.partial(expert_fwd_kernel, steps),
        grid=(steps,),
        in_specs=[
            whole,
            pl.BlockSpec((1, width, tile), lambda f: (0, 0, f)),
            pl.BlockSpec((1, width, tile), lambda f: (0, 0, f + steps)),
            pl.BlockSpec((1, tile, width), lambda f: (0, f, 0)),
        ],
        out_specs=[part, part, part] + [one] * groups,
        out_shape=[inner, inner, inner]
        + [jax.ShapeDtypeStruct((rows // groups, width), bf16)] * groups,
        scratch_shapes=[pltpu.VMEM((rows, width), f32)],
        compiler_params=pltpu.CompilerParams(vmem_limit_bytes=48 << 20),
        cost_estimate=cost(
            10 * rows * width * ff, 6 * width * ff + rows * (4 * width + 6 * ff), rows * ff
        ),
        name="expert_fwd",
    )(x, w_in, w_in, w_down)


def expert_bwd_kernel(
    steps, g_ref, gate_ref, act_ref, slope_ref, wg_ref, wu_ref, wd_ref,
    grads_ref, *refs,
):
    outs, pg, acc = refs[:-2], refs[-2], refs[-1]
    f = pl.program_id(0)

    @pl.when(f == 0)
    def _():
        pg[...] = (g_ref[...].astype(f32) * gate_ref[...]).astype(bf16)
        acc[...] = jnp.zeros_like(acc)

    hidden_grad = mm(pg[...], wd_ref[0], NT)
    dg = (slope_ref[...].astype(f32) * hidden_grad).astype(bf16)
    du = (act_ref[...].astype(f32) * hidden_grad).astype(bf16)
    grads_ref[0] = dg
    grads_ref[1] = du
    acc[...] += mm(dg, wg_ref[0], NT) + mm(du, wu_ref[0], NT)

    @pl.when(f == steps - 1)
    def _():
        write_groups(acc, outs)


def expert_bwd(g, gate, act, slope, w_in, w_down, groups, tile=256):
    rows, width = g.shape
    ff = w_down.shape[1]
    steps = ff // tile
    whole = pl.BlockSpec((rows, width), lambda f: (0, 0))
    part = pl.BlockSpec((rows, tile), lambda f: (0, f))
    one = pl.BlockSpec((rows // groups, width), lambda f: (0, 0))
    return pl.pallas_call(
        functools.partial(expert_bwd_kernel, steps),
        grid=(steps,),
        in_specs=[
            whole,
            pl.BlockSpec((rows, 1), lambda f: (0, 0)),
            part,
            part,
            pl.BlockSpec((1, width, tile), lambda f: (0, 0, f)),
            pl.BlockSpec((1, width, tile), lambda f: (0, 0, f + steps)),
            pl.BlockSpec((1, tile, width), lambda f: (0, f, 0)),
        ],
        out_specs=[pl.BlockSpec((2, rows, tile), lambda f: (0, 0, f))] + [one] * groups,
        out_shape=[jax.ShapeDtypeStruct((2, rows, ff), bf16)]
        + [jax.ShapeDtypeStruct((rows // groups, width), bf16)] * groups,
        scratch_shapes=[pltpu.VMEM((rows, width), bf16), pltpu.VMEM((rows, width), f32)],
        compiler_params=pltpu.CompilerParams(vmem_limit_bytes=48 << 20),
        cost_estimate=cost(
            10 * rows * width * ff, 6 * width * ff + rows * (4 * width + 8 * ff)
        ),
        name="expert_bwd",
    )(g, gate, act, slope, w_in, w_in, w_down)


def column_block(ref, copies, ctx, flip, a):
    blk = ref.shape[1] // copies
    low = ref[:, 2 * a * blk : (2 * a + 1) * blk]
    high = ref[:, (2 * a + 1) * blk : (2 * a + 2) * blk]
    return jnp.where(lax.rem(ctx + flip, 2) == 0, low, high)


def in_grad_kernel(copies, ctx_ref, *refs):
    n = (len(refs) - 3) // 2
    xs, gs = refs[:n], refs[n : 2 * n]
    own_ref, other_ref, xt = refs[2 * n :]
    width = xs[0].shape[1]
    blk = width // copies

    @pl.when(pl.program_id(0) == 0)
    def _():
        at = 0
        for x_ref in xs:
            rows = x_ref.shape[0]
            for flip in range(2):
                for a in range(copies // 2):
                    to = (flip * (copies // 2) + a) * blk
                    xt[to : to + blk, at : at + rows] = column_block(
                        x_ref, copies, ctx_ref[0], flip, a
                    ).T
            at += rows

    grads = jnp.concatenate([g[0] for g in gs], axis=0)
    grad = mm(xt[...], grads, NN).astype(bf16)
    own_ref[...] = grad[: width // 2]
    other_ref[...] = grad[width // 2 :]


def in_grad(ctx, xs, grads, copies, first, count, tile=256):
    width = xs[0].shape[1]
    steps = grads[0].shape[2] // tile
    total = sum(x.shape[0] for x in xs)
    half = jax.ShapeDtypeStruct((width // 2, count * tile), bf16)
    out = pl.BlockSpec((width // 2, tile), lambda f, c: (0, f))

    def at(f, c):
        return ((f + first) // steps, 0, (f + first) % steps)

    return pl.pallas_call(
        functools.partial(in_grad_kernel, copies),
        grid_spec=pltpu.PrefetchScalarGridSpec(
            num_scalar_prefetch=1,
            grid=(count,),
            in_specs=[pl.BlockSpec(x.shape, lambda f, c: (0, 0)) for x in xs]
            + [pl.BlockSpec((1, g.shape[1], tile), at) for g in grads],
            out_specs=[out, out],
            scratch_shapes=[pltpu.VMEM((width, total), bf16)],
        ),
        out_shape=[half, half],
        compiler_params=pltpu.CompilerParams(vmem_limit_bytes=48 << 20),
        cost_estimate=cost(
            4 * total * width * count * tile, 2 * (total + width) * count * tile + 2 * total * width
        ),
        name="in_grad",
    )(ctx, *xs, *grads)


def down_grad_kernel(copies, ctx_ref, *refs):
    n = (len(refs) - 3) // 3
    hs, ps, gates = refs[:n], refs[n : 2 * n], refs[2 * n : 3 * n]
    own_ref, other_ref, pg = refs[3 * n :]
    blk = ps[0].shape[1] // copies

    @pl.when(pl.program_id(0) == 0)
    def _():
        at = 0
        for p_ref, gate_ref in zip(ps, gates):
            rows = p_ref.shape[0]
            for flip in range(2):
                for a in range(copies // 2):
                    to = (flip * (copies // 2) + a) * blk
                    block = column_block(p_ref, copies, ctx_ref[0], flip, a).astype(f32)
                    pg[at : at + rows, to : to + blk] = (block * gate_ref[...]).astype(bf16)
            at += rows

    grad = mm(jnp.concatenate([h[...] for h in hs], axis=0), pg[...], TN).astype(bf16)
    for a in range(copies // 2):
        own_ref[a] = grad[:, a * blk : (a + 1) * blk]
        to = (copies // 2 + a) * blk
        other_ref[a] = grad[:, to : to + blk]


def down_grad(ctx, hs, ps, gates, copies, first, count, tile=256):
    ff = count * tile
    width = ps[0].shape[1]
    total = sum(h.shape[0] for h in hs)
    blk = width // copies
    half = jax.ShapeDtypeStruct((copies // 2, ff, blk), bf16)
    out = pl.BlockSpec((copies // 2, tile, blk), lambda f, c: (0, f, 0))
    return pl.pallas_call(
        functools.partial(down_grad_kernel, copies),
        grid_spec=pltpu.PrefetchScalarGridSpec(
            num_scalar_prefetch=1,
            grid=(count,),
            in_specs=[pl.BlockSpec((h.shape[0], tile), lambda f, c: (0, f + first)) for h in hs]
            + [pl.BlockSpec(p.shape, lambda f, c: (0, 0)) for p in ps]
            + [pl.BlockSpec(g.shape, lambda f, c: (0, 0)) for g in gates],
            out_specs=[out, out],
            scratch_shapes=[pltpu.VMEM((total, width), bf16)],
        ),
        out_shape=[half, half],
        compiler_params=pltpu.CompilerParams(vmem_limit_bytes=48 << 20),
        cost_estimate=cost(4 * total * width * ff, 2 * (total * (width + ff) + width * ff)),
        name="down_grad",
    )(ctx, *hs, *ps, *gates)


def project_kernel(x_ref, gain_ref, w_ref, normed_ref, *refs):
    outs, normed_t = refs[:-1], refs[-1]
    heads = len(outs)

    @pl.when((pl.program_id(0) == 0) & (pl.program_id(1) == 0))
    def _():
        x = x_ref[...].astype(f32)
        scale = lax.rsqrt(jnp.mean(x * x, axis=1, keepdims=True) + 1e-06)
        normed = (x * scale * gain_ref[...]).astype(bf16)
        normed_ref[...] = normed
        normed_t[...] = normed.T

    cols = w_ref.shape[1]
    tok = normed_t.shape[1]
    rows = mm(w_ref[...], normed_t[...], TN).astype(bf16)
    rows = rows.reshape(cols // (heads * HEAD_DIM), heads, HEAD_DIM, tok)
    for h in range(heads):
        outs[h][:, 0] = rows[:, h]


def project(x, gain, weight, groups, heads, cols=512):
    tok, width = x.shape
    per = cols // (heads * HEAD_DIM)
    blocks = width // cols
    return pl.pallas_call(
        project_kernel,
        grid=(3, blocks),
        in_specs=[
            pl.BlockSpec((tok, width), lambda p, j: (0, 0)),
            pl.BlockSpec((1, width), lambda p, j: (0, 0)),
            pl.BlockSpec((width, cols), lambda p, j: (0, p * blocks + j)),
        ],
        out_specs=[pl.BlockSpec((tok, width), lambda p, j: (0, 0))]
        + [pl.BlockSpec((per, 1, HEAD_DIM, tok), lambda p, j: (j, p, 0, 0))] * heads,
        out_shape=[jax.ShapeDtypeStruct((tok, width), bf16)]
        + [jax.ShapeDtypeStruct((groups, 3, HEAD_DIM, tok), bf16)] * heads,
        scratch_shapes=[pltpu.VMEM((width, tok), bf16)],
        compiler_params=pltpu.CompilerParams(vmem_limit_bytes=48 << 20),
        cost_estimate=cost(6 * tok * width * width, 6 * width * width + 10 * tok * width),
        name="project",
    )(x, gain.reshape(1, width), weight)


def input_grad_kernel(steps, x_ref, gain_ref, mid_ref, w_ref, *refs):
    grads, out_ref, acc = refs[:-2], refs[-2], refs[-1]
    step = pl.program_id(0)
    cols = w_ref.shape[1]
    tok = out_ref.shape[0]

    @pl.when(step == 0)
    def _():
        acc[...] = jnp.zeros_like(acc)

    rows = jnp.stack([g[:, 0] for g in grads], axis=1).reshape(cols, tok)
    acc[...] += mm(w_ref[...], rows, NN)

    @pl.when(step == steps - 1)
    def _():
        x = x_ref[...].astype(f32)
        scale = lax.rsqrt(jnp.mean(x * x, axis=1, keepdims=True) + 1e-06)
        dy = acc[...].T * gain_ref[...]
        pull = jnp.mean(x * dy, axis=1, keepdims=True)
        out_ref[...] = mid_ref[...] + scale * dy - x * (scale * scale * scale * pull)


def input_gradient(x, gain, middle_grad, weight, grads, cols=512):
    tok, width = x.shape
    heads = len(grads)
    per = cols // (heads * HEAD_DIM)
    blocks = width // cols
    whole = pl.BlockSpec((tok, width), lambda s: (0, 0))
    return pl.pallas_call(
        functools.partial(input_grad_kernel, 3 * blocks),
        grid=(3 * blocks,),
        in_specs=[
            whole,
            pl.BlockSpec((1, width), lambda s: (0, 0)),
            whole,
            pl.BlockSpec((width, cols), lambda s: (0, s)),
        ]
        + [
            pl.BlockSpec((per, 1, HEAD_DIM, tok), lambda s: (s % blocks, s // blocks, 0, 0))
            for _ in grads
        ],
        out_specs=whole,
        out_shape=jax.ShapeDtypeStruct((tok, width), f32),
        scratch_shapes=[pltpu.VMEM((width, tok), f32)],
        compiler_params=pltpu.CompilerParams(vmem_limit_bytes=48 << 20),
        cost_estimate=cost(6 * tok * width * width, 6 * width * width + 16 * tok * width),
        name="input_grad",
    )(x, gain.reshape(1, width), middle_grad, weight, *grads)


def rms_scale(values, gain_vec):
    return values * lax.rsqrt(jnp.mean(values * values, axis=-1, keepdims=True) + 1e-06) * gain_vec


def dot_f32(left, right, left_dim, right_dim):
    return mm(left, right, (((left_dim,), (right_dim,)), ((), ())))


def swap_blocks(blocks, axes):
    return lax.all_to_all(blocks, axes, split_axis=0, concat_axis=0, tiled=True)


def exchange(parts):
    n = len(parts)
    return [parts[0]] + [
        lax.ppermute(parts[d], "expert", [(i, i ^ d) for i in range(n)]) for d in range(1, n)
    ]


def after(value, *others):
    return lax.optimization_barrier((value, others))[0]


def attention_plan(block_row, bucket_ids, blocks, tok):
    length = blocks * tok
    pad = jnp.full((1,), -1, jnp.int32)
    buck_rev = jnp.broadcast_to(jnp.concatenate([pad, bucket_ids[::-1]])[None], (8, 2 * length))
    buck = jnp.broadcast_to(jnp.concatenate([pad, bucket_ids])[None], (8, 2 * length))
    ids = jnp.arange(16)
    hot = (block_row[None, :] == ids[:, None]).astype(bf16)
    hide = jnp.where(ids[:, None] > block_row[None, :], HIDE, 0.0).astype(bf16)
    kmask_t = jnp.concatenate(
        [hot, jnp.ones((3, length), bf16), jnp.zeros((45, length), bf16)], axis=0
    )
    qmask = jnp.concatenate([hide, jnp.zeros((48, length), bf16)], axis=0)
    last = block_row.reshape(blocks, tok)[:, -1]
    seen = jnp.sum((block_row[None, :] <= last[:, None]).astype(jnp.int32), axis=1)
    return buck_rev, buck, kmask_t.T, kmask_t, qmask, hide, seen


def shards(
    layer_input,
    attn_gain,
    qkv_weight,
    out_weight,
    bias_table,
    moe_gain,
    router_weight,
    expert_in,
    expert_down,
    expert_ids,
    fill_order,
    block_ids,
    bucket_ids,
    cotangent,
):
    tok, width = layer_input.shape
    n_dp, n_ctx, n_exp = lax.axis_size("dp"), lax.axis_size("ctx"), lax.axis_size("expert")
    groups = n_ctx * n_exp
    copies = n_dp * n_ctx
    head_exp = bias_table.shape[1]
    heads = head_exp // n_ctx
    experts = router_weight.shape[1]
    ff_width = expert_down.shape[1]
    capacity = 5 * TOP * tok // (4 * experts)
    cut = (capacity // 2 + 15) // 16 * 16
    spans = ((0, cut), (cut, capacity))
    ctx_index = lax.axis_index("ctx")
    exp_index = lax.axis_index("expert")
    ctx_arg = ctx_index.astype(jnp.int32).reshape(1)
    pair = ("expert", "ctx")
    step_k = 512

    def order(p):
        return (p % n_exp) * n_ctx + p // n_exp

    def in_swap_order(blocks):
        shape = blocks.shape
        return jnp.swapaxes(blocks.reshape((n_ctx, n_exp) + shape[1:]), 0, 1).reshape(shape)

    inputs = layer_input.astype(f32)
    normed, *parts = project(layer_input, attn_gain, qkv_weight, groups, heads)
    qkv = [swap_blocks(part, pair) for part in parts]
    table_dev = lax.dynamic_slice_in_dim(bias_table, ctx_index * heads, heads, 1)
    buck_rev, buck, kmask, kmask_t, qmask, hide, seen = attention_plan(
        block_ids[0], bucket_ids, groups, tok
    )
    chunks = (seen + step_k - 1) // step_k

    flat_ids = expert_ids.reshape(TOP * tok)
    fill_rank = fill_order.reshape(TOP * tok)
    same_expert = flat_ids[:, None] == flat_ids[None, :]
    earlier = fill_rank[None, :] < fill_rank[:, None]
    slot_of = jnp.sum((same_expert & earlier).astype(jnp.int32), axis=1)
    slots = slot_of.reshape(tok, TOP)
    choose = (expert_ids[:, :, None] == jnp.arange(experts)[None, None, :]).astype(f32)

    expert_at = jnp.bitwise_xor(jnp.arange(experts), exp_index)

    def hits(d, low, high):
        slot_at = jnp.arange(low, high)[:, None]
        return [
            (expert_at[d] == expert_ids[None, :, j]) & (slot_at == slots[None, :, j])
            for j in range(TOP)
        ]

    pick = [
        [[one.astype(bf16) for one in hits(d, low, high)] for d in range(experts)]
        for low, high in spans
    ]

    def to_slots(rows, part):
        return [
            dot_f32(first + second, rows, 1, 0).astype(bf16) for first, second in pick[part]
        ]

    forward, mixed, normed_seq = [], [], []
    slots_a = to_slots(cotangent, 0)
    slots_b = to_slots(cotangent, 1)
    qkv[0], pick, slots_a, slots_b, buck_rev, buck, kmask, kmask_t, qmask, hide = (
        lax.optimization_barrier(
            (qkv[0], pick, slots_a, slots_b, buck_rev, buck, kmask, kmask_t, qmask, hide)
        )
    )
    part_width = width // heads
    for h in range(heads):
        arg = after(qkv[h], *forward, *normed_seq)
        piece = after(normed[:, h * part_width : (h + 1) * part_width], arg)
        normed_seq.append(lax.all_gather(piece, pair, axis=0, tiled=True))
        if h == heads - 1:
            grad_a = exchange(after(slots_a, arg))
        out = attention_fwd(order, chunks, table_dev[:, h], buck_rev, kmask, qmask, arg, step_k)
        if h == heads - 1:
            out = after(out, normed_seq, grad_a)
        forward.append(out)
        mixed.append(swap_blocks(out[0], pair).reshape(groups * HEAD_DIM, tok))
    out_heads = out_weight.reshape(groups, heads, HEAD_DIM, width)
    out_weights = [out_heads[:, h].reshape(groups * HEAD_DIM, width) for h in range(heads)]
    branch = sum(dot_f32(m, w, 0, 0) for m, w in zip(mixed, out_weights))
    middle = inputs + branch
    normed_moe_f, norm_moe_back = jax.vjp(rms_scale, middle, moe_gain)
    normed_moe = normed_moe_f.astype(bf16)

    arrived = [exchange(to_slots(normed_moe, 0))]
    arrived.append(exchange(to_slots(after(normed_moe, arrived[0][0]), 1)))
    logits = jnp.dot(normed_moe.astype(f32), router_weight.astype(f32), precision=highest)
    probs = jax.nn.softmax(logits, axis=-1)
    gate_vals = jnp.sum(probs[:, None, :] * choose, axis=2)
    gate_slots = [
        [
            jnp.sum(
                first.astype(f32) * gate_vals[None, :, 0]
                + second.astype(f32) * gate_vals[None, :, 1],
                axis=1,
            )
            for first, second in part
        ]
        for part in pick
    ]
    sent_gates = [jnp.concatenate(both) for both in zip(*gate_slots)]
    gates = jnp.stack(exchange(sent_gates))

    x_a, x_b = [jnp.concatenate(part, axis=0) for part in arrived]
    gate_rows = [gates[:, low:high].reshape(-1, 1) for low, high in spans]
    grad_b = exchange(after(slots_b, x_a))
    run_a = expert_fwd(x_a, expert_in, expert_down, experts)
    run_b = expert_fwd(after(x_b, run_a, grad_b), expert_in, expert_down, experts)
    produced_a = exchange(list(run_a[3:]))
    g_a, g_b = jnp.concatenate(grad_a, axis=0), jnp.concatenate(grad_b, axis=0)
    hidden = [run_a[0], run_b[0]]
    tiles = ff_width // 256
    cuts = (0, (tiles + 1) // 2, tiles)
    g_args = after([g_a, g_b], run_b, produced_a)
    down_1 = down_grad(ctx_arg, hidden, g_args, gate_rows, copies, 0, cuts[1])
    produced_b = exchange(list(run_b[3:]))

    def ctx_sum(own, other):
        came = lax.ppermute(other, "ctx", [(0, 1), (1, 0)])
        return (own.astype(f32) + came.astype(f32)).astype(bf16)

    halves = [ctx_sum(*down_1)]
    g_args = after([g_a, g_b], down_1)
    down_2 = down_grad(ctx_arg, hidden, g_args, gate_rows, copies, cuts[1], tiles - cuts[1])
    undo_a = expert_bwd(
        after(g_a, down_2), gate_rows[0], run_a[1], run_a[2], expert_in, expert_down, experts
    )
    halves.append(ctx_sum(down_2[0], after(down_2[1], halves[0])))
    undo_b = expert_bwd(
        after(g_b, undo_a, halves[0], produced_b),
        gate_rows[1], run_b[1], run_b[2], expert_in, expert_down, experts,
    )
    grads_a = exchange(list(undo_a[1:]))
    grads_in = [undo_a[0], undo_b[0]]
    bounds = (0, 2 * tiles * 4 // 11, 2 * tiles * 8 // 11, 2 * tiles)
    xs = after([x_a, x_b], undo_b, grads_a)
    in_1 = in_grad(ctx_arg, xs, grads_in, copies, bounds[0], bounds[1] - bounds[0])
    grads_b = exchange(list(undo_b[1:]))
    xs = after([x_a, x_b], in_1, halves[1])
    in_2 = in_grad(ctx_arg, xs, grads_in, copies, bounds[1], bounds[2] - bounds[1])
    halves.append(ctx_sum(in_1[0], after(in_1[1], halves[1])))
    xs = after([x_a, x_b], in_2)
    in_3 = in_grad(ctx_arg, xs, grads_in, copies, bounds[2], bounds[3] - bounds[2])
    produced = after([produced_a, produced_b], in_3)
    row_grad = after([grads_a, grads_b], in_3)

    def from_slots(picks, slot_rows):
        rows = jnp.concatenate([one for part in slot_rows for one in part], axis=0)
        return dot_f32(jnp.concatenate([one for part in picks for one in part], axis=0), rows, 0, 0)

    first_out = from_slots([[p[0] for p in part] for part in pick], produced)
    second_out = from_slots([[p[1] for p in part] for part in pick], produced)
    normed_moe_grad = from_slots([[p[0] + p[1] for p in part] for part in pick], row_grad)
    moe_sum = gate_vals[:, 0:1] * first_out + gate_vals[:, 1:2] * second_out
    layer_output = (middle + moe_sum).astype(bf16)
    grad_out = cotangent.astype(f32)
    gate_grad = jnp.stack(
        [jnp.sum(grad_out * first_out, axis=1), jnp.sum(grad_out * second_out, axis=1)], axis=1
    )
    probs_grad = jnp.sum(gate_grad[:, :, None] * choose, axis=1)
    logits_grad = probs * (probs_grad - jnp.sum(probs * probs_grad, axis=1, keepdims=True))
    router_f = router_weight.astype(f32)
    route_grad = jnp.dot(logits_grad, router_f.T, precision=highest)
    middle_norm_grad, moe_gain_grad = norm_moe_back(normed_moe_grad + route_grad)
    middle_grad = grad_out + middle_norm_grad
    branch_grad = middle_grad.astype(bf16)
    branch_grad = after(branch_grad, halves[2])
    mixed_grad = [
        swap_blocks(
            dot_f32(w, branch_grad, 1, 1).astype(bf16).reshape(groups, HEAD_DIM, tok), pair
        )
        for w in out_weights
    ]

    out_grad = jnp.stack(
        [dot_f32(m, branch_grad, 1, 0).astype(bf16).reshape(groups, HEAD_DIM, width) for m in mixed],
        axis=1,
    ).reshape(width, width)
    wide_logits = jnp.pad(logits_grad, ((0, 0), (0, 128 - experts)))
    router_grad = lax.dot_general(
        normed_moe.astype(f32), wide_logits, (((0,), (0,)), ((), ())), precision=highest
    )
    lane = jnp.arange(128)[None, :]
    small = jnp.where(lane == experts, moe_gain_grad[:, None], router_grad).astype(bf16)
    rows_dev = width // (n_dp * groups)
    early = jnp.concatenate([out_grad, small], axis=1)
    early = early.reshape(copies, n_exp, rows_dev, width + 128)

    def sum_dp(half):
        return lax.psum_scatter(half, "dp", scatter_dimension=0, tiled=True)

    summed = [sum_dp(halves[0]), sum_dp(halves[1])]
    last_own, last_other = [sum_dp(half) for half in in_3]

    buckets = bias_table.shape[0] // copies
    lanes = -(-(3 * HEAD_DIM + 1) // 128) * 128
    backward, grads, late = [], [], []
    for h in range(heads):
        arg = after(mixed_grad[h], backward, halves, summed)
        if h == 0:
            halves.append(ctx_sum(in_2[0], after(in_2[1], arg)))
            summed.append(sum_dp(halves[2]))
            pieces = after(early, arg)
            early_parts = exchange(
                [
                    lax.dynamic_index_in_dim(
                        pieces, jnp.bitwise_xor(exp_index, d), 1, False
                    ).reshape(-1, width + 128)
                    for d in range(n_exp)
                ]
            )
            early_sum = sum(part.astype(f32) for part in early_parts).astype(bf16)
            early_half = sum_dp(early_sum).reshape(n_ctx, rows_dev, width + 128)
        else:
            arg = after(arg, early_parts, last_own, last_other)
        out, offsets = attention_bwd(
            order, chunks, table_dev[:, h], buck, kmask_t, hide, qkv[h], forward[h][0],
            arg, forward[h][1], step_k,
        )
        if h == heads - 1:
            summed.append(sum_dp(after(halves[3], arg)))
            summed.append(ctx_sum(last_own, after(last_other, arg)))
            out, offsets = after((out, offsets), grads, late, early_half, summed[4])
        backward.append(out)
        grads.append(swap_blocks(out, pair))
        columns = jnp.transpose(out, (1, 2, 0, 3)).reshape(3 * HEAD_DIM, groups * tok)
        local_grad = jnp.concatenate(
            [dot_f32(piece, columns, 0, 1) for piece in normed_seq], axis=0
        )
        table_grad = jnp.sum(offsets, axis=1)
        spread = jnp.pad(
            jnp.broadcast_to(
                table_grad.reshape(n_dp, n_ctx, 1, buckets), (n_dp, n_ctx, n_exp, buckets)
            ),
            ((0, 0), (0, 0), (0, 0), (0, rows_dev - buckets)),
        ).reshape(width, 1)
        local_grad = jnp.pad(local_grad, ((0, 0), (0, lanes - 3 * HEAD_DIM)))
        lane = jnp.arange(lanes)[None, :]
        packed = jnp.where(lane == 3 * HEAD_DIM, spread, local_grad).astype(bf16)
        late.append(sum_dp(packed))
    input_grad = input_gradient(layer_input, attn_gain, middle_grad, qkv_weight, grads)
    early_own, early_other = [
        lax.dynamic_index_in_dim(early_half, at, 0, False) for at in (ctx_index, 1 - ctx_index)
    ]
    early_rows = early_own.astype(f32) + lax.ppermute(
        early_other, "ctx", [(0, 1), (1, 0)]
    ).astype(f32)
    expert_in_grad = jnp.concatenate(summed[2:], axis=1).astype(f32)
    expert_down_grad = jnp.concatenate(summed[:2], axis=1).astype(f32)
    rows_out = swap_blocks(
        in_swap_order(jnp.concatenate(late, axis=1).reshape(groups, rows_dev, -1)), pair
    )
    late_rows = jnp.swapaxes(rows_out.reshape(groups, rows_dev, heads, lanes), 1, 2)
    qkv_grad = (
        jnp.transpose(
            late_rows[..., : 3 * HEAD_DIM].reshape(groups, heads, rows_dev, 3, HEAD_DIM),
            (2, 3, 0, 1, 4),
        )
        .reshape(rows_dev, 3 * width)
        .astype(f32)
    )
    bias_rows = lax.dynamic_slice(
        late_rows[..., 3 * HEAD_DIM], (exp_index * n_ctx, 0, 0), (n_ctx, heads, buckets)
    )
    bias_grad = bias_rows.reshape(head_exp, buckets).T.astype(f32)
    my_rows = ((lax.axis_index("dp") * n_ctx + ctx_index) * n_exp + exp_index) * rows_dev
    attn_gain_grad = jnp.sum(
        lax.dynamic_slice_in_dim(qkv_weight, my_rows, rows_dev, 0).astype(f32) * qkv_grad, axis=1
    ) / lax.dynamic_slice_in_dim(attn_gain, my_rows, rows_dev, 0)
    return (
        layer_output,
        input_grad,
        attn_gain_grad,
        qkv_grad,
        early_rows[:, :width],
        bias_grad,
        early_rows[:, width + experts],
        early_rows[:, width : width + experts],
        expert_in_grad[None],
        expert_down_grad,
    )


def solution(mesh):
    rows = P(("dp", "ctx", "expert"), None)
    return jax.shard_map(
        shards,
        mesh=mesh,
        in_specs=(
            rows,
            P(),
            P(),
            P(),
            P(None, "expert"),
            P(),
            P(),
            P("expert", None, None),
            P("expert", None, None),
            rows,
            rows,
            P("dp", None),
            P(),
            rows,
        ),
        out_specs=(
            rows,
            rows,
            P(("dp", "ctx", "expert")),
            rows,
            rows,
            P(("dp", "ctx"), "expert"),
            P(("dp", "ctx", "expert")),
            rows,
            P("expert", ("dp", "ctx"), None),
            P("expert", None, ("dp", "ctx")),
        ),
        check_vma=False,
    )
```

```python
import functools

import jax
import jax.numpy as jnp
from jax import lax
from jax.experimental import pallas as pl
from jax.experimental.pallas import tpu as pltpu
from jax.sharding import PartitionSpec as P


HEAD_DIM = 64
TOP = 2
LOG2E = 1.4426950408889634
SCALE = 0.125 * LOG2E
HIDE = -(2.0**100)
f32 = jnp.float32
bf16 = jnp.bfloat16
highest = lax.Precision.HIGHEST
NN = (((1,), (0,)), ((), ()))
NT = (((1,), (1,)), ((), ()))
TN = (((0,), (0,)), ((), ()))


def mm(left, right, dims):
    return lax.dot_general(left, right, dims, preferred_element_type=f32)


def cost(flops, bytes_accessed, transcendentals=0):
    return pl.CostEstimate(
        flops=int(flops), bytes_accessed=int(bytes_accessed), transcendentals=int(transcendentals)
    )


def fill_table(tab_ref, buck_ref, tb_ref, width, mul):
    buck = buck_ref[...]
    row = jnp.zeros(buck.shape, f32)
    for b in range(tab_ref.shape[0]):
        row = jnp.where(buck == b, tab_ref[b] * mul, row)
    for m in range(16):
        rolled = pltpu.roll(row, 8 * m, 1, stride=1, stride_axis=0)
        for c in range(width // 128 - 1):
            lo = width - 128 - 128 * c
            tb_ref[16 * c + m] = rolled[:, lo : lo + 128]


def bias_tile(tb_ref, start, rows, cols):
    parts = [
        tb_ref[pl.ds(start - 16 * c, rows // 8)].reshape(rows, 128) for c in range(cols // 128)
    ]
    return jnp.concatenate(parts, axis=1)


def attention_fwd_kernel(
    bk, order, nch_ref, tab_ref, buck_ref, kmask_ref, qmask_ref, q_ref, k_ref, v_ref,
    o_ref, lse_ref, kaug, vaug, tb,
):
    qi = pl.program_id(0)
    blocks, _, _, tok = k_ref.shape
    length = blocks * tok

    @pl.when(qi == 0)
    def _():
        fill_table(tab_ref, buck_ref, tb, 2 * length, LOG2E)
        first = lax.broadcasted_iota(jnp.int32, (16, length), 0) == 0
        vaug[HEAD_DIM:, :] = first.astype(f32).astype(bf16)
        for p in range(blocks):
            rows = slice(p * tok, (p + 1) * tok)
            kaug[rows, :] = jnp.concatenate([k_ref[order(p), 0], kmask_ref[:, rows]], axis=0).T
            vaug[0:HEAD_DIM, rows] = v_ref[order(p), 0]

    qaug = jnp.concatenate([q_ref[0, 0], qmask_ref[...]], axis=0)
    base = (length - 128) // 8 - qi * (tok // 8)

    def step(j, carry):
        peak, acc = carry
        ks = pl.ds(pl.multiple_of(j * bk, bk), bk)
        scores = mm(kaug[ks, :], qaug, NN) * SCALE + bias_tile(tb, base + j * (bk // 8), bk, tok)
        now = jnp.maximum(peak, jnp.max(scores, axis=0, keepdims=True))
        weights = jnp.exp2(scores - now).astype(bf16)
        return now, acc * jnp.exp2(peak - now) + mm(vaug[:, ks], weights, NN)

    start = (jnp.full((1, tok), -1e37, f32), jnp.zeros((HEAD_DIM + 16, tok), f32))
    peak, acc = lax.fori_loop(0, nch_ref[qi], step, start)
    total = acc[HEAD_DIM : HEAD_DIM + 1]
    o_ref[0] = (acc[0:HEAD_DIM] / total).astype(bf16)
    lse_ref[0] = peak + jnp.log2(total)


def attention_fwd(order, chunks, table, buck, kmask, qmask, qkv, bk):
    blocks, _, dim, tok = qkv.shape
    length = blocks * tok
    return pl.pallas_call(
        functools.partial(attention_fwd_kernel, bk, order),
        grid_spec=pltpu.PrefetchScalarGridSpec(
            num_scalar_prefetch=2,
            grid=(blocks,),
            in_specs=[
                pl.BlockSpec((8, 2 * length), lambda i, *_: (0, 0)),
                pl.BlockSpec((64, length), lambda i, *_: (0, 0)),
                pl.BlockSpec((64, tok), lambda i, *_: (0, i)),
                pl.BlockSpec((1, 1, dim, tok), lambda i, *_: (order(i), 0, 0, 0)),
                pl.BlockSpec((blocks, 1, dim, tok), lambda i, *_: (0, 1, 0, 0)),
                pl.BlockSpec((blocks, 1, dim, tok), lambda i, *_: (0, 2, 0, 0)),
            ],
            out_specs=[
                pl.BlockSpec((1, dim, tok), lambda i, *_: (order(i), 0, 0)),
                pl.BlockSpec((1, 1, tok), lambda i, *_: (i, 0, 0)),
            ],
            scratch_shapes=[
                pltpu.VMEM((length, 128), bf16),
                pltpu.VMEM((dim + 16, length), bf16),
                pltpu.VMEM((2 * length // 8 - 16, 8, 128), f32),
            ],
        ),
        out_shape=[
            jax.ShapeDtypeStruct((blocks, dim, tok), bf16),
            jax.ShapeDtypeStruct((blocks, 1, tok), f32),
        ],
        compiler_params=pltpu.CompilerParams(vmem_limit_bytes=60 << 20),
        cost_estimate=cost(2000 * length * length // 2, 4 * length * 2 * dim, length * length // 2),
        name="attention_fwd",
    )(chunks, table, buck, kmask, qmask, qkv, qkv, qkv)


def three_rows(values, rows):
    high = values.astype(bf16).astype(f32)
    mid = (values - high).astype(bf16).astype(f32)
    row = lax.broadcasted_iota(jnp.int32, (rows, values.shape[1]), 0)
    out = jnp.where(row == 0, high, jnp.where(row == 1, mid, jnp.where(row == 2, values - high - mid, 0.0)))
    return out.astype(bf16)


def attention_bwd_kernel(
    bk, order, nch_ref, tab_ref, buck_ref, kmask_ref, qmask_ref, q_ref, k_ref, v_ref, o_ref,
    do_ref, lse_ref, out_ref, off_ref, knat, kaug, vaug, tb, gb, dkacc, dvacc,
):
    qi = pl.program_id(0)
    blocks, _, _, tok = k_ref.shape
    length = blocks * tok

    @pl.when(qi == 0)
    def _():
        fill_table(tab_ref, buck_ref, tb, 2 * length, LOG2E)
        gb[...] = jnp.zeros_like(gb)
        dkacc[...] = jnp.zeros_like(dkacc)
        dvacc[...] = jnp.zeros_like(dvacc)
        three = lax.broadcasted_iota(jnp.int32, (64, length), 0) < 3
        vaug[64:128, :] = three.astype(f32).astype(bf16)
        kaug[64:128, :] = kmask_ref[...]
        for p in range(blocks):
            rows = slice(p * tok, (p + 1) * tok)
            knat[rows, :] = k_ref[order(p), 0].T
            kaug[0:64, rows] = k_ref[order(p), 0]
            vaug[0:64, rows] = v_ref[order(p), 0]

    q_t = q_ref[0, 0]
    do_t = do_ref[0]
    delta = jnp.sum(do_t.astype(f32) * o_ref[0].astype(f32), axis=0, keepdims=True)
    lse = lse_ref[0] * (1.0 / SCALE)
    blank = jnp.zeros((32, tok), bf16)
    qaug = jnp.concatenate([q_t, qmask_ref[...], three_rows(-lse, 16), blank], axis=0).T
    doaug = jnp.concatenate([do_t, three_rows(-delta, 32), blank], axis=0).T
    base = (length - 128) // 8 + qi * (tok // 8)

    def step(j, dq):
        ks = pl.ds(pl.multiple_of(j * bk, bk), bk)
        start = base - j * (bk // 8)
        probs = jnp.exp2(mm(qaug, kaug[:, ks], NN) * SCALE + bias_tile(tb, start, tok, bk))
        ds = probs * mm(doaug, vaug[:, ks], NN)
        for c in range(bk // 128):
            at = pl.ds(start - 16 * c, tok // 8)
            gb[at] += ds[:, 128 * c : 128 * c + 128].reshape(tok // 8, 8, 128)
        low = ds.astype(bf16)
        dvacc[:, ks] += mm(do_t, probs.astype(bf16), NN)
        dkacc[:, ks] += mm(q_t, low, NN)
        return dq + mm(low, knat[ks, :], NN)

    dq = lax.fori_loop(0, nch_ref[qi], step, jnp.zeros((tok, 64), f32))
    out_ref[order(qi), 0] = (dq * 0.125).T.astype(bf16)

    @pl.when(qi == blocks - 1)
    def _():
        for p in range(blocks):
            rows = slice(p * tok, (p + 1) * tok)
            out_ref[order(p), 1] = (dkacc[:, rows] * 0.125).astype(bf16)
            out_ref[order(p), 2] = dvacc[:, rows].astype(bf16)
        width = 2 * length
        total = jnp.zeros((8, width), f32)
        for m in range(16):
            tiles = [gb[16 * c + m] for c in range(width // 128 - 2, -1, -1)]
            skewed = jnp.concatenate([jnp.zeros((8, 128), f32)] + tiles, axis=1)
            total = total + (pltpu.roll(skewed, width - 8 * m, 1) if m else skewed)
        row = total[0:1]
        for s in range(1, 8):
            row = row + pltpu.roll(total[s : s + 1], width - s, 1)
        buck = buck_ref[0:1, :]
        for b in range(off_ref.shape[0]):
            mine = jnp.where(buck == b, row, 0.0)
            parts = [mine[:, 128 * c : 128 * c + 128] for c in range(width // 128)]
            while len(parts) > 1:
                parts = [x + y for x, y in zip(parts[::2], parts[1::2])]
            off_ref[b : b + 1, :] = parts[0]


def attention_bwd(order, chunks, table, buck, kmask, qmask, qkv, mixed, mixed_grad, lse, bk):
    blocks, _, dim, tok = qkv.shape
    length = blocks * tok
    one = pl.BlockSpec((1, dim, tok), lambda i, *_: (order(i), 0, 0))
    return pl.pallas_call(
        functools.partial(attention_bwd_kernel, bk, order),
        grid_spec=pltpu.PrefetchScalarGridSpec(
            num_scalar_prefetch=2,
            grid=(blocks,),
            in_specs=[
                pl.BlockSpec((8, 2 * length), lambda i, *_: (0, 0)),
                pl.BlockSpec((64, length), lambda i, *_: (0, 0)),
                pl.BlockSpec((16, tok), lambda i, *_: (0, i)),
                pl.BlockSpec((1, 1, dim, tok), lambda i, *_: (order(i), 0, 0, 0)),
                pl.BlockSpec((blocks, 1, dim, tok), lambda i, *_: (0, 1, 0, 0)),
                pl.BlockSpec((blocks, 1, dim, tok), lambda i, *_: (0, 2, 0, 0)),
                one,
                one,
                pl.BlockSpec((1, 1, tok), lambda i, *_: (i, 0, 0)),
            ],
            out_specs=[
                pl.BlockSpec((blocks, 3, dim, tok), lambda i, *_: (0, 0, 0, 0)),
                pl.BlockSpec((table.shape[0], 128), lambda i, *_: (0, 0)),
            ],
            scratch_shapes=[
                pltpu.VMEM((length, dim), bf16),
                pltpu.VMEM((128, length), bf16),
                pltpu.VMEM((128, length), bf16),
                pltpu.VMEM((2 * length // 8 - 16, 8, 128), f32),
                pltpu.VMEM((2 * length // 8 - 16, 8, 128), f32),
                pltpu.VMEM((dim, length), f32),
                pltpu.VMEM((dim, length), f32),
            ],
        ),
        out_shape=[
            jax.ShapeDtypeStruct((blocks, 3, dim, tok), bf16),
            jax.ShapeDtypeStruct((table.shape[0], 128), f32),
        ],
        compiler_params=pltpu.CompilerParams(vmem_limit_bytes=60 << 20),
        cost_estimate=cost(5000 * length * length // 2, 8 * length * 2 * dim, length * length // 2),
        name="attention_bwd",
    )(chunks, table, buck, kmask, qmask, qkv, qkv, qkv, mixed, mixed_grad, lse)


def write_groups(acc, refs):
    rows = refs[0].shape[0]
    for d, ref in enumerate(refs):
        ref[...] = acc[d * rows : (d + 1) * rows, :].astype(bf16)


def join_rows(refs, scratch):
    at = 0
    for ref in refs:
        scratch[at : at + ref.shape[0], :] = ref[:, : scratch.shape[1]]
        at += ref.shape[0]


def gate_column(refs):
    return jnp.concatenate(
        [jnp.sum(ref[...].astype(f32), axis=1, keepdims=True) for ref in refs], axis=0
    )


def expert_fwd_kernel(steps, groups, wg_ref, wu_ref, wd_ref, *refs):
    xs, refs = refs[:groups], refs[groups:]
    h_ref, act_ref, slope_ref, *outs, rows, acc = refs
    f = pl.program_id(0)

    @pl.when(f == 0)
    def _():
        join_rows(xs, rows)
        acc[...] = jnp.zeros_like(acc)

    x = rows[...]
    gate = mm(x, wg_ref[0], NN)
    up = mm(x, wu_ref[0], NN)
    square = gate * gate
    t = jnp.tanh(gate * (0.7978845608028654 + 0.035677408136300125 * square))
    half = 0.5 + 0.5 * t
    act = gate * half
    slope = half + (gate * (0.5 - 0.5 * t * t)) * (
        0.7978845608028654 + 0.10703222440890037 * square
    )
    hidden = (act * up).astype(bf16)
    h_ref[...] = hidden
    act_ref[...] = act.astype(bf16)
    slope_ref[...] = (slope * up).astype(bf16)
    acc[...] += mm(hidden, wd_ref[0], NN)

    @pl.when(f == steps - 1)
    def _():
        write_groups(acc, outs)


def expert_fwd(xs, w_in, w_down, tile=256):
    groups = len(xs)
    ff, width = w_down.shape[1:]
    rows = groups * xs[0].shape[0]
    steps = ff // tile
    part = pl.BlockSpec((rows, tile), lambda f: (0, f))
    inner = jax.ShapeDtypeStruct((rows, ff), bf16)
    one = pl.BlockSpec((rows // groups, width), lambda f: (0, 0))
    return pl.pallas_call(
        functools.partial(expert_fwd_kernel, steps, groups),
        grid=(steps,),
        in_specs=[
            pl.BlockSpec((1, width, tile), lambda f: (0, 0, f)),
            pl.BlockSpec((1, width, tile), lambda f: (0, 0, f + steps)),
            pl.BlockSpec((1, tile, width), lambda f: (0, f, 0)),
        ]
        + [pl.BlockSpec(xs[0].shape, lambda f: (0, 0))] * groups,
        out_specs=[part, part, part] + [one] * groups,
        out_shape=[inner, inner, inner]
        + [jax.ShapeDtypeStruct((rows // groups, width), bf16)] * groups,
        scratch_shapes=[pltpu.VMEM((rows, width), bf16), pltpu.VMEM((rows, width), f32)],
        compiler_params=pltpu.CompilerParams(vmem_limit_bytes=60 << 20),
        cost_estimate=cost(
            10 * rows * width * ff, 6 * width * ff + rows * (4 * width + 6 * ff), rows * ff
        ),
        name="expert_fwd",
    )(w_in, w_in, w_down, *xs)


def expert_bwd_kernel(steps, groups, act_ref, slope_ref, wg_ref, wu_ref, wd_ref, *refs):
    gs, gates, refs = refs[:groups], refs[groups : 2 * groups], refs[2 * groups :]
    grads_ref, *outs, pg, acc = refs
    f = pl.program_id(0)

    @pl.when(f == 0)
    def _():
        join_rows(gs, pg)
        pg[...] = (pg[...].astype(f32) * gate_column(gates)).astype(bf16)
        acc[...] = jnp.zeros_like(acc)

    hidden_grad = mm(pg[...], wd_ref[0], NT)
    dg = (slope_ref[...].astype(f32) * hidden_grad).astype(bf16)
    du = (act_ref[...].astype(f32) * hidden_grad).astype(bf16)
    grads_ref[0] = dg
    grads_ref[1] = du
    acc[...] += mm(dg, wg_ref[0], NT) + mm(du, wu_ref[0], NT)

    @pl.when(f == steps - 1)
    def _():
        write_groups(acc, outs)


def gate_block(x, width):
    return pl.BlockSpec((x.shape[0], 128), lambda f, *_: (0, width // 128))


def expert_bwd(gs, xs, act, slope, w_in, w_down, tile=256):
    groups = len(gs)
    rows, width = groups * gs[0].shape[0], gs[0].shape[1]
    ff = w_down.shape[1]
    steps = ff // tile
    part = pl.BlockSpec((rows, tile), lambda f: (0, f))
    one = pl.BlockSpec((rows // groups, width), lambda f: (0, 0))
    return pl.pallas_call(
        functools.partial(expert_bwd_kernel, steps, groups),
        grid=(steps,),
        in_specs=[
            part,
            part,
            pl.BlockSpec((1, width, tile), lambda f: (0, 0, f)),
            pl.BlockSpec((1, width, tile), lambda f: (0, 0, f + steps)),
            pl.BlockSpec((1, tile, width), lambda f: (0, f, 0)),
        ]
        + [one] * groups
        + [gate_block(x, width) for x in xs],
        out_specs=[pl.BlockSpec((2, rows, tile), lambda f: (0, 0, f))] + [one] * groups,
        out_shape=[jax.ShapeDtypeStruct((2, rows, ff), bf16)]
        + [jax.ShapeDtypeStruct((rows // groups, width), bf16)] * groups,
        scratch_shapes=[pltpu.VMEM((rows, width), bf16), pltpu.VMEM((rows, width), f32)],
        compiler_params=pltpu.CompilerParams(vmem_limit_bytes=60 << 20),
        cost_estimate=cost(
            10 * rows * width * ff, 6 * width * ff + rows * (4 * width + 8 * ff)
        ),
        name="expert_bwd",
    )(act, slope, w_in, w_in, w_down, *gs, *xs)


def column_block(ref, blk, ctx, flip, a):
    low = ref[:, 2 * a * blk : (2 * a + 1) * blk]
    high = ref[:, (2 * a + 1) * blk : (2 * a + 2) * blk]
    return jnp.where(lax.rem(ctx + flip, 2) == 0, low, high)


def in_grad_kernel(copies, n, ctx_ref, *refs):
    xs, (*gs, own_ref, other_ref, xt) = refs[:n], refs[n:]
    width = xt.shape[0]
    blk = width // copies

    @pl.when(pl.program_id(0) == 0)
    def _():
        at = 0
        for x_ref in xs:
            rows = x_ref.shape[0]
            for flip in range(2):
                for a in range(copies // 2):
                    to = (flip * (copies // 2) + a) * blk
                    xt[to : to + blk, at : at + rows] = column_block(
                        x_ref, blk, ctx_ref[0], flip, a
                    ).T
            at += rows

    grads = jnp.concatenate([g[0] for g in gs], axis=0)
    grad = mm(xt[...], grads, NN).astype(bf16)
    own_ref[...] = grad[: width // 2]
    other_ref[...] = grad[width // 2 :]


def in_grad(ctx, xs, grads, copies, first, count, tile=256):
    width = xs[0].shape[1] - 128
    steps = grads[0].shape[2] // tile
    total = sum(x.shape[0] for x in xs)
    half = jax.ShapeDtypeStruct((width // 2, count * tile), bf16)
    out = pl.BlockSpec((width // 2, tile), lambda f, c: (0, f))

    def at(f, c):
        return ((f + first) // steps, 0, (f + first) % steps)

    return pl.pallas_call(
        functools.partial(in_grad_kernel, copies, len(xs)),
        grid_spec=pltpu.PrefetchScalarGridSpec(
            num_scalar_prefetch=1,
            grid=(count,),
            in_specs=[pl.BlockSpec(x.shape, lambda f, c: (0, 0)) for x in xs]
            + [pl.BlockSpec((1, g.shape[1], tile), at) for g in grads],
            out_specs=[out, out],
            scratch_shapes=[pltpu.VMEM((width, total), bf16)],
        ),
        out_shape=[half, half],
        compiler_params=pltpu.CompilerParams(vmem_limit_bytes=60 << 20),
        cost_estimate=cost(
            4 * total * width * count * tile, 2 * (total + width) * count * tile + 2 * total * width
        ),
        name="in_grad",
    )(ctx, *xs, *grads)


def down_grad_kernel(copies, n, ctx_ref, *refs):
    ps, gates, (*hs, own_ref, other_ref, pg) = refs[:n], refs[n : 2 * n], refs[2 * n :]
    blk = ps[0].shape[1] // copies

    @pl.when(pl.program_id(0) == 0)
    def _():
        at = 0
        for p_ref, gate_ref in zip(ps, gates):
            rows = p_ref.shape[0]
            gate = gate_column([gate_ref])
            for flip in range(2):
                for a in range(copies // 2):
                    to = (flip * (copies // 2) + a) * blk
                    block = column_block(p_ref, blk, ctx_ref[0], flip, a).astype(f32)
                    pg[at : at + rows, to : to + blk] = (block * gate).astype(bf16)
            at += rows

    grad = mm(jnp.concatenate([h[...] for h in hs], axis=0), pg[...], TN).astype(bf16)
    for a in range(copies // 2):
        own_ref[a] = grad[:, a * blk : (a + 1) * blk]
        to = (copies // 2 + a) * blk
        other_ref[a] = grad[:, to : to + blk]


def down_grad(ctx, hs, ps, xs, copies, first, count, tile=256):
    ff = count * tile
    width = ps[0].shape[1]
    total = sum(h.shape[0] for h in hs)
    blk = width // copies
    half = jax.ShapeDtypeStruct((copies // 2, ff, blk), bf16)
    out = pl.BlockSpec((copies // 2, tile, blk), lambda f, c: (0, f, 0))
    return pl.pallas_call(
        functools.partial(down_grad_kernel, copies, len(ps)),
        grid_spec=pltpu.PrefetchScalarGridSpec(
            num_scalar_prefetch=1,
            grid=(count,),
            in_specs=[pl.BlockSpec(p.shape, lambda f, c: (0, 0)) for p in ps]
            + [gate_block(x, width) for x in xs]
            + [pl.BlockSpec((h.shape[0], tile), lambda f, c: (0, f + first)) for h in hs],
            out_specs=[out, out],
            scratch_shapes=[pltpu.VMEM((total, width), bf16)],
        ),
        out_shape=[half, half],
        compiler_params=pltpu.CompilerParams(vmem_limit_bytes=60 << 20),
        cost_estimate=cost(4 * total * width * ff, 2 * (total * (width + ff) + width * ff)),
        name="down_grad",
    )(ctx, *ps, *xs, *hs)


def project_kernel(x_ref, gain_ref, w_ref, normed_ref, *refs):
    outs, normed_t = refs[:-1], refs[-1]
    heads = len(outs)

    @pl.when((pl.program_id(0) == 0) & (pl.program_id(1) == 0))
    def _():
        x = x_ref[...].astype(f32)
        scale = lax.rsqrt(jnp.mean(x * x, axis=1, keepdims=True) + 1e-06)
        normed = (x * scale * gain_ref[...]).astype(bf16)
        normed_ref[...] = normed
        normed_t[...] = normed.T

    cols = w_ref.shape[1]
    tok = normed_t.shape[1]
    rows = mm(w_ref[...], normed_t[...], TN).astype(bf16)
    rows = rows.reshape(cols // (heads * HEAD_DIM), heads, HEAD_DIM, tok)
    for h in range(heads):
        outs[h][:, 0] = rows[:, h]


def project(x, gain, weight, groups, heads, cols=512):
    tok, width = x.shape
    per = cols // (heads * HEAD_DIM)
    blocks = width // cols
    return pl.pallas_call(
        project_kernel,
        grid=(3, blocks),
        in_specs=[
            pl.BlockSpec((tok, width), lambda p, j: (0, 0)),
            pl.BlockSpec((1, width), lambda p, j: (0, 0)),
            pl.BlockSpec((width, cols), lambda p, j: (0, p * blocks + j)),
        ],
        out_specs=[pl.BlockSpec((tok, width), lambda p, j: (0, 0))]
        + [pl.BlockSpec((per, 1, HEAD_DIM, tok), lambda p, j: (j, p, 0, 0))] * heads,
        out_shape=[jax.ShapeDtypeStruct((tok, width), bf16)]
        + [jax.ShapeDtypeStruct((groups, 3, HEAD_DIM, tok), bf16)] * heads,
        scratch_shapes=[pltpu.VMEM((width, tok), bf16)],
        compiler_params=pltpu.CompilerParams(vmem_limit_bytes=60 << 20),
        cost_estimate=cost(6 * tok * width * width, 6 * width * width + 10 * tok * width),
        name="project",
    )(x, gain.reshape(1, width), weight)


def input_grad_kernel(steps, x_ref, gain_ref, mid_ref, w_ref, *refs):
    grads, out_ref, acc = refs[:-2], refs[-2], refs[-1]
    step = pl.program_id(0)
    cols = w_ref.shape[1]
    tok = out_ref.shape[0]

    @pl.when(step == 0)
    def _():
        acc[...] = jnp.zeros_like(acc)

    rows = jnp.stack([g[:, 0] for g in grads], axis=1).reshape(cols, tok)
    acc[...] += mm(w_ref[...], rows, NN)

    @pl.when(step == steps - 1)
    def _():
        x = x_ref[...].astype(f32)
        scale = lax.rsqrt(jnp.mean(x * x, axis=1, keepdims=True) + 1e-06)
        dy = acc[...].T * gain_ref[...]
        pull = jnp.mean(x * dy, axis=1, keepdims=True)
        out_ref[...] = mid_ref[...] + scale * dy - x * (scale * scale * scale * pull)


def input_gradient(x, gain, middle_grad, weight, grads, cols=512):
    tok, width = x.shape
    heads = len(grads)
    per = cols // (heads * HEAD_DIM)
    blocks = width // cols
    whole = pl.BlockSpec((tok, width), lambda s: (0, 0))
    return pl.pallas_call(
        functools.partial(input_grad_kernel, 3 * blocks),
        grid=(3 * blocks,),
        in_specs=[
            whole,
            pl.BlockSpec((1, width), lambda s: (0, 0)),
            whole,
            pl.BlockSpec((width, cols), lambda s: (0, s)),
        ]
        + [
            pl.BlockSpec((per, 1, HEAD_DIM, tok), lambda s: (s % blocks, s // blocks, 0, 0))
            for _ in grads
        ],
        out_specs=whole,
        out_shape=jax.ShapeDtypeStruct((tok, width), f32),
        scratch_shapes=[pltpu.VMEM((width, tok), f32)],
        compiler_params=pltpu.CompilerParams(vmem_limit_bytes=60 << 20),
        cost_estimate=cost(6 * tok * width * width, 6 * width * width + 16 * tok * width),
        name="input_grad",
    )(x, gain.reshape(1, width), middle_grad, weight, *grads)


def wide_thirds(values):
    high = values.astype(bf16)
    rest = values - high.astype(f32)
    mid = rest.astype(bf16)
    low = (rest - mid.astype(f32)).astype(bf16)
    rows, lanes = values.shape
    blank = jnp.zeros((rows, 128 - 3 * lanes), bf16)
    return jnp.concatenate([high, mid, low, blank], axis=1)


def combine_kernel(
    counts, exp_ref, place_ref, ids_ref, probs_ref, middle_ref, cot_ref, normed_ref, gain_ref,
    router_ref, weight_ref, *refs,
):
    blocks, heads, parts, copies = counts
    experts = probs_ref.shape[1]
    backs, refs = refs[:blocks], refs[blocks:]
    row_grads, refs = refs[:blocks], refs[blocks:]
    mixed, refs = refs[:heads], refs[heads:]
    out_ref, mid_ref, refs = refs[0], refs[1], refs[2:]
    mixed_grads, refs = refs[:heads], refs[heads:]
    early, (slot_rows, slot_grads, wide) = refs[:parts], refs[parts:]
    tok, width = middle_ref.shape
    total = slot_rows.shape[0]

    at = 0
    for back, row_grad in zip(backs, row_grads):
        rows = slice(at, at + back.shape[0])
        slot_rows[rows, :] = back[...]
        slot_grads[rows, :] = row_grad[...]
        at += back.shape[0]

    slot = lax.broadcasted_iota(jnp.int32, (tok, total), 1)
    one = (slot == place_ref[:, 0:1]).astype(f32).astype(bf16)
    two = (slot == place_ref[:, 1:2]).astype(f32).astype(bf16)
    first = mm(one, slot_rows[...], NN)
    second = mm(two, slot_rows[...], NN)
    dy = mm(one + two, slot_grads[...], NN)

    lane = lax.broadcasted_iota(jnp.int32, (tok, experts), 1)
    is_first, is_second = lane == ids_ref[:, 0:1], lane == ids_ref[:, 1:2]
    probs = probs_ref[...]
    gate_first = jnp.sum(jnp.where(is_first, probs, 0.0), axis=1, keepdims=True)
    gate_second = jnp.sum(jnp.where(is_second, probs, 0.0), axis=1, keepdims=True)
    middle = middle_ref[...]
    cot = cot_ref[...].astype(f32)
    out_ref[...] = (middle + gate_first * first + gate_second * second).astype(bf16)
    grad_first = jnp.sum(cot * first, axis=1, keepdims=True)
    grad_second = jnp.sum(cot * second, axis=1, keepdims=True)
    probs_grad = jnp.where(is_first, grad_first, 0.0) + jnp.where(is_second, grad_second, 0.0)
    logits_grad = probs * (probs_grad - jnp.sum(probs * probs_grad, axis=1, keepdims=True))
    for e in range(experts):
        dy = dy + logits_grad[:, e : e + 1] * router_ref[e : e + 1, :]

    scale = lax.rsqrt(jnp.mean(middle * middle, axis=1, keepdims=True) + 1e-06)
    unit = middle * scale
    gain_terms = unit * dy
    dy = dy * gain_ref[...]
    middle_grad = cot + scale * (dy - unit * jnp.mean(unit * dy, axis=1, keepdims=True))
    mid_ref[...] = middle_grad
    branch = middle_grad.astype(bf16)

    groups, dim, _ = mixed_grads[0].shape
    back = mm(weight_ref[...], branch, NT).astype(bf16).reshape(groups, heads, dim, tok)
    for h in range(heads):
        mixed_grads[h][...] = back[:, h]
    for h in range(heads):
        grad = mm(mixed[h][...], branch, NN)
        for g in range(groups):
            at = (g * heads + h) * dim
            wide[at : at + dim, 0:width] = grad[g * dim : (g + 1) * dim]
    mark = lax.broadcasted_iota(jnp.int32, (tok, 128), 1) == 3 * experts
    mark = mark.astype(f32).astype(bf16)
    high = gain_terms.astype(bf16)
    low = (gain_terms - high.astype(f32)).astype(bf16)
    wide[:, width:] = (
        mm(normed_ref[...], wide_thirds(logits_grad), TN) + mm(high, mark, TN) + mm(low, mark, TN)
    )
    per = wide.shape[0] // (parts * copies)
    for d in range(parts):
        e = jnp.bitwise_xor(exp_ref[0], d)
        rows = [
            wide[pl.ds(pl.multiple_of((k * parts + e) * per, per), per), :] for k in range(copies)
        ]
        early[d][...] = jnp.concatenate(rows, axis=0).astype(bf16)


def combine(
    exp, place, ids, probs, middle, cot, normed, gain, router, weight, backs, row_grads, mixed,
    copies,
):
    tok, width = middle.shape
    heads = len(mixed)
    parts = probs.shape[1]
    groups = width // (heads * HEAD_DIM)
    total = sum(b.shape[0] for b in backs)
    sds = jax.ShapeDtypeStruct
    return pl.pallas_call(
        functools.partial(combine_kernel, (len(backs), heads, parts, copies)),
        in_specs=[pl.BlockSpec(memory_space=pltpu.SMEM)]
        + [pl.BlockSpec(memory_space=pltpu.VMEM)] * (9 + 2 * len(backs) + heads),
        out_specs=[pl.BlockSpec(memory_space=pltpu.VMEM)] * (2 + heads + parts),
        out_shape=[sds((tok, width), bf16), sds((tok, width), f32)]
        + [sds((groups, HEAD_DIM, tok), bf16)] * heads
        + [sds((width // parts, width + 128), bf16)] * parts,
        scratch_shapes=[
            pltpu.VMEM((total, width), bf16),
            pltpu.VMEM((total, width), bf16),
            pltpu.VMEM((width, width + 128), f32),
        ],
        compiler_params=pltpu.CompilerParams(vmem_limit_bytes=60 << 20),
        cost_estimate=cost(
            6 * tok * total * width + 4 * tok * width * width,
            4 * total * width + 18 * tok * width + 4 * width * width,
        ),
        name="combine",
    )(exp, place, ids, probs, middle, cot, normed, gain.reshape(1, width), router, weight,
      *backs, *row_grads, *mixed)


def finish_kernel(heads, lanes, n_ctx, exp_ref, rows_ref, weight_ref, gain_ref, grad_ref, gain_grad_ref, bias_ref):
    groups = rows_ref.shape[0]
    width = weight_ref.shape[1] // 3
    for part in range(3):
        pieces = []
        for g in range(groups):
            for h in range(heads):
                lo = h * lanes + part * HEAD_DIM
                pieces.append(rows_ref[g][:, lo : lo + HEAD_DIM].astype(f32))
        grad_ref[:, part * width : (part + 1) * width] = jnp.concatenate(pieces, axis=1)
    terms = weight_ref[...].astype(f32) * grad_ref[...]
    gain_grad_ref[...] = jnp.sum(terms, axis=1, keepdims=True) / gain_ref[...]
    columns = []
    for c in range(n_ctx):
        mine = rows_ref[exp_ref[0] * n_ctx + c].astype(f32)
        for h in range(heads):
            lo = h * lanes + 3 * HEAD_DIM
            columns.append(mine[:, lo : lo + 1])
    bias_ref[...] = jnp.concatenate(columns, axis=1)


def finish(exp, rows, weight_rows, gain_rows, heads, lanes, n_ctx):
    count, columns = weight_rows.shape
    sds = jax.ShapeDtypeStruct
    vmem = pl.BlockSpec(memory_space=pltpu.VMEM)
    return pl.pallas_call(
        functools.partial(finish_kernel, heads, lanes, n_ctx),
        in_specs=[pl.BlockSpec(memory_space=pltpu.SMEM), vmem, vmem, vmem],
        out_specs=[vmem, vmem, vmem],
        out_shape=[
            sds((count, columns), f32), sds((count, 1), f32), sds((count, heads * n_ctx), f32)
        ],
        cost_estimate=cost(4 * count * columns, 8 * count * columns),
        name="finish",
    )(exp, rows, weight_rows, gain_rows)


def route_kernel(heads, x_ref, place_ref, ids_ref, gain_ref, router_ref, weight_ref, *refs):
    mixed, (middle_ref, normed_ref, probs_ref, *slots, joined) = refs[:heads], refs[heads:]
    tok, width = x_ref.shape
    experts = probs_ref.shape[1]
    for h in range(heads):
        for g in range(width // (heads * HEAD_DIM)):
            at = (g * heads + h) * HEAD_DIM
            joined[at : at + HEAD_DIM, :] = mixed[h][g * HEAD_DIM : (g + 1) * HEAD_DIM, :]
    middle = x_ref[...].astype(f32) + mm(joined[...], weight_ref[...], TN)
    middle_ref[...] = middle
    scale = lax.rsqrt(jnp.mean(middle * middle, axis=1, keepdims=True) + 1e-06)
    normed = (middle * scale * gain_ref[...]).astype(bf16)
    normed_ref[...] = normed
    logits = mm(normed, router_ref[...], NN)[:, :experts]
    weights = jnp.exp(logits - jnp.max(logits, axis=1, keepdims=True))
    probs = weights / jnp.sum(weights, axis=1, keepdims=True)
    probs_ref[...] = probs
    lane = lax.broadcasted_iota(jnp.int32, (tok, experts), 1)
    gates = [
        wide_thirds(jnp.sum(jnp.where(lane == ids_ref[:, j : j + 1], probs, 0.0), axis=1, keepdims=True))
        for j in range(2)
    ]
    at = 0
    for slot_ref in slots:
        rows = slot_ref.shape[0]
        slot = lax.broadcasted_iota(jnp.int32, (rows, tok), 0) + at
        one = (slot == place_ref[0:1, :]).astype(f32).astype(bf16)
        two = (slot == place_ref[1:2, :]).astype(f32).astype(bf16)
        slot_ref[:, 0:width] = mm(one + two, normed, NN).astype(bf16)
        slot_ref[:, width:] = (mm(one, gates[0], NN) + mm(two, gates[1], NN)).astype(bf16)
        at += rows


def route(x, place, ids, gain, router, weight, mixed, sizes):
    tok, width = x.shape
    experts = router.shape[1]
    heads = len(mixed)
    sds = jax.ShapeDtypeStruct
    vmem = pl.BlockSpec(memory_space=pltpu.VMEM)
    return pl.pallas_call(
        functools.partial(route_kernel, heads),
        in_specs=[vmem] * (6 + heads),
        out_specs=[vmem] * (3 + len(sizes)),
        out_shape=[sds((tok, width), f32), sds((tok, width), bf16), sds((tok, experts), f32)]
        + [sds((size, width + 128), bf16) for size in sizes],
        scratch_shapes=[pltpu.VMEM((width, tok), bf16)],
        compiler_params=pltpu.CompilerParams(vmem_limit_bytes=60 << 20),
        cost_estimate=cost(
            2 * tok * width * (width + sum(sizes)), 12 * tok * width + 2 * width * width
        ),
        name="route",
    )(x, place.T, ids, gain.reshape(1, width), jnp.pad(router, ((0, 0), (0, 128 - experts))),
      weight, *mixed)


def dot_f32(left, right, left_dim, right_dim):
    return mm(left, right, (((left_dim,), (right_dim,)), ((), ())))


def swap_blocks(blocks, axes):
    return lax.all_to_all(blocks, axes, split_axis=0, concat_axis=0, tiled=True)


def exchange(parts, axis="expert"):
    n = len(parts)
    return [parts[0]] + [
        lax.ppermute(parts[d], axis, [(i, i ^ d) for i in range(n)]) for d in range(1, n)
    ]


def scatter_dp(rows):
    n = lax.axis_size("dp")
    shares = rows.reshape((n, rows.shape[0] // n) + rows.shape[1:])
    mine = lax.axis_index("dp")
    return exchange(
        [
            lax.dynamic_index_in_dim(shares, jnp.bitwise_xor(mine, d), 0, False)
            for d in range(n)
        ],
        "dp",
    )


def add_low(parts):
    return sum(part.astype(f32) for part in parts).astype(bf16)


def after(value, *others):
    return lax.optimization_barrier((value, others))[0]


def attention_plan(block_row, bucket_ids, blocks, tok):
    length = blocks * tok
    pad = jnp.full((1,), -1, jnp.int32)
    buck_rev = jnp.broadcast_to(jnp.concatenate([pad, bucket_ids[::-1]])[None], (8, 2 * length))
    buck = jnp.broadcast_to(jnp.concatenate([pad, bucket_ids])[None], (8, 2 * length))
    ids = jnp.arange(16)
    hot = (block_row[None, :] == ids[:, None]).astype(bf16)
    hide = jnp.where(ids[:, None] > block_row[None, :], HIDE, 0.0).astype(bf16)
    kmask_t = jnp.concatenate(
        [hot, jnp.ones((3, length), bf16), jnp.zeros((45, length), bf16)], axis=0
    )
    qmask = jnp.concatenate([hide, jnp.zeros((48, length), bf16)], axis=0)
    last = block_row.reshape(blocks, tok)[:, -1]
    seen = jnp.sum((block_row[None, :] <= last[:, None]).astype(jnp.int32), axis=1)
    return buck_rev, buck, kmask_t, qmask, hide, seen


def shards(
    layer_input,
    attn_gain,
    qkv_weight,
    out_weight,
    bias_table,
    moe_gain,
    router_weight,
    expert_in,
    expert_down,
    expert_ids,
    fill_order,
    block_ids,
    bucket_ids,
    cotangent,
):
    tok, width = layer_input.shape
    n_dp, n_ctx, n_exp = lax.axis_size("dp"), lax.axis_size("ctx"), lax.axis_size("expert")
    groups = n_ctx * n_exp
    copies = n_dp * n_ctx
    head_exp = bias_table.shape[1]
    heads = head_exp // n_ctx
    experts = router_weight.shape[1]
    ff_width = expert_down.shape[1]
    capacity = 5 * TOP * tok // (4 * experts)
    cut = (capacity // 2 + 15) // 16 * 16
    spans = ((0, cut), (cut, capacity))
    ctx_index = lax.axis_index("ctx")
    exp_index = lax.axis_index("expert")
    ctx_arg = ctx_index.astype(jnp.int32).reshape(1)
    pair = ("expert", "ctx")
    step_k = 512

    def order(p):
        return (p % n_exp) * n_ctx + p // n_exp

    def in_swap_order(blocks):
        shape = blocks.shape
        return jnp.swapaxes(blocks.reshape((n_ctx, n_exp) + shape[1:]), 0, 1).reshape(shape)

    exp_arg = exp_index.astype(jnp.int32).reshape(1)
    normed, *parts = project(layer_input, attn_gain, qkv_weight, groups, heads)
    qkv = [swap_blocks(part, pair) for part in parts]
    table_dev = lax.dynamic_slice_in_dim(bias_table, ctx_index * heads, heads, 1)
    buck_rev, buck, kmask, qmask, hide, seen = attention_plan(
        block_ids[0], bucket_ids, groups, tok
    )
    chunks = (seen + step_k - 1) // step_k

    flat_ids = expert_ids.reshape(TOP * tok)
    fill_rank = fill_order.reshape(TOP * tok)
    same_expert = flat_ids[:, None] == flat_ids[None, :]
    earlier = fill_rank[None, :] < fill_rank[:, None]
    slot_of = jnp.sum((same_expert & earlier).astype(jnp.int32), axis=1)
    slots = slot_of.reshape(tok, TOP)
    part_at = jnp.where(slots < cut, 0, experts * cut - cut)
    stride = jnp.where(slots < cut, cut, capacity - cut)
    place = jnp.where(
        slots < capacity,
        part_at + jnp.bitwise_xor(expert_ids, exp_index) * stride + slots,
        -1,
    )
    sizes = [high - low for low, high in spans for _ in range(experts)]

    def to_slots(rows):
        parts, at = [], 0
        for size in sizes:
            slot = jnp.arange(at, at + size)[:, None]
            hot = (slot == place[None, :, 0]) | (slot == place[None, :, 1])
            parts.append(dot_f32(hot.astype(bf16), rows, 1, 0).astype(bf16))
            at += size
        return parts

    forward, mixed = [], []
    cot_slots = to_slots(cotangent)
    slots_a, slots_b = cot_slots[:experts], cot_slots[experts:]
    qkv[0], place, slots_a, slots_b, buck_rev, buck, kmask, qmask, hide = (
        lax.optimization_barrier(
            (qkv[0], place, slots_a, slots_b, buck_rev, buck, kmask, qmask, hide)
        )
    )
    normed_seq = lax.all_gather(after(normed, qkv[0]), pair, axis=0, tiled=True)
    for h in range(heads):
        arg = after(qkv[h], forward)
        if h == heads - 1:
            grad_a = exchange(after(slots_a, arg))
        out = attention_fwd(order, chunks, table_dev[:, h], buck_rev, kmask, qmask, arg, step_k)
        out = after(out, qkv[h + 1] if h < heads - 1 else grad_a, mixed)
        forward.append(out)
        mixed.append(swap_blocks(out[0], pair).reshape(groups * HEAD_DIM, tok))
    mixed = after(mixed, forward)
    middle, normed_moe, probs, *sent = route(
        layer_input, place, expert_ids, moe_gain, router_weight, out_weight, mixed, sizes
    )
    x_a, x_b = exchange(sent[:experts]), exchange(sent[experts:])

    grad_b = exchange(after(slots_b, x_a))
    run_a = after(expert_fwd(x_a, expert_in, expert_down), x_b, grad_b)
    produced_a = exchange(list(run_a[3:]))
    run_b = expert_fwd(after(x_b, run_a), expert_in, expert_down)
    run_b = after(run_b, produced_a, normed_seq)
    produced_b = exchange(list(run_b[3:]))
    hidden = [run_a[0], run_b[0]]
    tiles = ff_width // 256
    cuts = (0, (tiles + 1) // 2, tiles)
    g_args = after(grad_a + grad_b, run_b)
    down_1 = down_grad(ctx_arg, hidden, g_args, x_a + x_b, copies, 0, cuts[1])

    def to_ctx(half):
        return lax.ppermute(half, "ctx", [(0, 1), (1, 0)])

    came = to_ctx(down_1[1])
    g_args = after(grad_a + grad_b, down_1)
    down_2 = down_grad(ctx_arg, hidden, g_args, x_a + x_b, copies, cuts[1], tiles - cuts[1])
    undo_a = expert_bwd(
        after(grad_a, down_2), x_a, run_a[1], run_a[2], expert_in, expert_down
    )
    undo_a, came = lax.optimization_barrier((after(undo_a, produced_b), came))
    halves = [add_low((down_1[0], came))]
    grads_a = exchange(list(undo_a[1:]))
    came = to_ctx(after(down_2[1], undo_a))
    undo_b = expert_bwd(
        after(grad_b, undo_a), x_b, run_b[1], run_b[2], expert_in, expert_down
    )
    undo_b, came = lax.optimization_barrier((after(undo_b, grads_a), came))
    halves.append(add_low((down_2[0], came)))
    grads_b = exchange(list(undo_b[1:]))
    grads_in = [undo_a[0], undo_b[0]]
    share = 2 * tiles * 2 // 11
    sizes = (share, 2 * tiles - 4 * share, share, 2 * share)
    in_parts, first = [], 0
    xs = after(x_a + x_b, undo_b)
    for size in sizes:
        in_parts.append(in_grad(ctx_arg, xs, grads_in, copies, first, size))
        first += size
        xs = after(x_a + x_b, in_parts[-1])
        if len(in_parts) == 1:
            came = to_ctx(after(in_parts[0][1], halves[1]))
    in_parts[3], came, grads_b = lax.optimization_barrier((in_parts[3], came, grads_b))
    halves.append(add_low((in_parts[0][0], came)))
    came = to_ctx(after(in_parts[2][1], halves[2]))

    produced, row_grad = after((produced_a + produced_b, grads_a + grads_b), in_parts)
    layer_output, middle_grad, *outs = combine(
        exp_arg, place, expert_ids, probs, middle, cotangent, normed_moe, moe_gain,
        router_weight.T.astype(f32), out_weight, produced, row_grad, mixed, copies,
    )
    outs, came = lax.optimization_barrier((outs, came))
    halves.append(add_low((in_parts[2][0], came)))
    early = outs[heads:]
    mixed_grad = [swap_blocks(part, pair) for part in outs[:heads]]
    rows_dev = width // (n_dp * groups)

    def sum_dp(half):
        return lax.psum_scatter(half, "dp", scatter_dimension=0, tiled=True)

    down_sums = [sum_dp(halves[0]), sum_dp(halves[1])]
    last_own, last_other = [sum_dp(half) for half in in_parts[1]]
    in_sums = [sum_dp(halves[2]), None, sum_dp(halves[3]), None]

    buckets = bias_table.shape[0] // copies
    lanes = -(-(3 * HEAD_DIM + 1) // 128) * 128
    backward, grads = [], []
    for h in range(heads):
        arg = after(mixed_grad[h], backward)
        beside = [grads[h - 1]] if h else []
        if h == 0:
            came = to_ctx(after(in_parts[3][1], arg))
            early_parts = exchange(after(early, arg))
            beside += [came, early_parts, last_own, last_other] + mixed_grad[1:2]
        if h == heads - 1:
            last_came = to_ctx(after(last_other, arg))
            beside += [last_came, in_sums[0]] + ([early_parts] if h else [])
        out = attention_bwd(
            order, chunks, table_dev[:, h], buck, kmask, hide, qkv[h], forward[h][0],
            arg, forward[h][1], step_k,
        )
        out, beside = lax.optimization_barrier((out, beside))
        if h == 0:
            came, early_parts = beside[0], beside[1]
            in_sums[3] = sum_dp(add_low((in_parts[3][0], came)))
            early_parts = scatter_dp(add_low(early_parts))
        if h == heads - 1:
            in_sums[1] = add_low((last_own, after(last_came, out)))
            early_half = add_low(early_parts)
        backward.append(out)
        grads.append(swap_blocks(out[0], pair))
    packed = []
    for out, offsets in backward:
        columns = jnp.transpose(after(out, backward), (1, 2, 0, 3))
        columns = columns.reshape(3 * HEAD_DIM, groups * tok)
        local_grad = dot_f32(normed_seq, columns, 0, 1)
        table_grad = jnp.sum(offsets, axis=1)
        spread = jnp.pad(
            jnp.broadcast_to(
                table_grad.reshape(n_dp, n_ctx, 1, buckets), (n_dp, n_ctx, n_exp, buckets)
            ),
            ((0, 0), (0, 0), (0, 0), (0, rows_dev - buckets)),
        ).reshape(width, 1)
        local_grad = jnp.pad(local_grad, ((0, 0), (0, lanes - 3 * HEAD_DIM)))
        lane = jnp.arange(lanes)[None, :]
        packed.append(jnp.where(lane == 3 * HEAD_DIM, spread, local_grad).astype(bf16))
    packed, grads = lax.optimization_barrier((jnp.concatenate(packed, axis=1), grads))
    late = scatter_dp(packed)
    input_grad = input_gradient(layer_input, attn_gain, middle_grad, qkv_weight, grads)
    input_grad, late = lax.optimization_barrier((input_grad, late))
    late = add_low(late)
    early_half = early_half.reshape(n_ctx, rows_dev, width + 128)
    early_own, early_other = [
        lax.dynamic_index_in_dim(early_half, at, 0, False) for at in (ctx_index, 1 - ctx_index)
    ]
    early_rows = early_own.astype(f32) + lax.ppermute(
        early_other, "ctx", [(0, 1), (1, 0)]
    ).astype(f32)
    expert_in_grad = jnp.concatenate(in_sums, axis=1).astype(f32)
    expert_down_grad = jnp.concatenate(down_sums, axis=1).astype(f32)
    rows_out = swap_blocks(in_swap_order(late.reshape(groups, rows_dev, -1)), pair)
    my_rows = ((lax.axis_index("dp") * n_ctx + ctx_index) * n_exp + exp_index) * rows_dev
    qkv_grad, attn_gain_grad, bias_rows = finish(
        exp_arg,
        rows_out,
        lax.dynamic_slice_in_dim(qkv_weight, my_rows, rows_dev, 0),
        lax.dynamic_slice_in_dim(attn_gain, my_rows, rows_dev, 0).reshape(rows_dev, 1),
        heads,
        lanes,
        n_ctx,
    )
    router_grad = sum(
        early_rows[:, width + i * experts : width + (i + 1) * experts] for i in range(3)
    )
    return (
        layer_output,
        input_grad,
        attn_gain_grad.reshape(rows_dev),
        qkv_grad,
        early_rows[:, :width],
        bias_rows[:buckets],
        early_rows[:, width + 3 * experts],
        router_grad,
        expert_in_grad[None],
        expert_down_grad,
    )


def solution(mesh):
    rows = P(("dp", "ctx", "expert"), None)
    return jax.shard_map(
        shards,
        mesh=mesh,
        in_specs=(
            rows,
            P(),
            P(),
            P(),
            P(None, "expert"),
            P(),
            P(),
            P("expert", None, None),
            P("expert", None, None),
            rows,
            rows,
            P("dp", None),
            P(),
            rows,
        ),
        out_specs=(
            rows,
            rows,
            P(("dp", "ctx", "expert")),
            rows,
            rows,
            P(("dp", "ctx"), "expert"),
            P(("dp", "ctx", "expert")),
            rows,
            P("expert", ("dp", "ctx"), None),
            P("expert", None, ("dp", "ctx")),
        ),
        check_vma=False,
    )
```

```python
import functools

import jax
import jax.numpy as jnp
from jax import lax
from jax.experimental import pallas as pl
from jax.experimental.pallas import tpu as pltpu
from jax.sharding import PartitionSpec as P


HEAD_DIM = 64
TOP = 2
LOG2E = 1.4426950408889634
SCALE = 0.125 * LOG2E
HIDE = -(2.0**100)
f32 = jnp.float32
bf16 = jnp.bfloat16
highest = lax.Precision.HIGHEST
NN = (((1,), (0,)), ((), ()))
NT = (((1,), (1,)), ((), ()))
TN = (((0,), (0,)), ((), ()))


def mm(left, right, dims):
    return lax.dot_general(left, right, dims, preferred_element_type=f32)


def stack_refs(refs):
    return jnp.concatenate([ref[...] for ref in refs], axis=0)


def cost(flops, bytes_accessed, transcendentals=0):
    return pl.CostEstimate(
        flops=int(flops), bytes_accessed=int(bytes_accessed), transcendentals=int(transcendentals)
    )


def fill_table(tab_ref, buck_ref, tb_ref, width, mul):
    buck = buck_ref[...]
    row = jnp.zeros(buck.shape, f32)
    for b in range(tab_ref.shape[0]):
        row = jnp.where(buck == b, tab_ref[b] * mul, row)
    for m in range(16):
        rolled = pltpu.roll(row, 8 * m, 1, stride=1, stride_axis=0)
        for c in range(width // 128 - 1):
            lo = width - 128 - 128 * c
            tb_ref[16 * c + m] = rolled[:, lo : lo + 128]


def bias_tile(tb_ref, start, rows, cols):
    parts = [
        tb_ref[pl.ds(start - 16 * c, rows // 8)].reshape(rows, 128) for c in range(cols // 128)
    ]
    return jnp.concatenate(parts, axis=1)


def attention_fwd_kernel(
    bk, order, nch_ref, tab_ref, buck_ref, kmask_ref, qmask_ref, q_ref, k_ref, v_ref,
    o_ref, lse_ref, kaug, vaug, tb,
):
    qi = pl.program_id(0)
    blocks, _, _, tok = k_ref.shape
    length = blocks * tok

    @pl.when(qi == 0)
    def _():
        fill_table(tab_ref, buck_ref, tb, 2 * length, LOG2E)
        first = lax.broadcasted_iota(jnp.int32, (16, length), 0) == 0
        vaug[HEAD_DIM:, :] = first.astype(f32).astype(bf16)
        for p in range(blocks):
            rows = slice(p * tok, (p + 1) * tok)
            kaug[rows, :] = jnp.concatenate([k_ref[order(p), 0], kmask_ref[:, rows]], axis=0).T
            vaug[0:HEAD_DIM, rows] = v_ref[order(p), 0]

    qaug = jnp.concatenate([q_ref[0, 0], qmask_ref[...]], axis=0)
    base = (length - 128) // 8 - qi * (tok // 8)

    def step(j, carry):
        peak, acc = carry
        ks = pl.ds(pl.multiple_of(j * bk, bk), bk)
        scores = mm(kaug[ks, :], qaug, NN) * SCALE + bias_tile(tb, base + j * (bk // 8), bk, tok)
        now = jnp.maximum(peak, jnp.max(scores, axis=0, keepdims=True))
        weights = jnp.exp2(scores - now).astype(bf16)
        return now, acc * jnp.exp2(peak - now) + mm(vaug[:, ks], weights, NN)

    start = (jnp.full((1, tok), -1e37, f32), jnp.zeros((HEAD_DIM + 16, tok), f32))
    peak, acc = lax.fori_loop(0, nch_ref[qi], step, start)
    total = acc[HEAD_DIM : HEAD_DIM + 1]
    o_ref[0] = (acc[0:HEAD_DIM] / total).astype(bf16)
    lse_ref[0] = peak + jnp.log2(total)


def attention_fwd(order, chunks, table, buck, kmask, qmask, qkv, bk):
    blocks, _, dim, tok = qkv.shape
    length = blocks * tok
    return pl.pallas_call(
        functools.partial(attention_fwd_kernel, bk, order),
        grid_spec=pltpu.PrefetchScalarGridSpec(
            num_scalar_prefetch=2,
            grid=(blocks,),
            in_specs=[
                pl.BlockSpec((8, 2 * length), lambda i, *_: (0, 0)),
                pl.BlockSpec((64, length), lambda i, *_: (0, 0)),
                pl.BlockSpec((64, tok), lambda i, *_: (0, i)),
                pl.BlockSpec((1, 1, dim, tok), lambda i, *_: (order(i), 0, 0, 0)),
                pl.BlockSpec((blocks, 1, dim, tok), lambda i, *_: (0, 1, 0, 0)),
                pl.BlockSpec((blocks, 1, dim, tok), lambda i, *_: (0, 2, 0, 0)),
            ],
            out_specs=[
                pl.BlockSpec((1, dim, tok), lambda i, *_: (order(i), 0, 0)),
                pl.BlockSpec((1, 1, tok), lambda i, *_: (i, 0, 0)),
            ],
            scratch_shapes=[
                pltpu.VMEM((length, 128), bf16),
                pltpu.VMEM((dim + 16, length), bf16),
                pltpu.VMEM((2 * length // 8 - 16, 8, 128), f32),
            ],
        ),
        out_shape=[
            jax.ShapeDtypeStruct((blocks, dim, tok), bf16),
            jax.ShapeDtypeStruct((blocks, 1, tok), f32),
        ],
        compiler_params=pltpu.CompilerParams(vmem_limit_bytes=60 << 20),
        cost_estimate=cost(2000 * length * length // 2, 4 * length * 2 * dim, length * length // 2),
        name="attention_fwd",
    )(chunks, table, buck, kmask, qmask, qkv, qkv, qkv)


def three_rows(values, rows):
    high = values.astype(bf16).astype(f32)
    mid = (values - high).astype(bf16).astype(f32)
    row = lax.broadcasted_iota(jnp.int32, (rows, values.shape[1]), 0)
    out = jnp.where(row == 0, high, jnp.where(row == 1, mid, jnp.where(row == 2, values - high - mid, 0.0)))
    return out.astype(bf16)


def attention_bwd_kernel(
    bk, order, nch_ref, tab_ref, buck_ref, kmask_ref, qmask_ref, q_ref, k_ref, v_ref, o_ref,
    do_ref, lse_ref, out_ref, off_ref, knat, kaug, vaug, tb, gb, dkacc, dvacc,
):
    qi = pl.program_id(0)
    blocks, _, _, tok = k_ref.shape
    length = blocks * tok

    @pl.when(qi == 0)
    def _():
        fill_table(tab_ref, buck_ref, tb, 2 * length, LOG2E)
        gb[...] = jnp.zeros_like(gb)
        dkacc[...] = jnp.zeros_like(dkacc)
        dvacc[...] = jnp.zeros_like(dvacc)
        three = lax.broadcasted_iota(jnp.int32, (64, length), 0) < 3
        vaug[64:128, :] = three.astype(f32).astype(bf16)
        kaug[64:128, :] = kmask_ref[...]
        for p in range(blocks):
            rows = slice(p * tok, (p + 1) * tok)
            knat[rows, :] = k_ref[order(p), 0].T
            kaug[0:64, rows] = k_ref[order(p), 0]
            vaug[0:64, rows] = v_ref[order(p), 0]

    q_t = q_ref[0, 0]
    do_t = do_ref[0]
    delta = jnp.sum(do_t.astype(f32) * o_ref[0].astype(f32), axis=0, keepdims=True)
    lse = lse_ref[0] * (1.0 / SCALE)
    blank = jnp.zeros((32, tok), bf16)
    qaug = jnp.concatenate([q_t, qmask_ref[...], three_rows(-lse, 16), blank], axis=0).T
    doaug = jnp.concatenate([do_t, three_rows(-delta, 32), blank], axis=0).T
    base = (length - 128) // 8 + qi * (tok // 8)

    def step(j, dq):
        ks = pl.ds(pl.multiple_of(j * bk, bk), bk)
        start = base - j * (bk // 8)
        probs = jnp.exp2(mm(qaug, kaug[:, ks], NN) * SCALE + bias_tile(tb, start, tok, bk))
        ds = probs * mm(doaug, vaug[:, ks], NN)
        for c in range(bk // 128):
            at = pl.ds(start - 16 * c, tok // 8)
            gb[at] += ds[:, 128 * c : 128 * c + 128].reshape(tok // 8, 8, 128)
        low = ds.astype(bf16)
        dvacc[:, ks] += mm(do_t, probs.astype(bf16), NN)
        dkacc[:, ks] += mm(q_t, low, NN)
        return dq + mm(low, knat[ks, :], NN)

    dq = lax.fori_loop(0, nch_ref[qi], step, jnp.zeros((tok, 64), f32))
    out_ref[order(qi), 0] = (dq * 0.125).T.astype(bf16)

    @pl.when(qi == blocks - 1)
    def _():
        for p in range(blocks):
            rows = slice(p * tok, (p + 1) * tok)
            out_ref[order(p), 1] = (dkacc[:, rows] * 0.125).astype(bf16)
            out_ref[order(p), 2] = dvacc[:, rows].astype(bf16)
        width = 2 * length
        total = jnp.zeros((8, width), f32)
        for m in range(16):
            tiles = [gb[16 * c + m] for c in range(width // 128 - 2, -1, -1)]
            skewed = jnp.concatenate([jnp.zeros((8, 128), f32)] + tiles, axis=1)
            total = total + (pltpu.roll(skewed, width - 8 * m, 1) if m else skewed)
        row = total[0:1]
        for s in range(1, 8):
            row = row + pltpu.roll(total[s : s + 1], width - s, 1)
        buck = buck_ref[0:1, :]
        for b in range(off_ref.shape[0]):
            mine = jnp.where(buck == b, row, 0.0)
            parts = [mine[:, 128 * c : 128 * c + 128] for c in range(width // 128)]
            while len(parts) > 1:
                parts = [x + y for x, y in zip(parts[::2], parts[1::2])]
            off_ref[b : b + 1, :] = parts[0]


def attention_bwd(order, chunks, table, buck, kmask, qmask, qkv, mixed, mixed_grad, lse, bk):
    blocks, _, dim, tok = qkv.shape
    length = blocks * tok
    one = pl.BlockSpec((1, dim, tok), lambda i, *_: (order(i), 0, 0))
    return pl.pallas_call(
        functools.partial(attention_bwd_kernel, bk, order),
        grid_spec=pltpu.PrefetchScalarGridSpec(
            num_scalar_prefetch=2,
            grid=(blocks,),
            in_specs=[
                pl.BlockSpec((8, 2 * length), lambda i, *_: (0, 0)),
                pl.BlockSpec((64, length), lambda i, *_: (0, 0)),
                pl.BlockSpec((16, tok), lambda i, *_: (0, i)),
                pl.BlockSpec((1, 1, dim, tok), lambda i, *_: (order(i), 0, 0, 0)),
                pl.BlockSpec((blocks, 1, dim, tok), lambda i, *_: (0, 1, 0, 0)),
                pl.BlockSpec((blocks, 1, dim, tok), lambda i, *_: (0, 2, 0, 0)),
                one,
                one,
                pl.BlockSpec((1, 1, tok), lambda i, *_: (i, 0, 0)),
            ],
            out_specs=[
                pl.BlockSpec((blocks, 3, dim, tok), lambda i, *_: (0, 0, 0, 0)),
                pl.BlockSpec((table.shape[0], 128), lambda i, *_: (0, 0)),
            ],
            scratch_shapes=[
                pltpu.VMEM((length, dim), bf16),
                pltpu.VMEM((128, length), bf16),
                pltpu.VMEM((128, length), bf16),
                pltpu.VMEM((2 * length // 8 - 16, 8, 128), f32),
                pltpu.VMEM((2 * length // 8 - 16, 8, 128), f32),
                pltpu.VMEM((dim, length), f32),
                pltpu.VMEM((dim, length), f32),
            ],
        ),
        out_shape=[
            jax.ShapeDtypeStruct((blocks, 3, dim, tok), bf16),
            jax.ShapeDtypeStruct((table.shape[0], 128), f32),
        ],
        compiler_params=pltpu.CompilerParams(vmem_limit_bytes=60 << 20),
        cost_estimate=cost(5000 * length * length // 2, 8 * length * 2 * dim, length * length // 2),
        name="attention_bwd",
    )(chunks, table, buck, kmask, qmask, qkv, qkv, qkv, mixed, mixed_grad, lse)


def write_groups(acc, refs):
    rows = refs[0].shape[0]
    for d, ref in enumerate(refs):
        ref[...] = acc[d * rows : (d + 1) * rows, :].astype(bf16)


def join_rows(refs, scratch):
    at = 0
    for ref in refs:
        scratch[at : at + ref.shape[0], :] = ref[:, : scratch.shape[1]]
        at += ref.shape[0]


def gate_column(refs):
    return jnp.concatenate(
        [jnp.sum(ref[...].astype(f32), axis=1, keepdims=True) for ref in refs], axis=0
    )


def expert_fwd_kernel(steps, groups, wg_ref, wu_ref, wd_ref, *refs):
    xs, refs = refs[:groups], refs[groups:]
    ht_ref, act_ref, slope_ref, *outs, rows, acc = refs
    f = pl.program_id(0)

    @pl.when(f == 0)
    def _():
        join_rows(xs, rows)
        acc[...] = jnp.zeros_like(acc)

    x = rows[...]
    gate = mm(x, wg_ref[0], NN)
    up = mm(x, wu_ref[0], NN)
    square = gate * gate
    t = jnp.tanh(gate * (0.7978845608028654 + 0.035677408136300125 * square))
    half = 0.5 + 0.5 * t
    act = gate * half
    slope = half + (gate * (0.5 - 0.5 * t * t)) * (
        0.7978845608028654 + 0.10703222440890037 * square
    )
    hidden = (act * up).astype(bf16)
    ht_ref[...] = hidden.T
    act_ref[...] = act.astype(bf16)
    slope_ref[...] = (slope * up).astype(bf16)
    acc[...] += mm(hidden, wd_ref[0], NN)

    @pl.when(f == steps - 1)
    def _():
        write_groups(acc, outs)


def expert_fwd(xs, w_in, w_down, tile=256):
    groups = len(xs)
    ff, width = w_down.shape[1:]
    rows = groups * xs[0].shape[0]
    steps = ff // tile
    part = pl.BlockSpec((rows, tile), lambda f: (0, f))
    inner = jax.ShapeDtypeStruct((rows, ff), bf16)
    one = pl.BlockSpec((rows // groups, width), lambda f: (0, 0))
    return pl.pallas_call(
        functools.partial(expert_fwd_kernel, steps, groups),
        grid=(steps,),
        in_specs=[
            pl.BlockSpec((1, width, tile), lambda f: (0, 0, f)),
            pl.BlockSpec((1, width, tile), lambda f: (0, 0, f + steps)),
            pl.BlockSpec((1, tile, width), lambda f: (0, f, 0)),
        ]
        + [pl.BlockSpec(xs[0].shape, lambda f: (0, 0))] * groups,
        out_specs=[pl.BlockSpec((tile, rows), lambda f: (f, 0)), part, part] + [one] * groups,
        out_shape=[jax.ShapeDtypeStruct((ff, rows), bf16), inner, inner]
        + [jax.ShapeDtypeStruct((rows // groups, width), bf16)] * groups,
        scratch_shapes=[pltpu.VMEM((rows, width), bf16), pltpu.VMEM((rows, width), f32)],
        compiler_params=pltpu.CompilerParams(vmem_limit_bytes=60 << 20),
        cost_estimate=cost(
            10 * rows * width * ff, 6 * width * ff + rows * (4 * width + 6 * ff), rows * ff
        ),
        name="expert_fwd",
    )(w_in, w_in, w_down, *xs)


def expert_bwd_kernel(steps, groups, act_ref, slope_ref, wg_ref, wu_ref, wd_ref, *refs):
    gs, gates, refs = refs[:groups], refs[groups : 2 * groups], refs[2 * groups :]
    grads_ref, *outs, pg, acc = refs
    f = pl.program_id(0)

    @pl.when(f == 0)
    def _():
        join_rows(gs, pg)
        pg[...] = (pg[...].astype(f32) * gate_column(gates)).astype(bf16)
        acc[...] = jnp.zeros_like(acc)

    hidden_grad = mm(pg[...], wd_ref[0], NT)
    dg = (slope_ref[...].astype(f32) * hidden_grad).astype(bf16)
    du = (act_ref[...].astype(f32) * hidden_grad).astype(bf16)
    grads_ref[0] = dg
    grads_ref[1] = du
    acc[...] += mm(dg, wg_ref[0], NT) + mm(du, wu_ref[0], NT)

    @pl.when(f == steps - 1)
    def _():
        write_groups(acc, outs)


def gate_block(x, width):
    return pl.BlockSpec((x.shape[0], 128), lambda f, *_: (0, width // 128))


def expert_bwd(gs, xs, act, slope, w_in, w_down, tile=256):
    groups = len(gs)
    rows, width = groups * gs[0].shape[0], gs[0].shape[1]
    ff = w_down.shape[1]
    steps = ff // tile
    part = pl.BlockSpec((rows, tile), lambda f: (0, f))
    one = pl.BlockSpec((rows // groups, width), lambda f: (0, 0))
    return pl.pallas_call(
        functools.partial(expert_bwd_kernel, steps, groups),
        grid=(steps,),
        in_specs=[
            part,
            part,
            pl.BlockSpec((1, width, tile), lambda f: (0, 0, f)),
            pl.BlockSpec((1, width, tile), lambda f: (0, 0, f + steps)),
            pl.BlockSpec((1, tile, width), lambda f: (0, f, 0)),
        ]
        + [one] * groups
        + [gate_block(x, width) for x in xs],
        out_specs=[pl.BlockSpec((2, rows, tile), lambda f: (0, 0, f))] + [one] * groups,
        out_shape=[jax.ShapeDtypeStruct((2, rows, ff), bf16)]
        + [jax.ShapeDtypeStruct((rows // groups, width), bf16)] * groups,
        scratch_shapes=[pltpu.VMEM((rows, width), bf16), pltpu.VMEM((rows, width), f32)],
        compiler_params=pltpu.CompilerParams(vmem_limit_bytes=60 << 20),
        cost_estimate=cost(
            10 * rows * width * ff, 6 * width * ff + rows * (4 * width + 8 * ff)
        ),
        name="expert_bwd",
    )(act, slope, w_in, w_in, w_down, *gs, *xs)


def column_block(ref, blk, ctx, flip, a):
    low = ref[:, 2 * a * blk : (2 * a + 1) * blk]
    high = ref[:, (2 * a + 1) * blk : (2 * a + 2) * blk]
    return jnp.where(lax.rem(ctx + flip, 2) == 0, low, high)


def turn_kernel(copies, ctx_ref, *refs):
    xs, xt_ref = refs[:-1], refs[-1]
    blk = xt_ref.shape[0] // copies
    at = 0
    for x_ref in xs:
        rows = x_ref.shape[0]
        for flip in range(2):
            for a in range(copies // 2):
                to = (flip * (copies // 2) + a) * blk
                block = column_block(x_ref, blk, ctx_ref[0], flip, a)
                xt_ref[to : to + blk, at : at + rows] = block.T
        at += rows


def turn(ctx, xs, copies):
    width = xs[0].shape[1] - 128
    total = sum(x.shape[0] for x in xs)
    return pl.pallas_call(
        functools.partial(turn_kernel, copies),
        in_specs=[pl.BlockSpec(memory_space=pltpu.SMEM)]
        + [pl.BlockSpec(memory_space=pltpu.VMEM)] * len(xs),
        out_specs=pl.BlockSpec(memory_space=pltpu.VMEM),
        out_shape=jax.ShapeDtypeStruct((width, total), bf16),
        compiler_params=pltpu.CompilerParams(vmem_limit_bytes=60 << 20),
        cost_estimate=cost(2 * total * width, 4 * total * width),
        name="turn",
    )(ctx, *xs)


def in_grad_kernel(*refs):
    x_refs, (*gs, own_ref, other_ref) = refs[:4], refs[4:]
    grads = jnp.concatenate([g[0] for g in gs], axis=0)
    half = own_ref.shape[0]
    grad = mm(stack_refs(x_refs), grads, NN).astype(bf16)
    own_ref[...] = grad[:half]
    other_ref[...] = grad[half:]


def in_grad(xt, grads, first, count, tile=256):
    width, total = xt.shape
    steps = grads[0].shape[2] // tile
    half = jax.ShapeDtypeStruct((width // 2, count * tile), bf16)
    out = pl.BlockSpec((width // 2, tile), lambda f: (0, f))

    def at(f):
        return ((f + first) // steps, 0, (f + first) % steps)

    return pl.pallas_call(
        in_grad_kernel,
        grid=(count,),
        in_specs=[pl.BlockSpec((width // 4, total), lambda f, i=i: (i, 0)) for i in range(4)]
        + [pl.BlockSpec((1, g.shape[1], tile), at) for g in grads],
        out_specs=[out, out],
        out_shape=[half, half],
        compiler_params=pltpu.CompilerParams(vmem_limit_bytes=60 << 20),
        cost_estimate=cost(
            4 * total * width * count * tile, 2 * (total + width) * count * tile + 2 * total * width
        ),
        name="in_grad",
    )(*[xt] * 4, *grads)


def down_grad_kernel(copies, n, ctx_ref, *refs):
    ps, gates, (*hs, own_ref, other_ref, pg) = refs[:n], refs[n : 2 * n], refs[2 * n :]
    blk = ps[0].shape[1] // copies

    @pl.when(pl.program_id(0) == 0)
    def _():
        at = 0
        for p_ref, gate_ref in zip(ps, gates):
            rows = p_ref.shape[0]
            gate = gate_column([gate_ref])
            for flip in range(2):
                for a in range(copies // 2):
                    to = (flip * (copies // 2) + a) * blk
                    block = column_block(p_ref, blk, ctx_ref[0], flip, a).astype(f32)
                    pg[at : at + rows, to : to + blk] = (block * gate).astype(bf16)
            at += rows

    grad = mm(jnp.concatenate([h[...] for h in hs], axis=1), pg[...], NN).astype(bf16)
    for a in range(copies // 2):
        own_ref[a] = grad[:, a * blk : (a + 1) * blk]
        to = (copies // 2 + a) * blk
        other_ref[a] = grad[:, to : to + blk]


def down_grad(ctx, hs, ps, xs, copies, first, count, tile=256):
    ff = count * tile
    width = ps[0].shape[1]
    total = sum(h.shape[1] for h in hs)
    blk = width // copies
    half = jax.ShapeDtypeStruct((copies // 2, ff, blk), bf16)
    out = pl.BlockSpec((copies // 2, tile, blk), lambda f, c: (0, f, 0))
    return pl.pallas_call(
        functools.partial(down_grad_kernel, copies, len(ps)),
        grid_spec=pltpu.PrefetchScalarGridSpec(
            num_scalar_prefetch=1,
            grid=(count,),
            in_specs=[pl.BlockSpec(p.shape, lambda f, c: (0, 0)) for p in ps]
            + [gate_block(x, width) for x in xs]
            + [pl.BlockSpec((tile, h.shape[1]), lambda f, c: (f + first, 0)) for h in hs],
            out_specs=[out, out],
            scratch_shapes=[pltpu.VMEM((total, width), bf16)],
        ),
        out_shape=[half, half],
        compiler_params=pltpu.CompilerParams(vmem_limit_bytes=60 << 20),
        cost_estimate=cost(4 * total * width * ff, 2 * (total * (width + ff) + width * ff)),
        name="down_grad",
    )(ctx, *ps, *xs, *hs)


def project_kernel(x_ref, gain_ref, *refs):
    w_refs, (normed_t, *outs) = refs[:4], refs[4:]
    heads = len(outs)

    @pl.when((pl.program_id(0) == 0) & (pl.program_id(1) == 0))
    def _():
        x = x_ref[...].astype(f32)
        scale = lax.rsqrt(jnp.mean(x * x, axis=1, keepdims=True) + 1e-06)
        normed = (x * scale * gain_ref[...]).astype(bf16)
        normed_t[...] = normed.T

    cols = w_refs[0].shape[1]
    tok = normed_t.shape[1]
    rows = mm(stack_refs(w_refs), normed_t[...], TN).astype(bf16)
    rows = rows.reshape(cols // (heads * HEAD_DIM), heads, HEAD_DIM, tok)
    for h in range(heads):
        outs[h][:, 0] = rows[:, h]


def project(x, gain, weight, groups, heads, cols=512):
    tok, width = x.shape
    per = cols // (heads * HEAD_DIM)
    blocks = width // cols
    return pl.pallas_call(
        project_kernel,
        grid=(3, blocks),
        in_specs=[
            pl.BlockSpec((tok, width), lambda p, j: (0, 0)),
            pl.BlockSpec((1, width), lambda p, j: (0, 0)),
        ]
        + [
            pl.BlockSpec((width // 4, cols), lambda p, j, i=i: (i, p * blocks + j))
            for i in range(4)
        ],
        out_specs=[pl.BlockSpec((width, tok), lambda p, j: (0, 0))]
        + [pl.BlockSpec((per, 1, HEAD_DIM, tok), lambda p, j: (j, p, 0, 0))] * heads,
        out_shape=[jax.ShapeDtypeStruct((width, tok), bf16)]
        + [jax.ShapeDtypeStruct((groups, 3, HEAD_DIM, tok), bf16)] * heads,
        compiler_params=pltpu.CompilerParams(vmem_limit_bytes=60 << 20),
        cost_estimate=cost(6 * tok * width * width, 6 * width * width + 10 * tok * width),
        name="project",
    )(x, gain.reshape(1, width), *[weight] * 4)


def input_grad_kernel(steps, x_ref, gain_ref, mid_ref, *refs):
    w_refs, (*grads, out_ref, acc) = refs[:4], refs[4:]
    step = pl.program_id(0)
    cols = w_refs[0].shape[1]
    tok = out_ref.shape[0]

    @pl.when(step == 0)
    def _():
        acc[...] = jnp.zeros_like(acc)

    rows = jnp.stack([g[:, 0] for g in grads], axis=1).reshape(cols, tok)
    acc[...] += mm(stack_refs(w_refs), rows, NN)

    @pl.when(step == steps - 1)
    def _():
        x = x_ref[...].astype(f32)
        scale = lax.rsqrt(jnp.mean(x * x, axis=1, keepdims=True) + 1e-06)
        dy = acc[...].T * gain_ref[...]
        pull = jnp.mean(x * dy, axis=1, keepdims=True)
        out_ref[...] = mid_ref[...] + scale * dy - x * (scale * scale * scale * pull)


def input_gradient(x, gain, middle_grad, weight, grads, cols=512):
    tok, width = x.shape
    heads = len(grads)
    per = cols // (heads * HEAD_DIM)
    blocks = width // cols
    whole = pl.BlockSpec((tok, width), lambda s: (0, 0))
    return pl.pallas_call(
        functools.partial(input_grad_kernel, 3 * blocks),
        grid=(3 * blocks,),
        in_specs=[
            whole,
            pl.BlockSpec((1, width), lambda s: (0, 0)),
            whole,
        ]
        + [pl.BlockSpec((width // 4, cols), lambda s, i=i: (i, s)) for i in range(4)]
        + [
            pl.BlockSpec((per, 1, HEAD_DIM, tok), lambda s: (s % blocks, s // blocks, 0, 0))
            for _ in grads
        ],
        out_specs=whole,
        out_shape=jax.ShapeDtypeStruct((tok, width), f32),
        scratch_shapes=[pltpu.VMEM((width, tok), f32)],
        compiler_params=pltpu.CompilerParams(vmem_limit_bytes=60 << 20),
        cost_estimate=cost(6 * tok * width * width, 6 * width * width + 16 * tok * width),
        name="input_grad",
    )(x, gain.reshape(1, width), middle_grad, *[weight] * 4, *grads)


def wide_thirds(values):
    high = values.astype(bf16)
    rest = values - high.astype(f32)
    mid = rest.astype(bf16)
    low = (rest - mid.astype(f32)).astype(bf16)
    rows, lanes = values.shape
    blank = jnp.zeros((rows, 128 - 3 * lanes), bf16)
    return jnp.concatenate([high, mid, low, blank], axis=1)


def combine_kernel(
    counts, exp_ref, place_ref, ids_ref, probs_ref, middle_ref, cot_ref, normed_ref, gain_ref,
    router_ref, weight_ref, *refs,
):
    blocks, heads, parts, copies = counts
    experts = probs_ref.shape[1]
    backs, refs = refs[:blocks], refs[blocks:]
    row_grads, refs = refs[:blocks], refs[blocks:]
    mixed, refs = refs[:heads], refs[heads:]
    out_ref, mid_ref, refs = refs[0], refs[1], refs[2:]
    mixed_grads, refs = refs[:heads], refs[heads:]
    early, (slot_rows, slot_grads, wide) = refs[:parts], refs[parts:]
    tok, width = middle_ref.shape
    total = slot_rows.shape[0]

    at = 0
    for back, row_grad in zip(backs, row_grads):
        rows = slice(at, at + back.shape[0])
        slot_rows[rows, :] = back[...]
        slot_grads[rows, :] = row_grad[...]
        at += back.shape[0]

    slot = lax.broadcasted_iota(jnp.int32, (tok, total), 1)
    one = (slot == place_ref[:, 0:1]).astype(f32).astype(bf16)
    two = (slot == place_ref[:, 1:2]).astype(f32).astype(bf16)
    first = mm(one, slot_rows[...], NN)
    second = mm(two, slot_rows[...], NN)
    dy = mm(one + two, slot_grads[...], NN)

    lane = lax.broadcasted_iota(jnp.int32, (tok, experts), 1)
    is_first, is_second = lane == ids_ref[:, 0:1], lane == ids_ref[:, 1:2]
    probs = probs_ref[...]
    gate_first = jnp.sum(jnp.where(is_first, probs, 0.0), axis=1, keepdims=True)
    gate_second = jnp.sum(jnp.where(is_second, probs, 0.0), axis=1, keepdims=True)
    middle = middle_ref[...]
    cot = cot_ref[...].astype(f32)
    out_ref[...] = (middle + gate_first * first + gate_second * second).astype(bf16)
    grad_first = jnp.sum(cot * first, axis=1, keepdims=True)
    grad_second = jnp.sum(cot * second, axis=1, keepdims=True)
    probs_grad = jnp.where(is_first, grad_first, 0.0) + jnp.where(is_second, grad_second, 0.0)
    logits_grad = probs * (probs_grad - jnp.sum(probs * probs_grad, axis=1, keepdims=True))
    for e in range(experts):
        dy = dy + logits_grad[:, e : e + 1] * router_ref[e : e + 1, :]

    scale = lax.rsqrt(jnp.mean(middle * middle, axis=1, keepdims=True) + 1e-06)
    unit = middle * scale
    gain_terms = unit * dy
    dy = dy * gain_ref[...]
    middle_grad = cot + scale * (dy - unit * jnp.mean(unit * dy, axis=1, keepdims=True))
    mid_ref[...] = middle_grad
    branch = middle_grad.astype(bf16)

    groups, dim, _ = mixed_grads[0].shape
    back = mm(weight_ref[...], branch, NT).astype(bf16).reshape(groups, heads, dim, tok)
    for h in range(heads):
        mixed_grads[h][...] = back[:, h]
    for h in range(heads):
        grad = mm(mixed[h][...], branch, NN)
        for g in range(groups):
            at = (g * heads + h) * dim
            wide[at : at + dim, 0:width] = grad[g * dim : (g + 1) * dim]
    mark = lax.broadcasted_iota(jnp.int32, (tok, 128), 1) == 3 * experts
    mark = mark.astype(f32).astype(bf16)
    high = gain_terms.astype(bf16)
    low = (gain_terms - high.astype(f32)).astype(bf16)
    wide[:, width:] = (
        mm(normed_ref[...], wide_thirds(logits_grad), TN) + mm(high, mark, TN) + mm(low, mark, TN)
    )
    per = wide.shape[0] // (parts * copies)
    for d in range(parts):
        e = jnp.bitwise_xor(exp_ref[0], d)
        rows = [
            wide[pl.ds(pl.multiple_of((k * parts + e) * per, per), per), :] for k in range(copies)
        ]
        early[d][...] = jnp.concatenate(rows, axis=0).astype(bf16)


def combine(
    exp, place, ids, probs, middle, cot, normed, gain, router, weight, backs, row_grads, mixed,
    copies,
):
    tok, width = middle.shape
    heads = len(mixed)
    parts = probs.shape[1]
    groups = width // (heads * HEAD_DIM)
    total = sum(b.shape[0] for b in backs)
    sds = jax.ShapeDtypeStruct
    return pl.pallas_call(
        functools.partial(combine_kernel, (len(backs), heads, parts, copies)),
        in_specs=[pl.BlockSpec(memory_space=pltpu.SMEM)]
        + [pl.BlockSpec(memory_space=pltpu.VMEM)] * (9 + 2 * len(backs) + heads),
        out_specs=[pl.BlockSpec(memory_space=pltpu.VMEM)] * (2 + heads + parts),
        out_shape=[sds((tok, width), bf16), sds((tok, width), f32)]
        + [sds((groups, HEAD_DIM, tok), bf16)] * heads
        + [sds((width // parts, width + 128), bf16)] * parts,
        scratch_shapes=[
            pltpu.VMEM((total, width), bf16),
            pltpu.VMEM((total, width), bf16),
            pltpu.VMEM((width, width + 128), f32),
        ],
        compiler_params=pltpu.CompilerParams(vmem_limit_bytes=60 << 20),
        cost_estimate=cost(
            6 * tok * total * width + 4 * tok * width * width,
            4 * total * width + 18 * tok * width + 4 * width * width,
        ),
        name="combine",
    )(exp, place, ids, probs, middle, cot, normed, gain.reshape(1, width), router, weight,
      *backs, *row_grads, *mixed)


def finish_kernel(heads, lanes, n_ctx, exp_ref, rows_ref, weight_ref, gain_ref, grad_ref, gain_grad_ref, bias_ref):
    groups = rows_ref.shape[0]
    width = weight_ref.shape[1] // 3
    for part in range(3):
        pieces = []
        for g in range(groups):
            for h in range(heads):
                lo = h * lanes + part * HEAD_DIM
                pieces.append(rows_ref[g][:, lo : lo + HEAD_DIM].astype(f32))
        grad_ref[:, part * width : (part + 1) * width] = jnp.concatenate(pieces, axis=1)
    terms = weight_ref[...].astype(f32) * grad_ref[...]
    gain_grad_ref[...] = jnp.sum(terms, axis=1, keepdims=True) / gain_ref[...]
    columns = []
    for c in range(n_ctx):
        mine = rows_ref[exp_ref[0] * n_ctx + c].astype(f32)
        for h in range(heads):
            lo = h * lanes + 3 * HEAD_DIM
            columns.append(mine[:, lo : lo + 1])
    bias_ref[...] = jnp.concatenate(columns, axis=1)


def finish(exp, rows, weight_rows, gain_rows, heads, lanes, n_ctx):
    count, columns = weight_rows.shape
    sds = jax.ShapeDtypeStruct
    vmem = pl.BlockSpec(memory_space=pltpu.VMEM)
    return pl.pallas_call(
        functools.partial(finish_kernel, heads, lanes, n_ctx),
        in_specs=[pl.BlockSpec(memory_space=pltpu.SMEM), vmem, vmem, vmem],
        out_specs=[vmem, vmem, vmem],
        out_shape=[
            sds((count, columns), f32), sds((count, 1), f32), sds((count, heads * n_ctx), f32)
        ],
        cost_estimate=cost(4 * count * columns, 8 * count * columns),
        name="finish",
    )(exp, rows, weight_rows, gain_rows)


def route_kernel(heads, x_ref, place_ref, ids_ref, gain_ref, router_ref, weight_ref, *refs):
    mixed, (middle_ref, normed_ref, probs_ref, *slots, joined) = refs[:heads], refs[heads:]
    tok, width = x_ref.shape
    experts = probs_ref.shape[1]
    for h in range(heads):
        for g in range(width // (heads * HEAD_DIM)):
            at = (g * heads + h) * HEAD_DIM
            joined[at : at + HEAD_DIM, :] = mixed[h][g * HEAD_DIM : (g + 1) * HEAD_DIM, :]
    middle = x_ref[...].astype(f32) + mm(joined[...], weight_ref[...], TN)
    middle_ref[...] = middle
    scale = lax.rsqrt(jnp.mean(middle * middle, axis=1, keepdims=True) + 1e-06)
    normed = (middle * scale * gain_ref[...]).astype(bf16)
    normed_ref[...] = normed
    logits = mm(normed, router_ref[...], NN)[:, :experts]
    weights = jnp.exp(logits - jnp.max(logits, axis=1, keepdims=True))
    probs = weights / jnp.sum(weights, axis=1, keepdims=True)
    probs_ref[...] = probs
    lane = lax.broadcasted_iota(jnp.int32, (tok, experts), 1)
    gates = [
        wide_thirds(jnp.sum(jnp.where(lane == ids_ref[:, j : j + 1], probs, 0.0), axis=1, keepdims=True))
        for j in range(2)
    ]
    at = 0
    for slot_ref in slots:
        rows = slot_ref.shape[0]
        slot = lax.broadcasted_iota(jnp.int32, (rows, tok), 0) + at
        one = (slot == place_ref[0:1, :]).astype(f32).astype(bf16)
        two = (slot == place_ref[1:2, :]).astype(f32).astype(bf16)
        slot_ref[:, 0:width] = mm(one + two, normed, NN).astype(bf16)
        slot_ref[:, width:] = (mm(one, gates[0], NN) + mm(two, gates[1], NN)).astype(bf16)
        at += rows


def route(x, place, ids, gain, router, weight, mixed, sizes):
    tok, width = x.shape
    experts = router.shape[1]
    heads = len(mixed)
    sds = jax.ShapeDtypeStruct
    vmem = pl.BlockSpec(memory_space=pltpu.VMEM)
    return pl.pallas_call(
        functools.partial(route_kernel, heads),
        in_specs=[vmem] * (6 + heads),
        out_specs=[vmem] * (3 + len(sizes)),
        out_shape=[sds((tok, width), f32), sds((tok, width), bf16), sds((tok, experts), f32)]
        + [sds((size, width + 128), bf16) for size in sizes],
        scratch_shapes=[pltpu.VMEM((width, tok), bf16)],
        compiler_params=pltpu.CompilerParams(vmem_limit_bytes=60 << 20),
        cost_estimate=cost(
            2 * tok * width * (width + sum(sizes)), 12 * tok * width + 2 * width * width
        ),
        name="route",
    )(x, place.T, ids, gain.reshape(1, width), jnp.pad(router, ((0, 0), (0, 128 - experts))),
      weight, *mixed)


def sequence_grad_kernel(n_exp, copies, dp_ref, out_ref, offsets_ref, *refs):
    normed_refs, (*shares, acc) = refs[:4], refs[4:]
    step = pl.program_id(0)
    width, lanes = acc.shape
    own = 3 * HEAD_DIM

    @pl.when(step == 0)
    def _():
        acc[...] = jnp.zeros_like(acc)

    normed = jnp.concatenate([ref[0] for ref in normed_refs], axis=0)
    acc[:, 0:own] += mm(normed, out_ref[0].reshape(own, out_ref.shape[3]), NT)

    @pl.when(step == pl.num_programs(0) - 1)
    def _():
        count = offsets_ref.shape[0]
        buckets, rows_dev = count // copies, width // (copies * n_exp)
        row = lax.broadcasted_iota(jnp.int32, (width, count), 0)
        bucket = lax.broadcasted_iota(jnp.int32, (width, count), 1)
        place = row // (n_exp * rows_dev) * buckets + row % rows_dev
        here = ((place == bucket) & (row % rows_dev < buckets)).astype(f32).astype(bf16)
        table = jnp.sum(offsets_ref[...], axis=1, keepdims=True)
        column = jnp.sum(mm(here, wide_thirds(table), NN), axis=1, keepdims=True)
        base = own // 128 * 128
        lane = lax.broadcasted_iota(jnp.int32, (width, 128), 1) + base
        acc[:, base : base + 128] += jnp.where(lane == own, column, 0.0)
        per = shares[0].shape[0]
        for d, share in enumerate(shares):
            start = pl.multiple_of(jnp.bitwise_xor(dp_ref[0], d) * per, per)
            share[...] = acc[pl.ds(start, per), :].astype(bf16)


def sequence_grad(dp, normed, out, offsets, n_dp, n_exp, copies, lanes):
    groups, _, dim, tok = out.shape
    width = normed.shape[1]
    return pl.pallas_call(
        functools.partial(sequence_grad_kernel, n_exp, copies),
        grid_spec=pltpu.PrefetchScalarGridSpec(
            num_scalar_prefetch=1,
            grid=(groups,),
            in_specs=[
                pl.BlockSpec((1, 3, dim, tok), lambda g, d: (g, 0, 0, 0)),
                pl.BlockSpec(offsets.shape, lambda g, d: (0, 0)),
            ]
            + [
                pl.BlockSpec((1, width // 4, tok), lambda g, d, i=i: (g, i, 0)) for i in range(4)
            ],
            out_specs=[pl.BlockSpec((width // n_dp, lanes), lambda g, d: (0, 0))] * n_dp,
            scratch_shapes=[pltpu.VMEM((width, lanes), f32)],
        ),
        out_shape=[jax.ShapeDtypeStruct((width // n_dp, lanes), bf16)] * n_dp,
        compiler_params=pltpu.CompilerParams(vmem_limit_bytes=60 << 20),
        cost_estimate=cost(
            6 * dim * groups * tok * width, 2 * groups * tok * (width + 3 * dim)
        ),
        name="sequence_grad",
    )(dp, out, offsets, *[normed] * 4)


def dot_f32(left, right, left_dim, right_dim):
    return mm(left, right, (((left_dim,), (right_dim,)), ((), ())))


def swap_blocks(blocks, axes):
    return lax.all_to_all(blocks, axes, split_axis=0, concat_axis=0, tiled=True)


def exchange(parts, axis="expert"):
    n = len(parts)
    return [parts[0]] + [
        lax.ppermute(parts[d], axis, [(i, i ^ d) for i in range(n)]) for d in range(1, n)
    ]


def add_low(parts):
    return sum(part.astype(f32) for part in parts).astype(bf16)


def after(value, *others):
    return lax.optimization_barrier((value, others))[0]


def attention_plan(block_row, bucket_ids, blocks, tok):
    length = blocks * tok
    pad = jnp.full((1,), -1, jnp.int32)
    buck_rev = jnp.broadcast_to(jnp.concatenate([pad, bucket_ids[::-1]])[None], (8, 2 * length))
    buck = jnp.broadcast_to(jnp.concatenate([pad, bucket_ids])[None], (8, 2 * length))
    ids = jnp.arange(16)
    hot = (block_row[None, :] == ids[:, None]).astype(bf16)
    hide = jnp.where(ids[:, None] > block_row[None, :], HIDE, 0.0).astype(bf16)
    kmask_t = jnp.concatenate(
        [hot, jnp.ones((3, length), bf16), jnp.zeros((45, length), bf16)], axis=0
    )
    qmask = jnp.concatenate([hide, jnp.zeros((48, length), bf16)], axis=0)
    last = block_row.reshape(blocks, tok)[:, -1]
    seen = jnp.sum((block_row[None, :] <= last[:, None]).astype(jnp.int32), axis=1)
    return buck_rev, buck, kmask_t, qmask, hide, seen


def shards(
    layer_input,
    attn_gain,
    qkv_weight,
    out_weight,
    bias_table,
    moe_gain,
    router_weight,
    expert_in,
    expert_down,
    expert_ids,
    fill_order,
    block_ids,
    bucket_ids,
    cotangent,
):
    tok, width = layer_input.shape
    n_dp, n_ctx, n_exp = lax.axis_size("dp"), lax.axis_size("ctx"), lax.axis_size("expert")
    groups = n_ctx * n_exp
    copies = n_dp * n_ctx
    head_exp = bias_table.shape[1]
    heads = head_exp // n_ctx
    experts = router_weight.shape[1]
    ff_width = expert_down.shape[1]
    capacity = 5 * TOP * tok // (4 * experts)
    cut = (capacity // 2 + 15) // 16 * 16
    spans = ((0, cut), (cut, capacity))
    ctx_index = lax.axis_index("ctx")
    exp_index = lax.axis_index("expert")
    ctx_arg = ctx_index.astype(jnp.int32).reshape(1)
    pair = ("expert", "ctx")
    step_k = 512

    def order(p):
        return (p % n_exp) * n_ctx + p // n_exp

    def in_swap_order(blocks):
        shape = blocks.shape
        return jnp.swapaxes(blocks.reshape((n_ctx, n_exp) + shape[1:]), 0, 1).reshape(shape)

    exp_arg = exp_index.astype(jnp.int32).reshape(1)
    normed_t, *parts = project(layer_input, attn_gain, qkv_weight, groups, heads)
    qkv = [swap_blocks(part, pair) for part in parts]
    table_dev = lax.dynamic_slice_in_dim(bias_table, ctx_index * heads, heads, 1)
    buck_rev, buck, kmask, qmask, hide, seen = attention_plan(
        block_ids[0], bucket_ids, groups, tok
    )
    chunks = (seen + step_k - 1) // step_k
    chunks_fwd = (seen + 2 * step_k - 1) // (2 * step_k)

    flat_ids = expert_ids.reshape(TOP * tok)
    fill_rank = fill_order.reshape(TOP * tok)
    same_expert = flat_ids[:, None] == flat_ids[None, :]
    earlier = fill_rank[None, :] < fill_rank[:, None]
    slot_of = jnp.sum((same_expert & earlier).astype(jnp.int32), axis=1)
    slots = slot_of.reshape(tok, TOP)
    part_at = jnp.where(slots < cut, 0, experts * cut - cut)
    stride = jnp.where(slots < cut, cut, capacity - cut)
    place = jnp.where(
        slots < capacity,
        part_at + jnp.bitwise_xor(expert_ids, exp_index) * stride + slots,
        -1,
    )
    sizes = [high - low for low, high in spans for _ in range(experts)]

    def to_slots(rows):
        parts, at = [], 0
        for size in sizes:
            slot = jnp.arange(at, at + size)[:, None]
            hot = (slot == place[None, :, 0]) | (slot == place[None, :, 1])
            parts.append(dot_f32(hot.astype(bf16), rows, 1, 0).astype(bf16))
            at += size
        return parts

    forward, mixed = [], []
    cot_slots = to_slots(cotangent)
    slots_a, slots_b = cot_slots[:experts], cot_slots[experts:]
    qkv[0], place, slots_a, slots_b, buck_rev, buck, kmask, qmask, hide = (
        lax.optimization_barrier(
            (qkv[0], place, slots_a, slots_b, buck_rev, buck, kmask, qmask, hide)
        )
    )
    normed_seq = lax.all_gather(after(normed_t, qkv[0]), pair)
    for h in range(heads):
        arg = after(qkv[h], forward)
        if h == heads - 1:
            grad_a = exchange(after(slots_a, arg))
        out = attention_fwd(
            order, chunks_fwd, table_dev[:, h], buck_rev, kmask, qmask, arg, 2 * step_k
        )
        out = after(out, qkv[h + 1] if h < heads - 1 else grad_a, mixed)
        forward.append(out)
        mixed.append(swap_blocks(out[0], pair).reshape(groups * HEAD_DIM, tok))
    mixed = after(mixed, forward)
    middle, normed_moe, probs, *sent = route(
        layer_input, place, expert_ids, moe_gain, router_weight, out_weight, mixed, sizes
    )
    x_a, x_b = exchange(sent[:experts]), exchange(sent[experts:])

    grad_b = exchange(after(slots_b, x_a))
    run_a = after(expert_fwd(x_a, expert_in, expert_down), x_b, grad_b)
    produced_a = exchange(list(run_a[3:]))
    run_b = expert_fwd(after(x_b, run_a), expert_in, expert_down)
    run_b = after(run_b, produced_a, normed_seq)
    produced_b = exchange(list(run_b[3:]))
    hidden = [run_a[0], run_b[0]]
    tiles = ff_width // 256
    cuts = (0, (tiles + 1) // 2, tiles)
    g_args = after(grad_a + grad_b, run_b)
    down_1 = down_grad(ctx_arg, hidden, g_args, x_a + x_b, copies, 0, cuts[1])

    def sum_dp(half):
        return lax.psum_scatter(half, "dp", scatter_dimension=0, tiled=True)

    def to_ctx(half):
        return lax.ppermute(half, "ctx", [(0, 1), (1, 0)])

    came = to_ctx(down_1[1])
    g_args = after(grad_a + grad_b, down_1)
    down_2 = down_grad(ctx_arg, hidden, g_args, x_a + x_b, copies, cuts[1], tiles - cuts[1])
    undo_a = expert_bwd(
        after(grad_a, down_2), x_a, run_a[1], run_a[2], expert_in, expert_down
    )
    undo_a, came = lax.optimization_barrier((after(undo_a, produced_b), came))
    halves = [add_low((down_1[0], came))]
    grads_a = exchange(list(undo_a[1:]))
    came = to_ctx(after(down_2[1], undo_a))
    undo_b = expert_bwd(
        after(grad_b, undo_a), x_b, run_b[1], run_b[2], expert_in, expert_down
    )
    undo_b, came = lax.optimization_barrier((after(undo_b, grads_a), came))
    halves.append(add_low((down_2[0], came)))
    grads_b = exchange(list(undo_b[1:]))
    grads_in = [undo_a[0], undo_b[0]]
    total = 2 * tiles
    size_a, size_d = total * 3 // 22, total * 8 // 22
    xt = turn(ctx_arg, x_a + x_b, copies)
    part_a = in_grad(after(xt, undo_b), grads_in, 0, size_a)
    came_a = to_ctx(after(part_a[1], halves[1]))
    part_b = in_grad(after(xt, part_a), grads_in, size_a, size_a)
    part_d = in_grad(after(xt, part_b), grads_in, 2 * size_a, size_d)

    part_d, grads_b, came_a = lax.optimization_barrier((part_d, grads_b, came_a))
    came_b = to_ctx(after(part_b[1], came_a))
    layer_output, middle_grad, *outs = combine(
        exp_arg, place, expert_ids, probs, middle, cotangent, normed_moe, moe_gain,
        router_weight.T.astype(f32), out_weight, produced_a + produced_b, grads_a + grads_b, mixed,
        copies,
    )
    down_sums = [sum_dp(half) for half in halves]
    outs, came_b, down_sums[0] = lax.optimization_barrier((outs, came_b, down_sums[0]))
    half_a = jnp.concatenate(
        [add_low((part_a[0], came_a)), add_low((part_b[0], came_b))], axis=1
    )
    first = 2 * size_a + size_d
    part_c = in_grad(after(xt, outs), grads_in, first, total - first)
    early = outs[heads:]
    mixed_grad = [swap_blocks(part, pair) for part in outs[:heads]]
    rows_dev = width // (n_dp * groups)

    last_own, last_other = [sum_dp(half) for half in part_d]
    sum_a = sum_dp(half_a)

    lanes = -(-(3 * HEAD_DIM + 1) // 128) * 128
    dp_arg = lax.axis_index("dp").astype(jnp.int32).reshape(1)
    backward, grads, late = [], [], []
    for h in range(heads):
        arg = after(mixed_grad[h], backward if h else part_c)
        beside = [grads[h - 1]] if h else []
        if h == 0:
            came_c = to_ctx(after(part_c[1], arg))
            early_parts = exchange(after(early, arg))
            beside += [came_c, early_parts, last_own, last_other, down_sums[1]] + mixed_grad[1:2]
        else:
            arg = after(arg, half_c)
        if h == heads - 1:
            last_came = to_ctx(after(last_other, arg))
            beside += [last_came, sum_a] + ([late] if h else [])
        out = attention_bwd(
            order, chunks, table_dev[:, h], buck, kmask, hide, qkv[h], forward[h][0],
            arg, forward[h][1], step_k,
        )
        out, beside = lax.optimization_barrier((out, beside))
        if h == 0:
            half_c = add_low((part_c[0], beside[0]))
            sum_c = sum_dp(half_c)
            early_half = sum_dp(add_low(beside[1]))
        elif h == heads - 1:
            late = beside[-1]
        backward.append(out)
        grads.append(swap_blocks(out[0], pair))
        shares = sequence_grad(dp_arg, normed_seq, *out, n_dp, n_exp, copies, lanes)
        late.append(exchange(shares, "dp"))
    in_sums = [sum_a, add_low((last_own, after(last_came, backward))), sum_c]
    late, grads = lax.optimization_barrier((late, grads))
    late = jnp.concatenate([add_low(parts) for parts in late], axis=1)
    rows_out = swap_blocks(in_swap_order(late.reshape(groups, rows_dev, -1)), pair)
    input_grad = input_gradient(layer_input, attn_gain, middle_grad, qkv_weight, grads)
    early_half = early_half.reshape(n_ctx, rows_dev, width + 128)
    early_own, early_other = [
        lax.dynamic_index_in_dim(early_half, at, 0, False) for at in (ctx_index, 1 - ctx_index)
    ]
    early_rows = early_own.astype(f32) + lax.ppermute(
        early_other, "ctx", [(0, 1), (1, 0)]
    ).astype(f32)
    expert_in_grad = jnp.concatenate(in_sums, axis=1).astype(f32)
    expert_down_grad = jnp.concatenate(down_sums, axis=1).astype(f32)
    rows_out, input_grad, expert_in_grad, expert_down_grad, early_rows = (
        lax.optimization_barrier(
            (rows_out, input_grad, expert_in_grad, expert_down_grad, early_rows)
        )
    )
    my_rows = ((lax.axis_index("dp") * n_ctx + ctx_index) * n_exp + exp_index) * rows_dev
    qkv_grad, attn_gain_grad, bias_rows = finish(
        exp_arg,
        rows_out,
        lax.dynamic_slice_in_dim(qkv_weight, my_rows, rows_dev, 0),
        lax.dynamic_slice_in_dim(attn_gain, my_rows, rows_dev, 0).reshape(rows_dev, 1),
        heads,
        lanes,
        n_ctx,
    )
    router_grad = sum(
        early_rows[:, width + i * experts : width + (i + 1) * experts] for i in range(3)
    )
    return (
        layer_output,
        input_grad,
        attn_gain_grad.reshape(rows_dev),
        qkv_grad,
        early_rows[:, :width],
        bias_rows[: bias_table.shape[0] // copies],
        early_rows[:, width + 3 * experts],
        router_grad,
        expert_in_grad[None],
        expert_down_grad,
    )


def solution(mesh):
    rows = P(("dp", "ctx", "expert"), None)
    return jax.shard_map(
        shards,
        mesh=mesh,
        in_specs=(
            rows,
            P(),
            P(),
            P(),
            P(None, "expert"),
            P(),
            P(),
            P("expert", None, None),
            P("expert", None, None),
            rows,
            rows,
            P("dp", None),
            P(),
            rows,
        ),
        out_specs=(
            rows,
            rows,
            P(("dp", "ctx", "expert")),
            rows,
            rows,
            P(("dp", "ctx"), "expert"),
            P(("dp", "ctx", "expert")),
            rows,
            P("expert", ("dp", "ctx"), None),
            P("expert", None, ("dp", "ctx")),
        ),
        check_vma=False,
    )
```

```python
import functools

import jax
import jax.numpy as jnp
from jax import lax
from jax.experimental import pallas as pl
from jax.experimental.pallas import tpu as pltpu
from jax.sharding import PartitionSpec as P


HEAD_DIM = 64
TOP = 2
LOG2E = 1.4426950408889634
SCALE = 0.125 * LOG2E
HIDE = -(2.0**100)
f32 = jnp.float32
bf16 = jnp.bfloat16
highest = lax.Precision.HIGHEST
NN = (((1,), (0,)), ((), ()))
NT = (((1,), (1,)), ((), ()))
TN = (((0,), (0,)), ((), ()))


def mm(left, right, dims):
    return lax.dot_general(left, right, dims, preferred_element_type=f32)


def stack_refs(refs):
    return jnp.concatenate([ref[...] for ref in refs], axis=0)


def cost(flops, bytes_accessed, transcendentals=0):
    return pl.CostEstimate(
        flops=int(flops), bytes_accessed=int(bytes_accessed), transcendentals=int(transcendentals)
    )


def fill_table(tab_ref, buck_ref, tb_ref, width, mul):
    buck = buck_ref[...]
    row = jnp.zeros(buck.shape, f32)
    for b in range(tab_ref.shape[0]):
        row = jnp.where(buck == b, tab_ref[b] * mul, row)
    for m in range(16):
        rolled = pltpu.roll(row, 8 * m, 1, stride=1, stride_axis=0)
        for c in range(width // 128 - 1):
            lo = width - 128 - 128 * c
            tb_ref[16 * c + m] = rolled[:, lo : lo + 128]


def bias_tile(tb_ref, start, rows, cols):
    parts = [
        tb_ref[pl.ds(start - 16 * c, rows // 8)].reshape(rows, 128) for c in range(cols // 128)
    ]
    return jnp.concatenate(parts, axis=1)


def attention_fwd_kernel(
    bk, order, nch_ref, tab_ref, buck_ref, kmask_ref, qmask_ref, q_ref, k_ref, v_ref,
    o_ref, lse_ref, kaug, vaug, tb,
):
    qi = pl.program_id(0)
    blocks, _, _, tok = k_ref.shape
    length = blocks * tok

    @pl.when(qi == 0)
    def _():
        fill_table(tab_ref, buck_ref, tb, 2 * length, LOG2E)
        first = lax.broadcasted_iota(jnp.int32, (16, length), 0) == 0
        vaug[HEAD_DIM:, :] = first.astype(f32).astype(bf16)
        for p in range(blocks):
            rows = slice(p * tok, (p + 1) * tok)
            kaug[rows, :] = jnp.concatenate([k_ref[order(p), 0], kmask_ref[:, rows]], axis=0).T
            vaug[0:HEAD_DIM, rows] = v_ref[order(p), 0]

    qaug = jnp.concatenate([q_ref[0, 0], qmask_ref[...]], axis=0)
    base = (length - 128) // 8 - qi * (tok // 8)

    def step(j, carry):
        peak, acc = carry
        ks = pl.ds(pl.multiple_of(j * bk, bk), bk)
        scores = mm(kaug[ks, :], qaug, NN) * SCALE + bias_tile(tb, base + j * (bk // 8), bk, tok)
        now = jnp.maximum(peak, jnp.max(scores, axis=0, keepdims=True))
        weights = jnp.exp2(scores - now).astype(bf16)
        return now, acc * jnp.exp2(peak - now) + mm(vaug[:, ks], weights, NN)

    start = (jnp.full((1, tok), -1e37, f32), jnp.zeros((HEAD_DIM + 16, tok), f32))
    peak, acc = lax.fori_loop(0, nch_ref[qi], step, start)
    total = acc[HEAD_DIM : HEAD_DIM + 1]
    o_ref[0] = (acc[0:HEAD_DIM] / total).astype(bf16)
    lse_ref[0] = peak + jnp.log2(total)


def attention_fwd(order, chunks, table, buck, kmask, qmask, qkv, bk):
    blocks, _, dim, tok = qkv.shape
    length = blocks * tok
    return pl.pallas_call(
        functools.partial(attention_fwd_kernel, bk, order),
        grid_spec=pltpu.PrefetchScalarGridSpec(
            num_scalar_prefetch=2,
            grid=(blocks,),
            in_specs=[
                pl.BlockSpec((8, 2 * length), lambda i, *_: (0, 0)),
                pl.BlockSpec((64, length), lambda i, *_: (0, 0)),
                pl.BlockSpec((64, tok), lambda i, *_: (0, i)),
                pl.BlockSpec((1, 1, dim, tok), lambda i, *_: (order(i), 0, 0, 0)),
                pl.BlockSpec((blocks, 1, dim, tok), lambda i, *_: (0, 1, 0, 0)),
                pl.BlockSpec((blocks, 1, dim, tok), lambda i, *_: (0, 2, 0, 0)),
            ],
            out_specs=[
                pl.BlockSpec((1, dim, tok), lambda i, *_: (order(i), 0, 0)),
                pl.BlockSpec((1, 1, tok), lambda i, *_: (i, 0, 0)),
            ],
            scratch_shapes=[
                pltpu.VMEM((length, 128), bf16),
                pltpu.VMEM((dim + 16, length), bf16),
                pltpu.VMEM((2 * length // 8 - 16, 8, 128), f32),
            ],
        ),
        out_shape=[
            jax.ShapeDtypeStruct((blocks, dim, tok), bf16),
            jax.ShapeDtypeStruct((blocks, 1, tok), f32),
        ],
        compiler_params=pltpu.CompilerParams(vmem_limit_bytes=60 << 20),
        cost_estimate=cost(2000 * length * length // 2, 4 * length * 2 * dim, length * length // 2),
        name="attention_fwd",
    )(chunks, table, buck, kmask, qmask, qkv, qkv, qkv)


def three_rows(values, rows):
    high = values.astype(bf16).astype(f32)
    mid = (values - high).astype(bf16).astype(f32)
    row = lax.broadcasted_iota(jnp.int32, (rows, values.shape[1]), 0)
    out = jnp.where(row == 0, high, jnp.where(row == 1, mid, jnp.where(row == 2, values - high - mid, 0.0)))
    return out.astype(bf16)


def attention_bwd_kernel(
    bk, order, nch_ref, tab_ref, buck_ref, kmask_ref, qmask_ref, q_ref, k_ref, v_ref, o_ref,
    do_ref, lse_ref, out_ref, off_ref, knat, kaug, vaug, tb, gb, dkacc, dvacc,
):
    qi = pl.program_id(0)
    blocks, _, _, tok = k_ref.shape
    length = blocks * tok

    @pl.when(qi == 0)
    def _():
        fill_table(tab_ref, buck_ref, tb, 2 * length, LOG2E)
        gb[...] = jnp.zeros_like(gb)
        dkacc[...] = jnp.zeros_like(dkacc)
        dvacc[...] = jnp.zeros_like(dvacc)
        three = lax.broadcasted_iota(jnp.int32, (64, length), 0) < 3
        vaug[64:128, :] = three.astype(f32).astype(bf16)
        kaug[64:128, :] = kmask_ref[...]
        for p in range(blocks):
            rows = slice(p * tok, (p + 1) * tok)
            knat[rows, :] = k_ref[order(p), 0].T
            kaug[0:64, rows] = k_ref[order(p), 0]
            vaug[0:64, rows] = v_ref[order(p), 0]

    q_t = q_ref[0, 0]
    do_t = do_ref[0]
    delta = jnp.sum(do_t.astype(f32) * o_ref[0].astype(f32), axis=0, keepdims=True)
    lse = lse_ref[0] * (1.0 / SCALE)
    blank = jnp.zeros((32, tok), bf16)
    qaug = jnp.concatenate([q_t, qmask_ref[...], three_rows(-lse, 16), blank], axis=0).T
    doaug = jnp.concatenate([do_t, three_rows(-delta, 32), blank], axis=0).T
    base = (length - 128) // 8 + qi * (tok // 8)

    half = tok // 2

    def step(j, dq):
        ks = pl.ds(pl.multiple_of(j * bk, bk), bk)
        parts = []
        for i in range(2):
            rows = slice(i * half, (i + 1) * half)
            start = base + i * (half // 8) - j * (bk // 8)
            scores = mm(qaug[rows], kaug[:, ks], NN) * SCALE + bias_tile(tb, start, half, bk)
            probs = jnp.exp2(scores)
            ds = probs * mm(doaug[rows], vaug[:, ks], NN)
            for c in range(bk // 128):
                at = pl.ds(start - 16 * c, half // 8)
                gb[at] += ds[:, 128 * c : 128 * c + 128].reshape(half // 8, 8, 128)
            low = ds.astype(bf16)
            dvacc[:, ks] += mm(do_t[:, rows], probs.astype(bf16), NN)
            dkacc[:, ks] += mm(q_t[:, rows], low, NN)
            parts.append(mm(low, knat[ks, :], NN))
        return dq + jnp.concatenate(parts, axis=0)

    dq = lax.fori_loop(0, nch_ref[qi], step, jnp.zeros((tok, 64), f32))
    out_ref[order(qi), 0] = (dq * 0.125).T.astype(bf16)

    @pl.when(qi == blocks - 1)
    def _():
        for p in range(blocks):
            rows = slice(p * tok, (p + 1) * tok)
            out_ref[order(p), 1] = (dkacc[:, rows] * 0.125).astype(bf16)
            out_ref[order(p), 2] = dvacc[:, rows].astype(bf16)
        width = 2 * length
        total = jnp.zeros((8, width), f32)
        for m in range(16):
            tiles = [gb[16 * c + m] for c in range(width // 128 - 2, -1, -1)]
            skewed = jnp.concatenate([jnp.zeros((8, 128), f32)] + tiles, axis=1)
            total = total + (pltpu.roll(skewed, width - 8 * m, 1) if m else skewed)
        row = total[0:1]
        for s in range(1, 8):
            row = row + pltpu.roll(total[s : s + 1], width - s, 1)
        buck = buck_ref[0:1, :]
        for b in range(off_ref.shape[0]):
            mine = jnp.where(buck == b, row, 0.0)
            parts = [mine[:, 128 * c : 128 * c + 128] for c in range(width // 128)]
            while len(parts) > 1:
                parts = [x + y for x, y in zip(parts[::2], parts[1::2])]
            off_ref[b : b + 1, :] = parts[0]


def attention_bwd(order, chunks, table, buck, kmask, qmask, qkv, mixed, mixed_grad, lse, bk):
    blocks, _, dim, tok = qkv.shape
    length = blocks * tok
    one = pl.BlockSpec((1, dim, tok), lambda i, *_: (order(i), 0, 0))
    return pl.pallas_call(
        functools.partial(attention_bwd_kernel, bk, order),
        grid_spec=pltpu.PrefetchScalarGridSpec(
            num_scalar_prefetch=2,
            grid=(blocks,),
            in_specs=[
                pl.BlockSpec((8, 2 * length), lambda i, *_: (0, 0)),
                pl.BlockSpec((64, length), lambda i, *_: (0, 0)),
                pl.BlockSpec((16, tok), lambda i, *_: (0, i)),
                pl.BlockSpec((1, 1, dim, tok), lambda i, *_: (order(i), 0, 0, 0)),
                pl.BlockSpec((blocks, 1, dim, tok), lambda i, *_: (0, 1, 0, 0)),
                pl.BlockSpec((blocks, 1, dim, tok), lambda i, *_: (0, 2, 0, 0)),
                one,
                one,
                pl.BlockSpec((1, 1, tok), lambda i, *_: (i, 0, 0)),
            ],
            out_specs=[
                pl.BlockSpec((blocks, 3, dim, tok), lambda i, *_: (0, 0, 0, 0)),
                pl.BlockSpec((table.shape[0], 128), lambda i, *_: (0, 0)),
            ],
            scratch_shapes=[
                pltpu.VMEM((length, dim), bf16),
                pltpu.VMEM((128, length), bf16),
                pltpu.VMEM((128, length), bf16),
                pltpu.VMEM((2 * length // 8 - 16, 8, 128), f32),
                pltpu.VMEM((2 * length // 8 - 16, 8, 128), f32),
                pltpu.VMEM((dim, length), f32),
                pltpu.VMEM((dim, length), f32),
            ],
        ),
        out_shape=[
            jax.ShapeDtypeStruct((blocks, 3, dim, tok), bf16),
            jax.ShapeDtypeStruct((table.shape[0], 128), f32),
        ],
        compiler_params=pltpu.CompilerParams(vmem_limit_bytes=60 << 20),
        cost_estimate=cost(5000 * length * length // 2, 8 * length * 2 * dim, length * length // 2),
        name="attention_bwd",
    )(chunks, table, buck, kmask, qmask, qkv, qkv, qkv, mixed, mixed_grad, lse)


def write_groups(acc, refs):
    rows = refs[0].shape[0]
    for d, ref in enumerate(refs):
        ref[...] = acc[d * rows : (d + 1) * rows, :].astype(bf16)


def join_rows(refs, scratch):
    at = 0
    for ref in refs:
        scratch[at : at + ref.shape[0], :] = ref[:, : scratch.shape[1]]
        at += ref.shape[0]


def gate_column(refs):
    return jnp.concatenate(
        [jnp.sum(ref[...].astype(f32), axis=1, keepdims=True) for ref in refs], axis=0
    )


def expert_fwd_kernel(steps, groups, wg_ref, wu_ref, wd_ref, *refs):
    xs, refs = refs[:groups], refs[groups:]
    ht_ref, act_ref, slope_ref, *outs, rows, acc = refs
    f = pl.program_id(0)

    @pl.when(f == 0)
    def _():
        join_rows(xs, rows)
        acc[...] = jnp.zeros_like(acc)

    x = rows[...]
    gate = mm(x, wg_ref[0], NN)
    up = mm(x, wu_ref[0], NN)
    square = gate * gate
    t = jnp.tanh(gate * (0.7978845608028654 + 0.035677408136300125 * square))
    half = 0.5 + 0.5 * t
    act = gate * half
    slope = half + (gate * (0.5 - 0.5 * t * t)) * (
        0.7978845608028654 + 0.10703222440890037 * square
    )
    hidden = (act * up).astype(bf16)
    ht_ref[...] = hidden.T
    act_ref[...] = act.astype(bf16)
    slope_ref[...] = (slope * up).astype(bf16)
    acc[...] += mm(hidden, wd_ref[0], NN)

    @pl.when(f == steps - 1)
    def _():
        write_groups(acc, outs)


def expert_fwd(xs, w_in, w_down, tile=256):
    groups = len(xs)
    ff, width = w_down.shape[1:]
    rows = groups * xs[0].shape[0]
    steps = ff // tile
    part = pl.BlockSpec((rows, tile), lambda f: (0, f))
    inner = jax.ShapeDtypeStruct((rows, ff), bf16)
    one = pl.BlockSpec((rows // groups, width), lambda f: (0, 0))
    return pl.pallas_call(
        functools.partial(expert_fwd_kernel, steps, groups),
        grid=(steps,),
        in_specs=[
            pl.BlockSpec((1, width, tile), lambda f: (0, 0, f)),
            pl.BlockSpec((1, width, tile), lambda f: (0, 0, f + steps)),
            pl.BlockSpec((1, tile, width), lambda f: (0, f, 0)),
        ]
        + [pl.BlockSpec(xs[0].shape, lambda f: (0, 0))] * groups,
        out_specs=[pl.BlockSpec((tile, rows), lambda f: (f, 0)), part, part] + [one] * groups,
        out_shape=[jax.ShapeDtypeStruct((ff, rows), bf16), inner, inner]
        + [jax.ShapeDtypeStruct((rows // groups, width), bf16)] * groups,
        scratch_shapes=[pltpu.VMEM((rows, width), bf16), pltpu.VMEM((rows, width), f32)],
        compiler_params=pltpu.CompilerParams(vmem_limit_bytes=60 << 20),
        cost_estimate=cost(
            10 * rows * width * ff, 6 * width * ff + rows * (4 * width + 6 * ff), rows * ff
        ),
        name="expert_fwd",
    )(w_in, w_in, w_down, *xs)


def expert_bwd_kernel(steps, groups, act_ref, slope_ref, wg_ref, wu_ref, wd_ref, *refs):
    gs, gates, refs = refs[:groups], refs[groups : 2 * groups], refs[2 * groups :]
    grads_ref, *outs, pg, acc = refs
    f = pl.program_id(0)

    @pl.when(f == 0)
    def _():
        join_rows(gs, pg)
        pg[...] = (pg[...].astype(f32) * gate_column(gates)).astype(bf16)
        acc[...] = jnp.zeros_like(acc)

    hidden_grad = mm(pg[...], wd_ref[0], NT)
    dg = (slope_ref[...].astype(f32) * hidden_grad).astype(bf16)
    du = (act_ref[...].astype(f32) * hidden_grad).astype(bf16)
    grads_ref[0] = dg
    grads_ref[1] = du
    acc[...] += mm(dg, wg_ref[0], NT) + mm(du, wu_ref[0], NT)

    @pl.when(f == steps - 1)
    def _():
        write_groups(acc, outs)


def gate_block(x, width):
    return pl.BlockSpec((x.shape[0], 128), lambda f, *_: (0, width // 128))


def expert_bwd(gs, xs, act, slope, w_in, w_down, tile=256):
    groups = len(gs)
    rows, width = groups * gs[0].shape[0], gs[0].shape[1]
    ff = w_down.shape[1]
    steps = ff // tile
    part = pl.BlockSpec((rows, tile), lambda f: (0, f))
    one = pl.BlockSpec((rows // groups, width), lambda f: (0, 0))
    return pl.pallas_call(
        functools.partial(expert_bwd_kernel, steps, groups),
        grid=(steps,),
        in_specs=[
            part,
            part,
            pl.BlockSpec((1, width, tile), lambda f: (0, 0, f)),
            pl.BlockSpec((1, width, tile), lambda f: (0, 0, f + steps)),
            pl.BlockSpec((1, tile, width), lambda f: (0, f, 0)),
        ]
        + [one] * groups
        + [gate_block(x, width) for x in xs],
        out_specs=[pl.BlockSpec((2, rows, tile), lambda f: (0, 0, f))] + [one] * groups,
        out_shape=[jax.ShapeDtypeStruct((2, rows, ff), bf16)]
        + [jax.ShapeDtypeStruct((rows // groups, width), bf16)] * groups,
        scratch_shapes=[pltpu.VMEM((rows, width), bf16), pltpu.VMEM((rows, width), f32)],
        compiler_params=pltpu.CompilerParams(vmem_limit_bytes=60 << 20),
        cost_estimate=cost(
            10 * rows * width * ff, 6 * width * ff + rows * (4 * width + 8 * ff)
        ),
        name="expert_bwd",
    )(act, slope, w_in, w_in, w_down, *gs, *xs)


def column_block(ref, blk, ctx, flip, a):
    low = ref[:, 2 * a * blk : (2 * a + 1) * blk]
    high = ref[:, (2 * a + 1) * blk : (2 * a + 2) * blk]
    return jnp.where(lax.rem(ctx + flip, 2) == 0, low, high)


def turn_kernel(copies, ctx_ref, *refs):
    xs, xt_ref = refs[:-1], refs[-1]
    blk = xt_ref.shape[0] // copies
    at = 0
    for x_ref in xs:
        rows = x_ref.shape[0]
        for flip in range(2):
            for a in range(copies // 2):
                to = (flip * (copies // 2) + a) * blk
                block = column_block(x_ref, blk, ctx_ref[0], flip, a)
                xt_ref[to : to + blk, at : at + rows] = block.T
        at += rows


def turn(ctx, xs, copies):
    width = xs[0].shape[1] - 128
    total = sum(x.shape[0] for x in xs)
    return pl.pallas_call(
        functools.partial(turn_kernel, copies),
        in_specs=[pl.BlockSpec(memory_space=pltpu.SMEM)]
        + [pl.BlockSpec(memory_space=pltpu.VMEM)] * len(xs),
        out_specs=pl.BlockSpec(memory_space=pltpu.VMEM),
        out_shape=jax.ShapeDtypeStruct((width, total), bf16),
        compiler_params=pltpu.CompilerParams(vmem_limit_bytes=60 << 20),
        cost_estimate=cost(2 * total * width, 4 * total * width),
        name="turn",
    )(ctx, *xs)


def in_grad_kernel(*refs):
    x_refs, (*gs, own_ref, other_ref) = refs[:4], refs[4:]
    grads = jnp.concatenate([g[0] for g in gs], axis=0)
    half = own_ref.shape[0]
    grad = mm(stack_refs(x_refs), grads, NN).astype(bf16)
    own_ref[...] = grad[:half]
    other_ref[...] = grad[half:]


def in_grad(xt, grads, first, count, tile=256):
    width, total = xt.shape
    steps = grads[0].shape[2] // tile
    half = jax.ShapeDtypeStruct((width // 2, count * tile), bf16)
    out = pl.BlockSpec((width // 2, tile), lambda f: (0, f))

    def at(f):
        return ((f + first) // steps, 0, (f + first) % steps)

    return pl.pallas_call(
        in_grad_kernel,
        grid=(count,),
        in_specs=[pl.BlockSpec((width // 4, total), lambda f, i=i: (i, 0)) for i in range(4)]
        + [pl.BlockSpec((1, g.shape[1], tile), at) for g in grads],
        out_specs=[out, out],
        out_shape=[half, half],
        compiler_params=pltpu.CompilerParams(vmem_limit_bytes=60 << 20),
        cost_estimate=cost(
            4 * total * width * count * tile, 2 * (total + width) * count * tile + 2 * total * width
        ),
        name="in_grad",
    )(*[xt] * 4, *grads)


def down_grad_kernel(copies, n, ctx_ref, *refs):
    ps, gates, (*hs, own_ref, other_ref, pg) = refs[:n], refs[n : 2 * n], refs[2 * n :]
    blk = ps[0].shape[1] // copies

    @pl.when(pl.program_id(0) == 0)
    def _():
        at = 0
        for p_ref, gate_ref in zip(ps, gates):
            rows = p_ref.shape[0]
            gate = gate_column([gate_ref])
            for flip in range(2):
                for a in range(copies // 2):
                    to = (flip * (copies // 2) + a) * blk
                    block = column_block(p_ref, blk, ctx_ref[0], flip, a).astype(f32)
                    pg[at : at + rows, to : to + blk] = (block * gate).astype(bf16)
            at += rows

    grad = mm(jnp.concatenate([h[...] for h in hs], axis=1), pg[...], NN).astype(bf16)
    for a in range(copies // 2):
        own_ref[a] = grad[:, a * blk : (a + 1) * blk]
        to = (copies // 2 + a) * blk
        other_ref[a] = grad[:, to : to + blk]


def down_grad(ctx, hs, ps, xs, copies, first, count, tile=256):
    ff = count * tile
    width = ps[0].shape[1]
    total = sum(h.shape[1] for h in hs)
    blk = width // copies
    half = jax.ShapeDtypeStruct((copies // 2, ff, blk), bf16)
    out = pl.BlockSpec((copies // 2, tile, blk), lambda f, c: (0, f, 0))
    return pl.pallas_call(
        functools.partial(down_grad_kernel, copies, len(ps)),
        grid_spec=pltpu.PrefetchScalarGridSpec(
            num_scalar_prefetch=1,
            grid=(count,),
            in_specs=[pl.BlockSpec(p.shape, lambda f, c: (0, 0)) for p in ps]
            + [gate_block(x, width) for x in xs]
            + [pl.BlockSpec((tile, h.shape[1]), lambda f, c: (f + first, 0)) for h in hs],
            out_specs=[out, out],
            scratch_shapes=[pltpu.VMEM((total, width), bf16)],
        ),
        out_shape=[half, half],
        compiler_params=pltpu.CompilerParams(vmem_limit_bytes=60 << 20),
        cost_estimate=cost(4 * total * width * ff, 2 * (total * (width + ff) + width * ff)),
        name="down_grad",
    )(ctx, *ps, *xs, *hs)


def project_kernel(x_ref, gain_ref, *refs):
    w_refs, (normed_t, *outs) = refs[:4], refs[4:]
    heads = len(outs)

    @pl.when((pl.program_id(0) == 0) & (pl.program_id(1) == 0))
    def _():
        x = x_ref[...].astype(f32)
        scale = lax.rsqrt(jnp.mean(x * x, axis=1, keepdims=True) + 1e-06)
        normed = (x * scale * gain_ref[...]).astype(bf16)
        normed_t[...] = normed.T

    cols = w_refs[0].shape[1]
    tok = normed_t.shape[1]
    rows = mm(stack_refs(w_refs), normed_t[...], TN).astype(bf16)
    rows = rows.reshape(cols // (heads * HEAD_DIM), heads, HEAD_DIM, tok)
    for h in range(heads):
        outs[h][:, 0] = rows[:, h]


def project(x, gain, weight, groups, heads, cols=512):
    tok, width = x.shape
    per = cols // (heads * HEAD_DIM)
    blocks = width // cols
    return pl.pallas_call(
        project_kernel,
        grid=(3, blocks),
        in_specs=[
            pl.BlockSpec((tok, width), lambda p, j: (0, 0)),
            pl.BlockSpec((1, width), lambda p, j: (0, 0)),
        ]
        + [
            pl.BlockSpec((width // 4, cols), lambda p, j, i=i: (i, p * blocks + j))
            for i in range(4)
        ],
        out_specs=[pl.BlockSpec((width, tok), lambda p, j: (0, 0))]
        + [pl.BlockSpec((per, 1, HEAD_DIM, tok), lambda p, j: (j, p, 0, 0))] * heads,
        out_shape=[jax.ShapeDtypeStruct((width, tok), bf16)]
        + [jax.ShapeDtypeStruct((groups, 3, HEAD_DIM, tok), bf16)] * heads,
        compiler_params=pltpu.CompilerParams(vmem_limit_bytes=60 << 20),
        cost_estimate=cost(6 * tok * width * width, 6 * width * width + 10 * tok * width),
        name="project",
    )(x, gain.reshape(1, width), *[weight] * 4)


def input_grad_kernel(steps, x_ref, gain_ref, mid_ref, *refs):
    w_refs, (*grads, out_ref, acc) = refs[:4], refs[4:]
    step = pl.program_id(0)
    cols = w_refs[0].shape[1]
    tok = out_ref.shape[0]

    @pl.when(step == 0)
    def _():
        acc[...] = jnp.zeros_like(acc)

    rows = jnp.stack([g[:, 0] for g in grads], axis=1).reshape(cols, tok)
    acc[...] += mm(stack_refs(w_refs), rows, NN)

    @pl.when(step == steps - 1)
    def _():
        x = x_ref[...].astype(f32)
        scale = lax.rsqrt(jnp.mean(x * x, axis=1, keepdims=True) + 1e-06)
        dy = acc[...].T * gain_ref[...]
        pull = jnp.mean(x * dy, axis=1, keepdims=True)
        out_ref[...] = mid_ref[...] + scale * dy - x * (scale * scale * scale * pull)


def input_gradient(x, gain, middle_grad, weight, grads, cols=512):
    tok, width = x.shape
    heads = len(grads)
    per = cols // (heads * HEAD_DIM)
    blocks = width // cols
    whole = pl.BlockSpec((tok, width), lambda s: (0, 0))
    return pl.pallas_call(
        functools.partial(input_grad_kernel, 3 * blocks),
        grid=(3 * blocks,),
        in_specs=[
            whole,
            pl.BlockSpec((1, width), lambda s: (0, 0)),
            whole,
        ]
        + [pl.BlockSpec((width // 4, cols), lambda s, i=i: (i, s)) for i in range(4)]
        + [
            pl.BlockSpec((per, 1, HEAD_DIM, tok), lambda s: (s % blocks, s // blocks, 0, 0))
            for _ in grads
        ],
        out_specs=whole,
        out_shape=jax.ShapeDtypeStruct((tok, width), f32),
        scratch_shapes=[pltpu.VMEM((width, tok), f32)],
        compiler_params=pltpu.CompilerParams(vmem_limit_bytes=60 << 20),
        cost_estimate=cost(6 * tok * width * width, 6 * width * width + 16 * tok * width),
        name="input_grad",
    )(x, gain.reshape(1, width), middle_grad, *[weight] * 4, *grads)


def wide_thirds(values):
    high = values.astype(bf16)
    rest = values - high.astype(f32)
    mid = rest.astype(bf16)
    low = (rest - mid.astype(f32)).astype(bf16)
    rows, lanes = values.shape
    blank = jnp.zeros((rows, 128 - 3 * lanes), bf16)
    return jnp.concatenate([high, mid, low, blank], axis=1)


def combine_kernel(
    counts, exp_ref, place_ref, ids_ref, probs_ref, middle_ref, cot_ref, normed_ref, gain_ref,
    router_ref, weight_ref, *refs,
):
    blocks, heads, parts, copies = counts
    experts = probs_ref.shape[1]
    backs, refs = refs[:blocks], refs[blocks:]
    row_grads, refs = refs[:blocks], refs[blocks:]
    mixed, refs = refs[:heads], refs[heads:]
    out_ref, mid_ref, refs = refs[0], refs[1], refs[2:]
    mixed_grads, refs = refs[:heads], refs[heads:]
    early, (slot_rows, slot_grads, wide) = refs[:parts], refs[parts:]
    tok, width = middle_ref.shape
    total = slot_rows.shape[0]

    at = 0
    for back, row_grad in zip(backs, row_grads):
        rows = slice(at, at + back.shape[0])
        slot_rows[rows, :] = back[...]
        slot_grads[rows, :] = row_grad[...]
        at += back.shape[0]

    slot = lax.broadcasted_iota(jnp.int32, (tok, total), 1)
    one = (slot == place_ref[:, 0:1]).astype(f32).astype(bf16)
    two = (slot == place_ref[:, 1:2]).astype(f32).astype(bf16)
    first = mm(one, slot_rows[...], NN)
    second = mm(two, slot_rows[...], NN)
    dy = mm(one + two, slot_grads[...], NN)

    lane = lax.broadcasted_iota(jnp.int32, (tok, experts), 1)
    is_first, is_second = lane == ids_ref[:, 0:1], lane == ids_ref[:, 1:2]
    probs = probs_ref[...]
    gate_first = jnp.sum(jnp.where(is_first, probs, 0.0), axis=1, keepdims=True)
    gate_second = jnp.sum(jnp.where(is_second, probs, 0.0), axis=1, keepdims=True)
    middle = middle_ref[...]
    cot = cot_ref[...].astype(f32)
    out_ref[...] = (middle + gate_first * first + gate_second * second).astype(bf16)
    grad_first = jnp.sum(cot * first, axis=1, keepdims=True)
    grad_second = jnp.sum(cot * second, axis=1, keepdims=True)
    probs_grad = jnp.where(is_first, grad_first, 0.0) + jnp.where(is_second, grad_second, 0.0)
    logits_grad = probs * (probs_grad - jnp.sum(probs * probs_grad, axis=1, keepdims=True))
    for e in range(experts):
        dy = dy + logits_grad[:, e : e + 1] * router_ref[e : e + 1, :]

    scale = lax.rsqrt(jnp.mean(middle * middle, axis=1, keepdims=True) + 1e-06)
    unit = middle * scale
    gain_terms = unit * dy
    dy = dy * gain_ref[...]
    middle_grad = cot + scale * (dy - unit * jnp.mean(unit * dy, axis=1, keepdims=True))
    mid_ref[...] = middle_grad
    branch = middle_grad.astype(bf16)

    groups, dim, _ = mixed_grads[0].shape
    back = mm(weight_ref[...], branch, NT).astype(bf16).reshape(groups, heads, dim, tok)
    for h in range(heads):
        mixed_grads[h][...] = back[:, h]
    for h in range(heads):
        grad = mm(mixed[h][...], branch, NN)
        for g in range(groups):
            at = (g * heads + h) * dim
            wide[at : at + dim, 0:width] = grad[g * dim : (g + 1) * dim]
    mark = lax.broadcasted_iota(jnp.int32, (tok, 128), 1) == 3 * experts
    mark = mark.astype(f32).astype(bf16)
    high = gain_terms.astype(bf16)
    low = (gain_terms - high.astype(f32)).astype(bf16)
    wide[:, width:] = (
        mm(normed_ref[...], wide_thirds(logits_grad), TN) + mm(high, mark, TN) + mm(low, mark, TN)
    )
    per = wide.shape[0] // (parts * copies)
    for d in range(parts):
        e = jnp.bitwise_xor(exp_ref[0], d)
        rows = [
            wide[pl.ds(pl.multiple_of((k * parts + e) * per, per), per), :] for k in range(copies)
        ]
        early[d][...] = jnp.concatenate(rows, axis=0).astype(bf16)


def combine(
    exp, place, ids, probs, middle, cot, normed, gain, router, weight, backs, row_grads, mixed,
    copies,
):
    tok, width = middle.shape
    heads = len(mixed)
    parts = probs.shape[1]
    groups = width // (heads * HEAD_DIM)
    total = sum(b.shape[0] for b in backs)
    sds = jax.ShapeDtypeStruct
    return pl.pallas_call(
        functools.partial(combine_kernel, (len(backs), heads, parts, copies)),
        in_specs=[pl.BlockSpec(memory_space=pltpu.SMEM)]
        + [pl.BlockSpec(memory_space=pltpu.VMEM)] * (9 + 2 * len(backs) + heads),
        out_specs=[pl.BlockSpec(memory_space=pltpu.VMEM)] * (2 + heads + parts),
        out_shape=[sds((tok, width), bf16), sds((tok, width), f32)]
        + [sds((groups, HEAD_DIM, tok), bf16)] * heads
        + [sds((width // parts, width + 128), bf16)] * parts,
        scratch_shapes=[
            pltpu.VMEM((total, width), bf16),
            pltpu.VMEM((total, width), bf16),
            pltpu.VMEM((width, width + 128), f32),
        ],
        compiler_params=pltpu.CompilerParams(vmem_limit_bytes=60 << 20),
        cost_estimate=cost(
            6 * tok * total * width + 4 * tok * width * width,
            4 * total * width + 18 * tok * width + 4 * width * width,
        ),
        name="combine",
    )(exp, place, ids, probs, middle, cot, normed, gain.reshape(1, width), router, weight,
      *backs, *row_grads, *mixed)


def finish_kernel(heads, lanes, n_ctx, exp_ref, rows_ref, weight_ref, gain_ref, grad_ref, gain_grad_ref, bias_ref):
    groups = rows_ref.shape[0]
    width = weight_ref.shape[1] // 3
    for part in range(3):
        pieces = []
        for g in range(groups):
            for h in range(heads):
                lo = h * lanes + part * HEAD_DIM
                pieces.append(rows_ref[g][:, lo : lo + HEAD_DIM].astype(f32))
        grad_ref[:, part * width : (part + 1) * width] = jnp.concatenate(pieces, axis=1)
    terms = weight_ref[...].astype(f32) * grad_ref[...]
    gain_grad_ref[...] = jnp.sum(terms, axis=1, keepdims=True) / gain_ref[...]
    columns = []
    for c in range(n_ctx):
        mine = rows_ref[exp_ref[0] * n_ctx + c].astype(f32)
        for h in range(heads):
            lo = h * lanes + 3 * HEAD_DIM
            columns.append(mine[:, lo : lo + 1])
    bias_ref[...] = jnp.concatenate(columns, axis=1)


def finish(exp, rows, weight_rows, gain_rows, heads, lanes, n_ctx):
    count, columns = weight_rows.shape
    sds = jax.ShapeDtypeStruct
    vmem = pl.BlockSpec(memory_space=pltpu.VMEM)
    return pl.pallas_call(
        functools.partial(finish_kernel, heads, lanes, n_ctx),
        in_specs=[pl.BlockSpec(memory_space=pltpu.SMEM), vmem, vmem, vmem],
        out_specs=[vmem, vmem, vmem],
        out_shape=[
            sds((count, columns), f32), sds((count, 1), f32), sds((count, heads * n_ctx), f32)
        ],
        cost_estimate=cost(4 * count * columns, 8 * count * columns),
        name="finish",
    )(exp, rows, weight_rows, gain_rows)


def route_kernel(heads, x_ref, place_ref, ids_ref, gain_ref, router_ref, weight_ref, *refs):
    mixed, (middle_ref, normed_ref, probs_ref, *slots, joined) = refs[:heads], refs[heads:]
    tok, width = x_ref.shape
    experts = probs_ref.shape[1]
    for h in range(heads):
        for g in range(width // (heads * HEAD_DIM)):
            at = (g * heads + h) * HEAD_DIM
            joined[at : at + HEAD_DIM, :] = mixed[h][g * HEAD_DIM : (g + 1) * HEAD_DIM, :]
    middle = x_ref[...].astype(f32) + mm(joined[...], weight_ref[...], TN)
    middle_ref[...] = middle
    scale = lax.rsqrt(jnp.mean(middle * middle, axis=1, keepdims=True) + 1e-06)
    normed = (middle * scale * gain_ref[...]).astype(bf16)
    normed_ref[...] = normed
    logits = mm(normed, router_ref[...], NN)[:, :experts]
    weights = jnp.exp(logits - jnp.max(logits, axis=1, keepdims=True))
    probs = weights / jnp.sum(weights, axis=1, keepdims=True)
    probs_ref[...] = probs
    lane = lax.broadcasted_iota(jnp.int32, (tok, experts), 1)
    gates = [
        wide_thirds(jnp.sum(jnp.where(lane == ids_ref[:, j : j + 1], probs, 0.0), axis=1, keepdims=True))
        for j in range(2)
    ]
    at = 0
    for slot_ref in slots:
        rows = slot_ref.shape[0]
        slot = lax.broadcasted_iota(jnp.int32, (rows, tok), 0) + at
        one = (slot == place_ref[0:1, :]).astype(f32).astype(bf16)
        two = (slot == place_ref[1:2, :]).astype(f32).astype(bf16)
        slot_ref[:, 0:width] = mm(one + two, normed, NN).astype(bf16)
        slot_ref[:, width:] = (mm(one, gates[0], NN) + mm(two, gates[1], NN)).astype(bf16)
        at += rows


def route(x, place, ids, gain, router, weight, mixed, sizes):
    tok, width = x.shape
    experts = router.shape[1]
    heads = len(mixed)
    sds = jax.ShapeDtypeStruct
    vmem = pl.BlockSpec(memory_space=pltpu.VMEM)
    return pl.pallas_call(
        functools.partial(route_kernel, heads),
        in_specs=[vmem] * (6 + heads),
        out_specs=[vmem] * (3 + len(sizes)),
        out_shape=[sds((tok, width), f32), sds((tok, width), bf16), sds((tok, experts), f32)]
        + [sds((size, width + 128), bf16) for size in sizes],
        scratch_shapes=[pltpu.VMEM((width, tok), bf16)],
        compiler_params=pltpu.CompilerParams(vmem_limit_bytes=60 << 20),
        cost_estimate=cost(
            2 * tok * width * (width + sum(sizes)), 12 * tok * width + 2 * width * width
        ),
        name="route",
    )(x, place.T, ids, gain.reshape(1, width), jnp.pad(router, ((0, 0), (0, 128 - experts))),
      weight, *mixed)


def sequence_grad_kernel(n_exp, copies, dp_ref, out_ref, offsets_ref, *refs):
    normed_refs, (*shares, acc) = refs[:4], refs[4:]
    step = pl.program_id(0)
    width, lanes = acc.shape
    own = 3 * HEAD_DIM

    @pl.when(step == 0)
    def _():
        acc[...] = jnp.zeros_like(acc)

    normed = jnp.concatenate([ref[0] for ref in normed_refs], axis=0)
    acc[:, 0:own] += mm(normed, out_ref[0].reshape(own, out_ref.shape[3]), NT)

    @pl.when(step == pl.num_programs(0) - 1)
    def _():
        count = offsets_ref.shape[0]
        buckets, rows_dev = count // copies, width // (copies * n_exp)
        row = lax.broadcasted_iota(jnp.int32, (width, count), 0)
        bucket = lax.broadcasted_iota(jnp.int32, (width, count), 1)
        place = row // (n_exp * rows_dev) * buckets + row % rows_dev
        here = ((place == bucket) & (row % rows_dev < buckets)).astype(f32).astype(bf16)
        table = jnp.sum(offsets_ref[...], axis=1, keepdims=True)
        column = jnp.sum(mm(here, wide_thirds(table), NN), axis=1, keepdims=True)
        base = own // 128 * 128
        lane = lax.broadcasted_iota(jnp.int32, (width, 128), 1) + base
        acc[:, base : base + 128] += jnp.where(lane == own, column, 0.0)
        per = shares[0].shape[0]
        for d, share in enumerate(shares):
            start = pl.multiple_of(jnp.bitwise_xor(dp_ref[0], d) * per, per)
            share[...] = acc[pl.ds(start, per), :].astype(bf16)


def sequence_grad(dp, normed, out, offsets, n_dp, n_exp, copies, lanes):
    groups, _, dim, tok = out.shape
    width = normed.shape[1]
    return pl.pallas_call(
        functools.partial(sequence_grad_kernel, n_exp, copies),
        grid_spec=pltpu.PrefetchScalarGridSpec(
            num_scalar_prefetch=1,
            grid=(groups,),
            in_specs=[
                pl.BlockSpec((1, 3, dim, tok), lambda g, d: (g, 0, 0, 0)),
                pl.BlockSpec(offsets.shape, lambda g, d: (0, 0)),
            ]
            + [
                pl.BlockSpec((1, width // 4, tok), lambda g, d, i=i: (g, i, 0)) for i in range(4)
            ],
            out_specs=[pl.BlockSpec((width // n_dp, lanes), lambda g, d: (0, 0))] * n_dp,
            scratch_shapes=[pltpu.VMEM((width, lanes), f32)],
        ),
        out_shape=[jax.ShapeDtypeStruct((width // n_dp, lanes), bf16)] * n_dp,
        compiler_params=pltpu.CompilerParams(vmem_limit_bytes=60 << 20),
        cost_estimate=cost(
            6 * dim * groups * tok * width, 2 * groups * tok * (width + 3 * dim)
        ),
        name="sequence_grad",
    )(dp, out, offsets, *[normed] * 4)


def dot_f32(left, right, left_dim, right_dim):
    return mm(left, right, (((left_dim,), (right_dim,)), ((), ())))


def swap_blocks(blocks, axes):
    return lax.all_to_all(blocks, axes, split_axis=0, concat_axis=0, tiled=True)


def exchange(parts, axis="expert"):
    n = len(parts)
    return [parts[0]] + [
        lax.ppermute(parts[d], axis, [(i, i ^ d) for i in range(n)]) for d in range(1, n)
    ]


def add_low(parts):
    return sum(part.astype(f32) for part in parts).astype(bf16)


def after(value, *others):
    return lax.optimization_barrier((value, others))[0]


def attention_plan(block_row, bucket_ids, blocks, tok):
    length = blocks * tok
    pad = jnp.full((1,), -1, jnp.int32)
    buck_rev = jnp.broadcast_to(jnp.concatenate([pad, bucket_ids[::-1]])[None], (8, 2 * length))
    buck = jnp.broadcast_to(jnp.concatenate([pad, bucket_ids])[None], (8, 2 * length))
    ids = jnp.arange(16)
    hot = (block_row[None, :] == ids[:, None]).astype(bf16)
    hide = jnp.where(ids[:, None] > block_row[None, :], HIDE, 0.0).astype(bf16)
    kmask_t = jnp.concatenate(
        [hot, jnp.ones((3, length), bf16), jnp.zeros((45, length), bf16)], axis=0
    )
    qmask = jnp.concatenate([hide, jnp.zeros((48, length), bf16)], axis=0)
    last = block_row.reshape(blocks, tok)[:, -1]
    seen = jnp.sum((block_row[None, :] <= last[:, None]).astype(jnp.int32), axis=1)
    return buck_rev, buck, kmask_t, qmask, hide, seen


def shards(
    layer_input,
    attn_gain,
    qkv_weight,
    out_weight,
    bias_table,
    moe_gain,
    router_weight,
    expert_in,
    expert_down,
    expert_ids,
    fill_order,
    block_ids,
    bucket_ids,
    cotangent,
):
    tok, width = layer_input.shape
    n_dp, n_ctx, n_exp = lax.axis_size("dp"), lax.axis_size("ctx"), lax.axis_size("expert")
    groups = n_ctx * n_exp
    copies = n_dp * n_ctx
    head_exp = bias_table.shape[1]
    heads = head_exp // n_ctx
    experts = router_weight.shape[1]
    ff_width = expert_down.shape[1]
    capacity = 5 * TOP * tok // (4 * experts)
    cut = (capacity // 2 + 15) // 16 * 16
    spans = ((0, cut), (cut, capacity))
    ctx_index = lax.axis_index("ctx")
    exp_index = lax.axis_index("expert")
    ctx_arg = ctx_index.astype(jnp.int32).reshape(1)
    pair = ("expert", "ctx")
    step_k = 1024

    def order(p):
        return (p % n_exp) * n_ctx + p // n_exp

    def in_swap_order(blocks):
        shape = blocks.shape
        return jnp.swapaxes(blocks.reshape((n_ctx, n_exp) + shape[1:]), 0, 1).reshape(shape)

    exp_arg = exp_index.astype(jnp.int32).reshape(1)
    normed_t, *parts = project(layer_input, attn_gain, qkv_weight, groups, heads)
    qkv = [swap_blocks(part, pair) for part in parts]
    table_dev = lax.dynamic_slice_in_dim(bias_table, ctx_index * heads, heads, 1)
    buck_rev, buck, kmask, qmask, hide, seen = attention_plan(
        block_ids[0], bucket_ids, groups, tok
    )
    chunks = (seen + step_k - 1) // step_k

    flat_ids = expert_ids.reshape(TOP * tok)
    fill_rank = fill_order.reshape(TOP * tok)
    same_expert = flat_ids[:, None] == flat_ids[None, :]
    earlier = fill_rank[None, :] < fill_rank[:, None]
    slot_of = jnp.sum((same_expert & earlier).astype(jnp.int32), axis=1)
    slots = slot_of.reshape(tok, TOP)
    part_at = jnp.where(slots < cut, 0, experts * cut - cut)
    stride = jnp.where(slots < cut, cut, capacity - cut)
    place = jnp.where(
        slots < capacity,
        part_at + jnp.bitwise_xor(expert_ids, exp_index) * stride + slots,
        -1,
    )
    sizes = [high - low for low, high in spans for _ in range(experts)]

    def to_slots(rows):
        parts, at = [], 0
        for size in sizes:
            slot = jnp.arange(at, at + size)[:, None]
            hot = (slot == place[None, :, 0]) | (slot == place[None, :, 1])
            parts.append(dot_f32(hot.astype(bf16), rows, 1, 0).astype(bf16))
            at += size
        return parts

    forward, mixed = [], []
    cot_slots = to_slots(cotangent)
    slots_a, slots_b = cot_slots[:experts], cot_slots[experts:]
    rows_dev = width // (n_dp * groups)
    my_rows = ((lax.axis_index("dp") * n_ctx + ctx_index) * n_exp + exp_index) * rows_dev
    weight_rows = lax.dynamic_slice_in_dim(qkv_weight, my_rows, rows_dev, 0)
    gain_rows = lax.dynamic_slice_in_dim(attn_gain, my_rows, rows_dev, 0).reshape(rows_dev, 1)
    qkv[0], place, slots_a, slots_b, buck_rev, buck, kmask, qmask, hide, weight_rows, gain_rows = (
        lax.optimization_barrier(
            (
                qkv[0], place, slots_a, slots_b, buck_rev, buck, kmask, qmask, hide, weight_rows,
                gain_rows,
            )
        )
    )
    normed_seq = lax.all_gather(after(normed_t, qkv[0]), pair)
    for h in range(heads):
        arg = after(qkv[h], forward)
        if h == heads - 1:
            grad_a = exchange(after(slots_a, arg))
        out = attention_fwd(
            order, chunks, table_dev[:, h], buck_rev, kmask, qmask, arg, step_k
        )
        out = after(out, qkv[h + 1] if h < heads - 1 else grad_a, mixed)
        forward.append(out)
        mixed.append(swap_blocks(out[0], pair).reshape(groups * HEAD_DIM, tok))
    mixed = after(mixed, forward)
    middle, normed_moe, probs, *sent = route(
        layer_input, place, expert_ids, moe_gain, router_weight, out_weight, mixed, sizes
    )
    x_a, x_b = exchange(sent[:experts]), exchange(sent[experts:])

    grad_b = exchange(after(slots_b, x_a))
    run_a = after(expert_fwd(x_a, expert_in, expert_down), x_b, grad_b)
    produced_a = exchange(list(run_a[3:]))
    run_b = expert_fwd(after(x_b, run_a), expert_in, expert_down)
    run_b = after(run_b, produced_a, normed_seq)
    produced_b = exchange(list(run_b[3:]))
    hidden = [run_a[0], run_b[0]]
    tiles = ff_width // 256
    cuts = (0, (tiles + 1) // 2, tiles)
    g_args = after(grad_a + grad_b, run_b)
    down_1 = down_grad(ctx_arg, hidden, g_args, x_a + x_b, copies, 0, cuts[1])

    def sum_dp(half):
        return lax.psum_scatter(half, "dp", scatter_dimension=0, tiled=True)

    def to_ctx(half):
        return lax.ppermute(half, "ctx", [(0, 1), (1, 0)])

    came = to_ctx(down_1[1])
    g_args = after(grad_a + grad_b, down_1)
    down_2 = down_grad(ctx_arg, hidden, g_args, x_a + x_b, copies, cuts[1], tiles - cuts[1])
    undo_a = expert_bwd(
        after(grad_a, down_2), x_a, run_a[1], run_a[2], expert_in, expert_down
    )
    undo_a, came = lax.optimization_barrier((after(undo_a, produced_b), came))
    halves = [add_low((down_1[0], came))]
    grads_a = exchange(list(undo_a[1:]))
    came = to_ctx(after(down_2[1], undo_a))
    undo_b = expert_bwd(
        after(grad_b, undo_a), x_b, run_b[1], run_b[2], expert_in, expert_down
    )
    undo_b, came = lax.optimization_barrier((after(undo_b, grads_a), came))
    halves.append(add_low((down_2[0], came)))
    grads_b = exchange(list(undo_b[1:]))
    grads_in = [undo_a[0], undo_b[0]]
    total = 2 * tiles
    size_a, size_d = total * 3 // 22, total * 8 // 22
    xt = turn(ctx_arg, x_a + x_b, copies)
    part_a = in_grad(after(xt, undo_b), grads_in, 0, size_a)
    came_a = to_ctx(after(part_a[1], halves[1]))
    part_b = in_grad(after(xt, part_a), grads_in, size_a, size_a)
    part_d = in_grad(after(xt, part_b), grads_in, 2 * size_a, size_d)

    part_d, grads_b, came_a = lax.optimization_barrier((part_d, grads_b, came_a))
    came_b = to_ctx(after(part_b[1], came_a))
    layer_output, middle_grad, *outs = combine(
        exp_arg, place, expert_ids, probs, middle, cotangent, normed_moe, moe_gain,
        router_weight.T.astype(f32), out_weight, produced_a + produced_b, grads_a + grads_b, mixed,
        copies,
    )
    down_sums = [sum_dp(half) for half in halves]
    outs, came_b, down_sums[0] = lax.optimization_barrier((outs, came_b, down_sums[0]))
    half_a = jnp.concatenate(
        [add_low((part_a[0], came_a)), add_low((part_b[0], came_b))], axis=1
    )
    first = 2 * size_a + size_d
    part_c = in_grad(after(xt, outs), grads_in, first, total - first)
    early = outs[heads:]
    mixed_grad = [swap_blocks(part, pair) for part in outs[:heads]]

    last_own, last_other = [sum_dp(half) for half in part_d]
    sum_a = sum_dp(half_a)

    lanes = -(-(3 * HEAD_DIM + 1) // 128) * 128
    dp_arg = lax.axis_index("dp").astype(jnp.int32).reshape(1)
    backward, grads = [], []
    for h in range(heads):
        arg = after(mixed_grad[h], backward if h else (part_c, half_a))
        beside = [grads[h - 1]] if h else []
        if h == 0:
            came_c = to_ctx(after(part_c[1], arg))
            early_parts = exchange(after(early, arg))
            beside += [came_c, early_parts, last_own, last_other, down_sums[1]] + mixed_grad[1:2]
        else:
            arg = after(arg, half_c)
        if h == heads - 1:
            last_came = to_ctx(after(last_other, arg))
            beside += [last_came, sum_a]
        out = attention_bwd(
            order, chunks, table_dev[:, h], buck, kmask, hide, qkv[h], forward[h][0],
            arg, forward[h][1], step_k,
        )
        out, beside = lax.optimization_barrier((out, beside))
        if h == 0:
            half_c = add_low((part_c[0], beside[0]))
            sum_c = sum_dp(half_c)
            early_half = sum_dp(add_low(beside[1]))
        backward.append(out)
        grads.append(swap_blocks(out[0], pair))
    late = []
    for out, offsets in reversed(backward):
        shares = sequence_grad(
            dp_arg, normed_seq, after(out, backward), offsets, n_dp, n_exp, copies, lanes
        )
        late.insert(0, exchange(shares, "dp"))
    in_sums = [sum_a, add_low((last_own, after(last_came, backward))), sum_c]
    input_grad = input_gradient(layer_input, attn_gain, middle_grad, qkv_weight, grads)
    late, input_grad = lax.optimization_barrier((late, input_grad))
    late = jnp.concatenate([add_low(parts) for parts in late], axis=1)
    rows_out = swap_blocks(in_swap_order(late.reshape(groups, rows_dev, -1)), pair)
    early_half = early_half.reshape(n_ctx, rows_dev, width + 128)
    early_own, early_other = [
        lax.dynamic_index_in_dim(early_half, at, 0, False) for at in (ctx_index, 1 - ctx_index)
    ]
    early_rows = early_own.astype(f32) + lax.ppermute(
        early_other, "ctx", [(0, 1), (1, 0)]
    ).astype(f32)
    expert_in_grad = jnp.concatenate(in_sums, axis=1).astype(f32)
    expert_down_grad = jnp.concatenate(after(down_sums, backward), axis=1).astype(f32)
    rows_out, input_grad, expert_in_grad, expert_down_grad, early_rows = (
        lax.optimization_barrier(
            (rows_out, input_grad, expert_in_grad, expert_down_grad, early_rows)
        )
    )
    qkv_grad, attn_gain_grad, bias_rows = finish(
        exp_arg,
        rows_out,
        weight_rows,
        gain_rows,
        heads,
        lanes,
        n_ctx,
    )
    router_grad = sum(
        early_rows[:, width + i * experts : width + (i + 1) * experts] for i in range(3)
    )
    return (
        layer_output,
        input_grad,
        attn_gain_grad.reshape(rows_dev),
        qkv_grad,
        early_rows[:, :width],
        bias_rows[: bias_table.shape[0] // copies],
        early_rows[:, width + 3 * experts],
        router_grad,
        expert_in_grad[None],
        expert_down_grad,
    )


def solution(mesh):
    rows = P(("dp", "ctx", "expert"), None)
    return jax.shard_map(
        shards,
        mesh=mesh,
        in_specs=(
            rows,
            P(),
            P(),
            P(),
            P(None, "expert"),
            P(),
            P(),
            P("expert", None, None),
            P("expert", None, None),
            rows,
            rows,
            P("dp", None),
            P(),
            rows,
        ),
        out_specs=(
            rows,
            rows,
            P(("dp", "ctx", "expert")),
            rows,
            rows,
            P(("dp", "ctx"), "expert"),
            P(("dp", "ctx", "expert")),
            rows,
            P("expert", ("dp", "ctx"), None),
            P("expert", None, ("dp", "ctx")),
        ),
        check_vma=False,
    )
```

```python
import functools

import jax
import jax.numpy as jnp
from jax import lax
from jax.experimental import pallas as pl
from jax.experimental.pallas import tpu as pltpu
from jax.sharding import PartitionSpec as P


HEAD_DIM = 64
TOP = 2
LOG2E = 1.4426950408889634
SCALE = 0.125 * LOG2E
HIDE = -(2.0**100)
f32 = jnp.float32
bf16 = jnp.bfloat16
highest = lax.Precision.HIGHEST
NN = (((1,), (0,)), ((), ()))
NT = (((1,), (1,)), ((), ()))
TN = (((0,), (0,)), ((), ()))


def mm(left, right, dims):
    return lax.dot_general(left, right, dims, preferred_element_type=f32)


def stack_refs(refs):
    return jnp.concatenate([ref[...] for ref in refs], axis=0)


def cost(flops, bytes_accessed, transcendentals=0):
    return pl.CostEstimate(
        flops=int(flops), bytes_accessed=int(bytes_accessed), transcendentals=int(transcendentals)
    )


def fill_table(tab_ref, buck_ref, tb_ref, width, mul):
    buck = buck_ref[...]
    row = jnp.zeros(buck.shape, f32)
    for b in range(tab_ref.shape[0]):
        row = jnp.where(buck == b, tab_ref[b] * mul, row)
    for m in range(16):
        rolled = pltpu.roll(row, 8 * m, 1, stride=1, stride_axis=0)
        for c in range(width // 128 - 1):
            lo = width - 128 - 128 * c
            tb_ref[16 * c + m] = rolled[:, lo : lo + 128]


def bias_tile(tb_ref, start, rows, cols):
    parts = [
        tb_ref[pl.ds(start - 16 * c, rows // 8)].reshape(rows, 128) for c in range(cols // 128)
    ]
    return jnp.concatenate(parts, axis=1)


def attention_fwd_kernel(
    bk, order, nch_ref, tab_ref, buck_ref, kmask_ref, qmask_ref, q_ref, k_ref, v_ref,
    o_ref, lse_ref, kaug, vaug, tb,
):
    qi = pl.program_id(0)
    blocks, _, _, tok = k_ref.shape
    length = blocks * tok

    @pl.when(qi == 0)
    def _():
        fill_table(tab_ref, buck_ref, tb, 2 * length, LOG2E)
        first = lax.broadcasted_iota(jnp.int32, (16, length), 0) == 0
        vaug[HEAD_DIM:, :] = first.astype(f32).astype(bf16)
        for p in range(blocks):
            rows = slice(p * tok, (p + 1) * tok)
            kaug[rows, :] = jnp.concatenate([k_ref[order(p), 0], kmask_ref[:, rows]], axis=0).T
            vaug[0:HEAD_DIM, rows] = v_ref[order(p), 0]

    qaug = jnp.concatenate([q_ref[0, 0], qmask_ref[...]], axis=0)
    base = (length - 128) // 8 - qi * (tok // 8)

    def step(j, carry):
        peak, acc = carry
        ks = pl.ds(pl.multiple_of(j * bk, bk), bk)
        scores = mm(kaug[ks, :], qaug, NN) * SCALE + bias_tile(tb, base + j * (bk // 8), bk, tok)
        now = jnp.maximum(peak, jnp.max(scores, axis=0, keepdims=True))
        weights = jnp.exp2(scores - now).astype(bf16)
        return now, acc * jnp.exp2(peak - now) + mm(vaug[:, ks], weights, NN)

    start = (jnp.full((1, tok), -1e37, f32), jnp.zeros((HEAD_DIM + 16, tok), f32))
    peak, acc = lax.fori_loop(0, nch_ref[qi], step, start)
    total = acc[HEAD_DIM : HEAD_DIM + 1]
    o_ref[0] = (acc[0:HEAD_DIM] / total).astype(bf16)
    lse_ref[0] = peak + jnp.log2(total)


def attention_fwd(order, chunks, table, buck, kmask, qmask, qkv, bk):
    blocks, _, dim, tok = qkv.shape
    length = blocks * tok
    return pl.pallas_call(
        functools.partial(attention_fwd_kernel, bk, order),
        grid_spec=pltpu.PrefetchScalarGridSpec(
            num_scalar_prefetch=2,
            grid=(blocks,),
            in_specs=[
                pl.BlockSpec((8, 2 * length), lambda i, *_: (0, 0)),
                pl.BlockSpec((64, length), lambda i, *_: (0, 0)),
                pl.BlockSpec((64, tok), lambda i, *_: (0, i)),
                pl.BlockSpec((1, 1, dim, tok), lambda i, *_: (order(i), 0, 0, 0)),
                pl.BlockSpec((blocks, 1, dim, tok), lambda i, *_: (0, 1, 0, 0)),
                pl.BlockSpec((blocks, 1, dim, tok), lambda i, *_: (0, 2, 0, 0)),
            ],
            out_specs=[
                pl.BlockSpec((1, dim, tok), lambda i, *_: (order(i), 0, 0)),
                pl.BlockSpec((1, 1, tok), lambda i, *_: (i, 0, 0)),
            ],
            scratch_shapes=[
                pltpu.VMEM((length, 128), bf16),
                pltpu.VMEM((dim + 16, length), bf16),
                pltpu.VMEM((2 * length // 8 - 16, 8, 128), f32),
            ],
        ),
        out_shape=[
            jax.ShapeDtypeStruct((blocks, dim, tok), bf16),
            jax.ShapeDtypeStruct((blocks, 1, tok), f32),
        ],
        compiler_params=pltpu.CompilerParams(vmem_limit_bytes=60 << 20),
        cost_estimate=cost(2000 * length * length // 2, 4 * length * 2 * dim, length * length // 2),
        name="attention_fwd",
    )(chunks, table, buck, kmask, qmask, qkv, qkv, qkv)


def three_rows(values, rows):
    high = values.astype(bf16).astype(f32)
    mid = (values - high).astype(bf16).astype(f32)
    row = lax.broadcasted_iota(jnp.int32, (rows, values.shape[1]), 0)
    out = jnp.where(row == 0, high, jnp.where(row == 1, mid, jnp.where(row == 2, values - high - mid, 0.0)))
    return out.astype(bf16)


def attention_bwd_kernel(
    bk, order, nch_ref, tab_ref, buck_ref, kmask_ref, qmask_ref, q_ref, k_ref, v_ref, o_ref,
    do_ref, lse_ref, out_ref, off_ref, knat, kaug, vaug, tb, gb, dkacc, dvacc,
):
    qi = pl.program_id(0)
    blocks, _, _, tok = k_ref.shape
    length = blocks * tok

    @pl.when(qi == 0)
    def _():
        fill_table(tab_ref, buck_ref, tb, 2 * length, LOG2E)
        gb[...] = jnp.zeros_like(gb)
        dkacc[...] = jnp.zeros_like(dkacc)
        dvacc[...] = jnp.zeros_like(dvacc)
        three = lax.broadcasted_iota(jnp.int32, (64, length), 0) < 3
        vaug[64:128, :] = three.astype(f32).astype(bf16)
        kaug[64:128, :] = kmask_ref[...]
        for p in range(blocks):
            rows = slice(p * tok, (p + 1) * tok)
            knat[rows, :] = k_ref[order(p), 0].T
            kaug[0:64, rows] = k_ref[order(p), 0]
            vaug[0:64, rows] = v_ref[order(p), 0]

    q_t = q_ref[0, 0]
    do_t = do_ref[0]
    delta = jnp.sum(do_t.astype(f32) * o_ref[0].astype(f32), axis=0, keepdims=True)
    lse = lse_ref[0] * (1.0 / SCALE)
    blank = jnp.zeros((32, tok), bf16)
    qaug = jnp.concatenate([q_t, qmask_ref[...], three_rows(-lse, 16), blank], axis=0).T
    doaug = jnp.concatenate([do_t, three_rows(-delta, 32), blank], axis=0).T
    base = (length - 128) // 8 + qi * (tok // 8)

    half = tok // 2

    def step(j, dq):
        ks = pl.ds(pl.multiple_of(j * bk, bk), bk)
        parts = []
        for i in range(2):
            rows = slice(i * half, (i + 1) * half)
            start = base + i * (half // 8) - j * (bk // 8)
            scores = mm(qaug[rows], kaug[:, ks], NN) * SCALE + bias_tile(tb, start, half, bk)
            probs = jnp.exp2(scores)
            ds = probs * mm(doaug[rows], vaug[:, ks], NN)
            for c in range(bk // 128):
                at = pl.ds(start - 16 * c, half // 8)
                gb[at] += ds[:, 128 * c : 128 * c + 128].reshape(half // 8, 8, 128)
            low = ds.astype(bf16)
            dvacc[:, ks] += mm(do_t[:, rows], probs.astype(bf16), NN)
            dkacc[:, ks] += mm(q_t[:, rows], low, NN)
            parts.append(mm(low, knat[ks, :], NN))
        return dq + jnp.concatenate(parts, axis=0)

    dq = lax.fori_loop(0, nch_ref[qi], step, jnp.zeros((tok, 64), f32))
    out_ref[order(qi), 0] = (dq * 0.125).T.astype(bf16)

    @pl.when(qi == blocks - 1)
    def _():
        for p in range(blocks):
            rows = slice(p * tok, (p + 1) * tok)
            out_ref[order(p), 1] = (dkacc[:, rows] * 0.125).astype(bf16)
            out_ref[order(p), 2] = dvacc[:, rows].astype(bf16)
        width = 2 * length
        total = jnp.zeros((8, width), f32)
        for m in range(16):
            tiles = [gb[16 * c + m] for c in range(width // 128 - 2, -1, -1)]
            skewed = jnp.concatenate([jnp.zeros((8, 128), f32)] + tiles, axis=1)
            total = total + (pltpu.roll(skewed, width - 8 * m, 1) if m else skewed)
        row = total[0:1]
        for s in range(1, 8):
            row = row + pltpu.roll(total[s : s + 1], width - s, 1)
        buck = buck_ref[0:1, :]
        for b in range(off_ref.shape[0]):
            mine = jnp.where(buck == b, row, 0.0)
            parts = [mine[:, 128 * c : 128 * c + 128] for c in range(width // 128)]
            while len(parts) > 1:
                parts = [x + y for x, y in zip(parts[::2], parts[1::2])]
            off_ref[b : b + 1, :] = parts[0]


def attention_bwd(order, chunks, table, buck, kmask, qmask, qkv, mixed, mixed_grad, lse, bk):
    blocks, _, dim, tok = qkv.shape
    length = blocks * tok
    one = pl.BlockSpec((1, dim, tok), lambda i, *_: (order(i), 0, 0))
    return pl.pallas_call(
        functools.partial(attention_bwd_kernel, bk, order),
        grid_spec=pltpu.PrefetchScalarGridSpec(
            num_scalar_prefetch=2,
            grid=(blocks,),
            in_specs=[
                pl.BlockSpec((8, 2 * length), lambda i, *_: (0, 0)),
                pl.BlockSpec((64, length), lambda i, *_: (0, 0)),
                pl.BlockSpec((16, tok), lambda i, *_: (0, i)),
                pl.BlockSpec((1, 1, dim, tok), lambda i, *_: (order(i), 0, 0, 0)),
                pl.BlockSpec((blocks, 1, dim, tok), lambda i, *_: (0, 1, 0, 0)),
                pl.BlockSpec((blocks, 1, dim, tok), lambda i, *_: (0, 2, 0, 0)),
                one,
                one,
                pl.BlockSpec((1, 1, tok), lambda i, *_: (i, 0, 0)),
            ],
            out_specs=[
                pl.BlockSpec((blocks, 3, dim, tok), lambda i, *_: (0, 0, 0, 0)),
                pl.BlockSpec((table.shape[0], 128), lambda i, *_: (0, 0)),
            ],
            scratch_shapes=[
                pltpu.VMEM((length, dim), bf16),
                pltpu.VMEM((128, length), bf16),
                pltpu.VMEM((128, length), bf16),
                pltpu.VMEM((2 * length // 8 - 16, 8, 128), f32),
                pltpu.VMEM((2 * length // 8 - 16, 8, 128), f32),
                pltpu.VMEM((dim, length), f32),
                pltpu.VMEM((dim, length), f32),
            ],
        ),
        out_shape=[
            jax.ShapeDtypeStruct((blocks, 3, dim, tok), bf16),
            jax.ShapeDtypeStruct((table.shape[0], 128), f32),
        ],
        compiler_params=pltpu.CompilerParams(vmem_limit_bytes=60 << 20),
        cost_estimate=cost(5000 * length * length // 2, 8 * length * 2 * dim, length * length // 2),
        name="attention_bwd",
    )(chunks, table, buck, kmask, qmask, qkv, qkv, qkv, mixed, mixed_grad, lse)


def write_groups(acc, refs):
    rows = refs[0].shape[0]
    for d, ref in enumerate(refs):
        ref[...] = acc[d * rows : (d + 1) * rows, :].astype(bf16)


def join_rows(refs, scratch):
    at = 0
    for ref in refs:
        scratch[at : at + ref.shape[0], :] = ref[:, : scratch.shape[1]]
        at += ref.shape[0]


def gate_column(refs):
    return jnp.concatenate(
        [jnp.sum(ref[...].astype(f32), axis=1, keepdims=True) for ref in refs], axis=0
    )


def expert_fwd_kernel(steps, groups, wg_ref, wu_ref, wd_ref, *refs):
    xs, refs = refs[:groups], refs[groups:]
    ht_ref, act_ref, slope_ref, *outs, rows, acc = refs
    f = pl.program_id(0)

    @pl.when(f == 0)
    def _():
        join_rows(xs, rows)
        acc[...] = jnp.zeros_like(acc)

    x = rows[...]
    gate = mm(x, wg_ref[0], NN)
    up = mm(x, wu_ref[0], NN)
    square = gate * gate
    t = jnp.tanh(gate * (0.7978845608028654 + 0.035677408136300125 * square))
    half = 0.5 + 0.5 * t
    act = gate * half
    slope = half + (gate * (0.5 - 0.5 * t * t)) * (
        0.7978845608028654 + 0.10703222440890037 * square
    )
    hidden = (act * up).astype(bf16)
    ht_ref[...] = hidden.T
    act_ref[...] = act.astype(bf16)
    slope_ref[...] = (slope * up).astype(bf16)
    acc[...] += mm(hidden, wd_ref[0], NN)

    @pl.when(f == steps - 1)
    def _():
        write_groups(acc, outs)


def expert_fwd(xs, w_in, w_down, tile=256):
    groups = len(xs)
    ff, width = w_down.shape[1:]
    rows = groups * xs[0].shape[0]
    steps = ff // tile
    part = pl.BlockSpec((rows, tile), lambda f: (0, f))
    inner = jax.ShapeDtypeStruct((rows, ff), bf16)
    one = pl.BlockSpec((rows // groups, width), lambda f: (0, 0))
    return pl.pallas_call(
        functools.partial(expert_fwd_kernel, steps, groups),
        grid=(steps,),
        in_specs=[
            pl.BlockSpec((1, width, tile), lambda f: (0, 0, f)),
            pl.BlockSpec((1, width, tile), lambda f: (0, 0, f + steps)),
            pl.BlockSpec((1, tile, width), lambda f: (0, f, 0)),
        ]
        + [pl.BlockSpec(xs[0].shape, lambda f: (0, 0))] * groups,
        out_specs=[pl.BlockSpec((tile, rows), lambda f: (f, 0)), part, part] + [one] * groups,
        out_shape=[jax.ShapeDtypeStruct((ff, rows), bf16), inner, inner]
        + [jax.ShapeDtypeStruct((rows // groups, width), bf16)] * groups,
        scratch_shapes=[pltpu.VMEM((rows, width), bf16), pltpu.VMEM((rows, width), f32)],
        compiler_params=pltpu.CompilerParams(vmem_limit_bytes=60 << 20),
        cost_estimate=cost(
            10 * rows * width * ff, 6 * width * ff + rows * (4 * width + 6 * ff), rows * ff
        ),
        name="expert_fwd",
    )(w_in, w_in, w_down, *xs)


def expert_bwd_kernel(steps, groups, act_ref, slope_ref, wg_ref, wu_ref, wd_ref, *refs):
    gs, gates, refs = refs[:groups], refs[groups : 2 * groups], refs[2 * groups :]
    grads_ref, *outs, pg, acc = refs
    f = pl.program_id(0)

    @pl.when(f == 0)
    def _():
        join_rows(gs, pg)
        pg[...] = (pg[...].astype(f32) * gate_column(gates)).astype(bf16)
        acc[...] = jnp.zeros_like(acc)

    hidden_grad = mm(pg[...], wd_ref[0], NT)
    dg = (slope_ref[...].astype(f32) * hidden_grad).astype(bf16)
    du = (act_ref[...].astype(f32) * hidden_grad).astype(bf16)
    grads_ref[0] = dg
    grads_ref[1] = du
    acc[...] += mm(dg, wg_ref[0], NT) + mm(du, wu_ref[0], NT)

    @pl.when(f == steps - 1)
    def _():
        write_groups(acc, outs)


def gate_block(x, width):
    return pl.BlockSpec((x.shape[0], 128), lambda f, *_: (0, width // 128))


def expert_bwd(gs, xs, act, slope, w_in, w_down, tile=256):
    groups = len(gs)
    rows, width = groups * gs[0].shape[0], gs[0].shape[1]
    ff = w_down.shape[1]
    steps = ff // tile
    part = pl.BlockSpec((rows, tile), lambda f: (0, f))
    one = pl.BlockSpec((rows // groups, width), lambda f: (0, 0))
    return pl.pallas_call(
        functools.partial(expert_bwd_kernel, steps, groups),
        grid=(steps,),
        in_specs=[
            part,
            part,
            pl.BlockSpec((1, width, tile), lambda f: (0, 0, f)),
            pl.BlockSpec((1, width, tile), lambda f: (0, 0, f + steps)),
            pl.BlockSpec((1, tile, width), lambda f: (0, f, 0)),
        ]
        + [one] * groups
        + [gate_block(x, width) for x in xs],
        out_specs=[pl.BlockSpec((2, rows, tile), lambda f: (0, 0, f))] + [one] * groups,
        out_shape=[jax.ShapeDtypeStruct((2, rows, ff), bf16)]
        + [jax.ShapeDtypeStruct((rows // groups, width), bf16)] * groups,
        scratch_shapes=[pltpu.VMEM((rows, width), bf16), pltpu.VMEM((rows, width), f32)],
        compiler_params=pltpu.CompilerParams(vmem_limit_bytes=60 << 20),
        cost_estimate=cost(
            10 * rows * width * ff, 6 * width * ff + rows * (4 * width + 8 * ff)
        ),
        name="expert_bwd",
    )(act, slope, w_in, w_in, w_down, *gs, *xs)


def column_block(ref, blk, ctx, flip, a):
    low = ref[:, 2 * a * blk : (2 * a + 1) * blk]
    high = ref[:, (2 * a + 1) * blk : (2 * a + 2) * blk]
    return jnp.where(lax.rem(ctx + flip, 2) == 0, low, high)


def turn_kernel(copies, ctx_ref, *refs):
    xs, xt_ref = refs[:-1], refs[-1]
    blk = xt_ref.shape[0] // copies
    at = 0
    for x_ref in xs:
        rows = x_ref.shape[0]
        for flip in range(2):
            for a in range(copies // 2):
                to = (flip * (copies // 2) + a) * blk
                block = column_block(x_ref, blk, ctx_ref[0], flip, a)
                xt_ref[to : to + blk, at : at + rows] = block.T
        at += rows


def turn(ctx, xs, copies):
    width = xs[0].shape[1] - 128
    total = sum(x.shape[0] for x in xs)
    return pl.pallas_call(
        functools.partial(turn_kernel, copies),
        in_specs=[pl.BlockSpec(memory_space=pltpu.SMEM)]
        + [pl.BlockSpec(memory_space=pltpu.VMEM)] * len(xs),
        out_specs=pl.BlockSpec(memory_space=pltpu.VMEM),
        out_shape=jax.ShapeDtypeStruct((width, total), bf16),
        compiler_params=pltpu.CompilerParams(vmem_limit_bytes=60 << 20),
        cost_estimate=cost(2 * total * width, 4 * total * width),
        name="turn",
    )(ctx, *xs)


def in_grad_kernel(*refs):
    x_refs, (*gs, own_ref, other_ref) = refs[:4], refs[4:]
    grads = jnp.concatenate([g[0] for g in gs], axis=0)
    half = own_ref.shape[0]
    grad = mm(stack_refs(x_refs), grads, NN).astype(bf16)
    own_ref[...] = grad[:half]
    other_ref[...] = grad[half:]


def in_grad(xt, grads, first, count, tile=256):
    width, total = xt.shape
    steps = grads[0].shape[2] // tile
    half = jax.ShapeDtypeStruct((width // 2, count * tile), bf16)
    out = pl.BlockSpec((width // 2, tile), lambda f: (0, f))

    def at(f):
        return ((f + first) // steps, 0, (f + first) % steps)

    return pl.pallas_call(
        in_grad_kernel,
        grid=(count,),
        in_specs=[pl.BlockSpec((width // 4, total), lambda f, i=i: (i, 0)) for i in range(4)]
        + [pl.BlockSpec((1, g.shape[1], tile), at) for g in grads],
        out_specs=[out, out],
        out_shape=[half, half],
        compiler_params=pltpu.CompilerParams(vmem_limit_bytes=60 << 20),
        cost_estimate=cost(
            4 * total * width * count * tile, 2 * (total + width) * count * tile + 2 * total * width
        ),
        name="in_grad",
    )(*[xt] * 4, *grads)


def down_grad_kernel(copies, n, ctx_ref, *refs):
    ps, gates, (*hs, own_ref, other_ref, pg) = refs[:n], refs[n : 2 * n], refs[2 * n :]
    blk = ps[0].shape[1] // copies

    @pl.when(pl.program_id(0) == 0)
    def _():
        at = 0
        for p_ref, gate_ref in zip(ps, gates):
            rows = p_ref.shape[0]
            gate = gate_column([gate_ref])
            for flip in range(2):
                for a in range(copies // 2):
                    to = (flip * (copies // 2) + a) * blk
                    block = column_block(p_ref, blk, ctx_ref[0], flip, a).astype(f32)
                    pg[at : at + rows, to : to + blk] = (block * gate).astype(bf16)
            at += rows

    grad = mm(jnp.concatenate([h[...] for h in hs], axis=1), pg[...], NN).astype(bf16)
    for a in range(copies // 2):
        own_ref[a] = grad[:, a * blk : (a + 1) * blk]
        to = (copies // 2 + a) * blk
        other_ref[a] = grad[:, to : to + blk]


def down_grad(ctx, hs, ps, xs, copies, first, count, tile=256):
    ff = count * tile
    width = ps[0].shape[1]
    total = sum(h.shape[1] for h in hs)
    blk = width // copies
    half = jax.ShapeDtypeStruct((copies // 2, ff, blk), bf16)
    out = pl.BlockSpec((copies // 2, tile, blk), lambda f, c: (0, f, 0))
    return pl.pallas_call(
        functools.partial(down_grad_kernel, copies, len(ps)),
        grid_spec=pltpu.PrefetchScalarGridSpec(
            num_scalar_prefetch=1,
            grid=(count,),
            in_specs=[pl.BlockSpec(p.shape, lambda f, c: (0, 0)) for p in ps]
            + [gate_block(x, width) for x in xs]
            + [pl.BlockSpec((tile, h.shape[1]), lambda f, c: (f + first, 0)) for h in hs],
            out_specs=[out, out],
            scratch_shapes=[pltpu.VMEM((total, width), bf16)],
        ),
        out_shape=[half, half],
        compiler_params=pltpu.CompilerParams(vmem_limit_bytes=60 << 20),
        cost_estimate=cost(4 * total * width * ff, 2 * (total * (width + ff) + width * ff)),
        name="down_grad",
    )(ctx, *ps, *xs, *hs)


def project_kernel(x_ref, gain_ref, *refs):
    w_refs, (normed_t, *outs) = refs[:4], refs[4:]
    heads = len(outs)

    @pl.when((pl.program_id(0) == 0) & (pl.program_id(1) == 0))
    def _():
        x = x_ref[...].astype(f32)
        scale = lax.rsqrt(jnp.mean(x * x, axis=1, keepdims=True) + 1e-06)
        normed = (x * scale * gain_ref[...]).astype(bf16)
        normed_t[...] = normed.T

    cols = w_refs[0].shape[1]
    tok = normed_t.shape[1]
    rows = mm(stack_refs(w_refs), normed_t[...], TN).astype(bf16)
    rows = rows.reshape(cols // (heads * HEAD_DIM), heads, HEAD_DIM, tok)
    for h in range(heads):
        outs[h][:, 0] = rows[:, h]


def project(x, gain, weight, groups, heads, cols=512):
    tok, width = x.shape
    per = cols // (heads * HEAD_DIM)
    blocks = width // cols
    return pl.pallas_call(
        project_kernel,
        grid=(3, blocks),
        in_specs=[
            pl.BlockSpec((tok, width), lambda p, j: (0, 0)),
            pl.BlockSpec((1, width), lambda p, j: (0, 0)),
        ]
        + [
            pl.BlockSpec((width // 4, cols), lambda p, j, i=i: (i, p * blocks + j))
            for i in range(4)
        ],
        out_specs=[pl.BlockSpec((width, tok), lambda p, j: (0, 0))]
        + [pl.BlockSpec((per, 1, HEAD_DIM, tok), lambda p, j: (j, p, 0, 0))] * heads,
        out_shape=[jax.ShapeDtypeStruct((width, tok), bf16)]
        + [jax.ShapeDtypeStruct((groups, 3, HEAD_DIM, tok), bf16)] * heads,
        compiler_params=pltpu.CompilerParams(vmem_limit_bytes=60 << 20),
        cost_estimate=cost(6 * tok * width * width, 6 * width * width + 10 * tok * width),
        name="project",
    )(x, gain.reshape(1, width), *[weight] * 4)


def input_grad_kernel(steps, x_ref, gain_ref, mid_ref, *refs):
    w_refs, (*grads, out_ref, acc) = refs[:4], refs[4:]
    step = pl.program_id(0)
    cols = w_refs[0].shape[1]
    tok = out_ref.shape[0]

    @pl.when(step == 0)
    def _():
        acc[...] = jnp.zeros_like(acc)

    rows = jnp.stack([g[:, 0] for g in grads], axis=1).reshape(cols, tok)
    acc[...] += mm(stack_refs(w_refs), rows, NN)

    @pl.when(step == steps - 1)
    def _():
        x = x_ref[...].astype(f32)
        scale = lax.rsqrt(jnp.mean(x * x, axis=1, keepdims=True) + 1e-06)
        dy = acc[...].T * gain_ref[...]
        pull = jnp.mean(x * dy, axis=1, keepdims=True)
        out_ref[...] = mid_ref[...] + scale * dy - x * (scale * scale * scale * pull)


def input_gradient(x, gain, middle_grad, weight, grads, cols=512):
    tok, width = x.shape
    heads = len(grads)
    per = cols // (heads * HEAD_DIM)
    blocks = width // cols
    whole = pl.BlockSpec((tok, width), lambda s: (0, 0))
    return pl.pallas_call(
        functools.partial(input_grad_kernel, 3 * blocks),
        grid=(3 * blocks,),
        in_specs=[
            whole,
            pl.BlockSpec((1, width), lambda s: (0, 0)),
            whole,
        ]
        + [pl.BlockSpec((width // 4, cols), lambda s, i=i: (i, s)) for i in range(4)]
        + [
            pl.BlockSpec((per, 1, HEAD_DIM, tok), lambda s: (s % blocks, s // blocks, 0, 0))
            for _ in grads
        ],
        out_specs=whole,
        out_shape=jax.ShapeDtypeStruct((tok, width), f32),
        scratch_shapes=[pltpu.VMEM((width, tok), f32)],
        compiler_params=pltpu.CompilerParams(vmem_limit_bytes=60 << 20),
        cost_estimate=cost(6 * tok * width * width, 6 * width * width + 16 * tok * width),
        name="input_grad",
    )(x, gain.reshape(1, width), middle_grad, *[weight] * 4, *grads)


def wide_thirds(values):
    high = values.astype(bf16)
    rest = values - high.astype(f32)
    mid = rest.astype(bf16)
    low = (rest - mid.astype(f32)).astype(bf16)
    rows, lanes = values.shape
    blank = jnp.zeros((rows, 128 - 3 * lanes), bf16)
    return jnp.concatenate([high, mid, low, blank], axis=1)


def combine_kernel(
    counts, exp_ref, place_ref, ids_ref, probs_ref, middle_ref, cot_ref, normed_ref, gain_ref,
    router_ref, weight_ref, *refs,
):
    blocks, heads, parts, copies = counts
    experts = probs_ref.shape[1]
    backs, refs = refs[:blocks], refs[blocks:]
    row_grads, refs = refs[:blocks], refs[blocks:]
    mixed, refs = refs[:heads], refs[heads:]
    out_ref, mid_ref, refs = refs[0], refs[1], refs[2:]
    mixed_grads, refs = refs[:heads], refs[heads:]
    early, (slot_rows, slot_grads, wide) = refs[:parts], refs[parts:]
    tok, width = middle_ref.shape
    total = slot_rows.shape[0]

    at = 0
    for back, row_grad in zip(backs, row_grads):
        rows = slice(at, at + back.shape[0])
        slot_rows[rows, :] = back[...]
        slot_grads[rows, :] = row_grad[...]
        at += back.shape[0]

    slot = lax.broadcasted_iota(jnp.int32, (tok, total), 1)
    one = (slot == place_ref[:, 0:1]).astype(f32).astype(bf16)
    two = (slot == place_ref[:, 1:2]).astype(f32).astype(bf16)
    first = mm(one, slot_rows[...], NN)
    second = mm(two, slot_rows[...], NN)
    dy = mm(one + two, slot_grads[...], NN)

    lane = lax.broadcasted_iota(jnp.int32, (tok, experts), 1)
    is_first, is_second = lane == ids_ref[:, 0:1], lane == ids_ref[:, 1:2]
    probs = probs_ref[...]
    gate_first = jnp.sum(jnp.where(is_first, probs, 0.0), axis=1, keepdims=True)
    gate_second = jnp.sum(jnp.where(is_second, probs, 0.0), axis=1, keepdims=True)
    middle = middle_ref[...]
    cot = cot_ref[...].astype(f32)
    out_ref[...] = (middle + gate_first * first + gate_second * second).astype(bf16)
    grad_first = jnp.sum(cot * first, axis=1, keepdims=True)
    grad_second = jnp.sum(cot * second, axis=1, keepdims=True)
    probs_grad = jnp.where(is_first, grad_first, 0.0) + jnp.where(is_second, grad_second, 0.0)
    logits_grad = probs * (probs_grad - jnp.sum(probs * probs_grad, axis=1, keepdims=True))
    for e in range(experts):
        dy = dy + logits_grad[:, e : e + 1] * router_ref[e : e + 1, :]

    scale = lax.rsqrt(jnp.mean(middle * middle, axis=1, keepdims=True) + 1e-06)
    unit = middle * scale
    gain_terms = unit * dy
    dy = dy * gain_ref[...]
    middle_grad = cot + scale * (dy - unit * jnp.mean(unit * dy, axis=1, keepdims=True))
    mid_ref[...] = middle_grad
    branch = middle_grad.astype(bf16)

    groups, dim, _ = mixed_grads[0].shape
    back = mm(weight_ref[...], branch, NT).astype(bf16).reshape(groups, heads, dim, tok)
    for h in range(heads):
        mixed_grads[h][...] = back[:, h]
    for h in range(heads):
        grad = mm(mixed[h][...], branch, NN)
        for g in range(groups):
            at = (g * heads + h) * dim
            wide[at : at + dim, 0:width] = grad[g * dim : (g + 1) * dim]
    mark = lax.broadcasted_iota(jnp.int32, (tok, 128), 1) == 3 * experts
    mark = mark.astype(f32).astype(bf16)
    high = gain_terms.astype(bf16)
    low = (gain_terms - high.astype(f32)).astype(bf16)
    wide[:, width:] = (
        mm(normed_ref[...], wide_thirds(logits_grad), TN) + mm(high, mark, TN) + mm(low, mark, TN)
    )
    per = wide.shape[0] // (parts * copies)
    for d in range(parts):
        e = jnp.bitwise_xor(exp_ref[0], d)
        rows = [
            wide[pl.ds(pl.multiple_of((k * parts + e) * per, per), per), :] for k in range(copies)
        ]
        early[d][...] = jnp.concatenate(rows, axis=0).astype(bf16)


def combine(
    exp, place, ids, probs, middle, cot, normed, gain, router, weight, backs, row_grads, mixed,
    copies,
):
    tok, width = middle.shape
    heads = len(mixed)
    parts = probs.shape[1]
    groups = width // (heads * HEAD_DIM)
    total = sum(b.shape[0] for b in backs)
    sds = jax.ShapeDtypeStruct
    return pl.pallas_call(
        functools.partial(combine_kernel, (len(backs), heads, parts, copies)),
        in_specs=[pl.BlockSpec(memory_space=pltpu.SMEM)]
        + [pl.BlockSpec(memory_space=pltpu.VMEM)] * (9 + 2 * len(backs) + heads),
        out_specs=[pl.BlockSpec(memory_space=pltpu.VMEM)] * (2 + heads + parts),
        out_shape=[sds((tok, width), bf16), sds((tok, width), f32)]
        + [sds((groups, HEAD_DIM, tok), bf16)] * heads
        + [sds((width // parts, width + 128), bf16)] * parts,
        scratch_shapes=[
            pltpu.VMEM((total, width), bf16),
            pltpu.VMEM((total, width), bf16),
            pltpu.VMEM((width, width + 128), f32),
        ],
        compiler_params=pltpu.CompilerParams(vmem_limit_bytes=60 << 20),
        cost_estimate=cost(
            6 * tok * total * width + 4 * tok * width * width,
            4 * total * width + 18 * tok * width + 4 * width * width,
        ),
        name="combine",
    )(exp, place, ids, probs, middle, cot, normed, gain.reshape(1, width), router, weight,
      *backs, *row_grads, *mixed)


def finish_kernel(heads, lanes, n_ctx, exp_ref, rows_ref, weight_ref, gain_ref, grad_ref, gain_grad_ref, bias_ref):
    groups = rows_ref.shape[0]
    width = weight_ref.shape[1] // 3
    for part in range(3):
        pieces = []
        for g in range(groups):
            for h in range(heads):
                lo = h * lanes + part * HEAD_DIM
                pieces.append(rows_ref[g][:, lo : lo + HEAD_DIM].astype(f32))
        grad_ref[:, part * width : (part + 1) * width] = jnp.concatenate(pieces, axis=1)
    terms = weight_ref[...].astype(f32) * grad_ref[...]
    gain_grad_ref[...] = jnp.sum(terms, axis=1, keepdims=True) / gain_ref[...]
    columns = []
    for c in range(n_ctx):
        mine = rows_ref[exp_ref[0] * n_ctx + c].astype(f32)
        for h in range(heads):
            lo = h * lanes + 3 * HEAD_DIM
            columns.append(mine[:, lo : lo + 1])
    bias_ref[...] = jnp.concatenate(columns, axis=1)


def finish(exp, rows, weight_rows, gain_rows, heads, lanes, n_ctx):
    count, columns = weight_rows.shape
    sds = jax.ShapeDtypeStruct
    vmem = pl.BlockSpec(memory_space=pltpu.VMEM)
    return pl.pallas_call(
        functools.partial(finish_kernel, heads, lanes, n_ctx),
        in_specs=[pl.BlockSpec(memory_space=pltpu.SMEM), vmem, vmem, vmem],
        out_specs=[vmem, vmem, vmem],
        out_shape=[
            sds((count, columns), f32), sds((count, 1), f32), sds((count, heads * n_ctx), f32)
        ],
        cost_estimate=cost(4 * count * columns, 8 * count * columns),
        name="finish",
    )(exp, rows, weight_rows, gain_rows)


def route_kernel(heads, x_ref, place_ref, ids_ref, gain_ref, router_ref, weight_ref, *refs):
    mixed, (middle_ref, normed_ref, probs_ref, *slots, joined) = refs[:heads], refs[heads:]
    tok, width = x_ref.shape
    experts = probs_ref.shape[1]
    for h in range(heads):
        for g in range(width // (heads * HEAD_DIM)):
            at = (g * heads + h) * HEAD_DIM
            joined[at : at + HEAD_DIM, :] = mixed[h][g * HEAD_DIM : (g + 1) * HEAD_DIM, :]
    middle = x_ref[...].astype(f32) + mm(joined[...], weight_ref[...], TN)
    middle_ref[...] = middle
    scale = lax.rsqrt(jnp.mean(middle * middle, axis=1, keepdims=True) + 1e-06)
    normed = (middle * scale * gain_ref[...]).astype(bf16)
    normed_ref[...] = normed
    logits = mm(normed, router_ref[...], NN)[:, :experts]
    weights = jnp.exp(logits - jnp.max(logits, axis=1, keepdims=True))
    probs = weights / jnp.sum(weights, axis=1, keepdims=True)
    probs_ref[...] = probs
    lane = lax.broadcasted_iota(jnp.int32, (tok, experts), 1)
    gates = [
        wide_thirds(jnp.sum(jnp.where(lane == ids_ref[:, j : j + 1], probs, 0.0), axis=1, keepdims=True))
        for j in range(2)
    ]
    at = 0
    for slot_ref in slots:
        rows = slot_ref.shape[0]
        slot = lax.broadcasted_iota(jnp.int32, (rows, tok), 0) + at
        one = (slot == place_ref[0:1, :]).astype(f32).astype(bf16)
        two = (slot == place_ref[1:2, :]).astype(f32).astype(bf16)
        slot_ref[:, 0:width] = mm(one + two, normed, NN).astype(bf16)
        slot_ref[:, width:] = (mm(one, gates[0], NN) + mm(two, gates[1], NN)).astype(bf16)
        at += rows


def route(x, place, ids, gain, router, weight, mixed, sizes):
    tok, width = x.shape
    experts = router.shape[1]
    heads = len(mixed)
    sds = jax.ShapeDtypeStruct
    vmem = pl.BlockSpec(memory_space=pltpu.VMEM)
    return pl.pallas_call(
        functools.partial(route_kernel, heads),
        in_specs=[vmem] * (6 + heads),
        out_specs=[vmem] * (3 + len(sizes)),
        out_shape=[sds((tok, width), f32), sds((tok, width), bf16), sds((tok, experts), f32)]
        + [sds((size, width + 128), bf16) for size in sizes],
        scratch_shapes=[pltpu.VMEM((width, tok), bf16)],
        compiler_params=pltpu.CompilerParams(vmem_limit_bytes=60 << 20),
        cost_estimate=cost(
            2 * tok * width * (width + sum(sizes)), 12 * tok * width + 2 * width * width
        ),
        name="route",
    )(x, place.T, ids, gain.reshape(1, width), jnp.pad(router, ((0, 0), (0, 128 - experts))),
      weight, *mixed)


def sequence_grad_kernel(heads, n_exp, copies, dp_ref, *refs):
    outs, offsets, refs = refs[:heads], refs[heads : 2 * heads], refs[2 * heads :]
    normed_refs, (*shares, acc) = refs[:4], refs[4:]
    step = pl.program_id(0)
    width, lanes = acc.shape[0], acc.shape[1] // heads
    own = 3 * HEAD_DIM

    @pl.when(step == 0)
    def _():
        acc[...] = jnp.zeros_like(acc)

    normed = jnp.concatenate([ref[0] for ref in normed_refs], axis=0)
    for h, out_ref in enumerate(outs):
        rows = out_ref[0].reshape(own, out_ref.shape[3])
        acc[:, h * lanes : h * lanes + own] += mm(normed, rows, NT)

    @pl.when(step == pl.num_programs(0) - 1)
    def _():
        count = offsets[0].shape[0]
        buckets, rows_dev = count // copies, width // (copies * n_exp)
        row = lax.broadcasted_iota(jnp.int32, (width, count), 0)
        bucket = lax.broadcasted_iota(jnp.int32, (width, count), 1)
        place = row // (n_exp * rows_dev) * buckets + row % rows_dev
        here = ((place == bucket) & (row % rows_dev < buckets)).astype(f32).astype(bf16)
        base = own // 128 * 128
        lane = lax.broadcasted_iota(jnp.int32, (width, 128), 1) + base
        for h, offsets_ref in enumerate(offsets):
            table = jnp.sum(offsets_ref[...], axis=1, keepdims=True)
            column = jnp.sum(mm(here, wide_thirds(table), NN), axis=1, keepdims=True)
            at = h * lanes + base
            acc[:, at : at + 128] += jnp.where(lane == own, column, 0.0)
        per = shares[0].shape[0]
        for d, share in enumerate(shares):
            start = pl.multiple_of(jnp.bitwise_xor(dp_ref[0], d) * per, per)
            share[...] = acc[pl.ds(start, per), :].astype(bf16)


def sequence_grad(dp, normed, outs, offsets, n_dp, n_exp, copies, lanes):
    groups, _, dim, tok = outs[0].shape
    width = normed.shape[1]
    heads = len(outs)
    columns = heads * lanes
    return pl.pallas_call(
        functools.partial(sequence_grad_kernel, heads, n_exp, copies),
        grid_spec=pltpu.PrefetchScalarGridSpec(
            num_scalar_prefetch=1,
            grid=(groups,),
            in_specs=[pl.BlockSpec((1, 3, dim, tok), lambda g, d: (g, 0, 0, 0)) for _ in outs]
            + [pl.BlockSpec(o.shape, lambda g, d: (0, 0)) for o in offsets]
            + [
                pl.BlockSpec((1, width // 4, tok), lambda g, d, i=i: (g, i, 0)) for i in range(4)
            ],
            out_specs=[pl.BlockSpec((width // n_dp, columns), lambda g, d: (0, 0))] * n_dp,
            scratch_shapes=[pltpu.VMEM((width, columns), f32)],
        ),
        out_shape=[jax.ShapeDtypeStruct((width // n_dp, columns), bf16)] * n_dp,
        compiler_params=pltpu.CompilerParams(vmem_limit_bytes=60 << 20),
        cost_estimate=cost(
            6 * heads * dim * groups * tok * width, 2 * groups * tok * (width + 3 * heads * dim)
        ),
        name="sequence_grad",
    )(dp, *outs, *offsets, *[normed] * 4)


def dot_f32(left, right, left_dim, right_dim):
    return mm(left, right, (((left_dim,), (right_dim,)), ((), ())))


def swap_blocks(blocks, axes):
    return lax.all_to_all(blocks, axes, split_axis=0, concat_axis=0, tiled=True)


def exchange(parts, axis="expert"):
    n = len(parts)
    return [parts[0]] + [
        lax.ppermute(parts[d], axis, [(i, i ^ d) for i in range(n)]) for d in range(1, n)
    ]


def add_low(parts):
    return sum(part.astype(f32) for part in parts).astype(bf16)


def after(value, *others):
    return lax.optimization_barrier((value, others))[0]


def attention_plan(block_row, bucket_ids, blocks, tok):
    length = blocks * tok
    pad = jnp.full((1,), -1, jnp.int32)
    buck_rev = jnp.broadcast_to(jnp.concatenate([pad, bucket_ids[::-1]])[None], (8, 2 * length))
    buck = jnp.broadcast_to(jnp.concatenate([pad, bucket_ids])[None], (8, 2 * length))
    ids = jnp.arange(16)
    hot = (block_row[None, :] == ids[:, None]).astype(bf16)
    hide = jnp.where(ids[:, None] > block_row[None, :], HIDE, 0.0).astype(bf16)
    kmask_t = jnp.concatenate(
        [hot, jnp.ones((3, length), bf16), jnp.zeros((45, length), bf16)], axis=0
    )
    qmask = jnp.concatenate([hide, jnp.zeros((48, length), bf16)], axis=0)
    last = block_row.reshape(blocks, tok)[:, -1]
    seen = jnp.sum((block_row[None, :] <= last[:, None]).astype(jnp.int32), axis=1)
    return buck_rev, buck, kmask_t, qmask, hide, seen


def shards(
    layer_input,
    attn_gain,
    qkv_weight,
    out_weight,
    bias_table,
    moe_gain,
    router_weight,
    expert_in,
    expert_down,
    expert_ids,
    fill_order,
    block_ids,
    bucket_ids,
    cotangent,
):
    tok, width = layer_input.shape
    n_dp, n_ctx, n_exp = lax.axis_size("dp"), lax.axis_size("ctx"), lax.axis_size("expert")
    groups = n_ctx * n_exp
    copies = n_dp * n_ctx
    head_exp = bias_table.shape[1]
    heads = head_exp // n_ctx
    experts = router_weight.shape[1]
    ff_width = expert_down.shape[1]
    capacity = 5 * TOP * tok // (4 * experts)
    cut = (capacity // 2 + 15) // 16 * 16
    spans = ((0, cut), (cut, capacity))
    ctx_index = lax.axis_index("ctx")
    exp_index = lax.axis_index("expert")
    ctx_arg = ctx_index.astype(jnp.int32).reshape(1)
    pair = ("expert", "ctx")
    step_k = 1024

    def order(p):
        return (p % n_exp) * n_ctx + p // n_exp

    def in_swap_order(blocks):
        shape = blocks.shape
        return jnp.swapaxes(blocks.reshape((n_ctx, n_exp) + shape[1:]), 0, 1).reshape(shape)

    exp_arg = exp_index.astype(jnp.int32).reshape(1)
    normed_t, *parts = project(layer_input, attn_gain, qkv_weight, groups, heads)
    qkv = [swap_blocks(part, pair) for part in parts]
    table_dev = lax.dynamic_slice_in_dim(bias_table, ctx_index * heads, heads, 1)
    buck_rev, buck, kmask, qmask, hide, seen = attention_plan(
        block_ids[0], bucket_ids, groups, tok
    )
    chunks = (seen + step_k - 1) // step_k

    flat_ids = expert_ids.reshape(TOP * tok)
    fill_rank = fill_order.reshape(TOP * tok)
    same_expert = flat_ids[:, None] == flat_ids[None, :]
    earlier = fill_rank[None, :] < fill_rank[:, None]
    slot_of = jnp.sum((same_expert & earlier).astype(jnp.int32), axis=1)
    slots = slot_of.reshape(tok, TOP)
    part_at = jnp.where(slots < cut, 0, experts * cut - cut)
    stride = jnp.where(slots < cut, cut, capacity - cut)
    place = jnp.where(
        slots < capacity,
        part_at + jnp.bitwise_xor(expert_ids, exp_index) * stride + slots,
        -1,
    )
    sizes = [high - low for low, high in spans for _ in range(experts)]

    def to_slots(rows):
        parts, at = [], 0
        for size in sizes:
            slot = jnp.arange(at, at + size)[:, None]
            hot = (slot == place[None, :, 0]) | (slot == place[None, :, 1])
            parts.append(dot_f32(hot.astype(bf16), rows, 1, 0).astype(bf16))
            at += size
        return parts

    forward, mixed = [], []
    cot_slots = to_slots(cotangent)
    slots_a, slots_b = cot_slots[:experts], cot_slots[experts:]
    rows_dev = width // (n_dp * groups)
    my_rows = ((lax.axis_index("dp") * n_ctx + ctx_index) * n_exp + exp_index) * rows_dev
    weight_rows = lax.dynamic_slice_in_dim(qkv_weight, my_rows, rows_dev, 0)
    gain_rows = lax.dynamic_slice_in_dim(attn_gain, my_rows, rows_dev, 0).reshape(rows_dev, 1)
    qkv[0], place, slots_a, slots_b, buck_rev, buck, kmask, qmask, hide, weight_rows, gain_rows = (
        lax.optimization_barrier(
            (
                qkv[0], place, slots_a, slots_b, buck_rev, buck, kmask, qmask, hide, weight_rows,
                gain_rows,
            )
        )
    )
    normed_seq = lax.all_gather(after(normed_t, qkv[0]), pair)
    for h in range(heads):
        arg = after(qkv[h], forward)
        if h == heads - 1:
            grad_a = exchange(after(slots_a, arg))
        out = attention_fwd(
            order, chunks, table_dev[:, h], buck_rev, kmask, qmask, arg, step_k
        )
        out = after(out, qkv[h + 1] if h < heads - 1 else grad_a, mixed)
        forward.append(out)
        mixed.append(swap_blocks(out[0], pair).reshape(groups * HEAD_DIM, tok))
    mixed = after(mixed, forward)
    middle, normed_moe, probs, *sent = route(
        layer_input, place, expert_ids, moe_gain, router_weight, out_weight, mixed, sizes
    )
    x_a, x_b = exchange(sent[:experts]), exchange(sent[experts:])

    grad_b = exchange(after(slots_b, x_a))
    run_a = after(expert_fwd(x_a, expert_in, expert_down), x_b, grad_b)
    produced_a = exchange(list(run_a[3:]))
    run_b = expert_fwd(after(x_b, run_a), expert_in, expert_down)
    run_b = after(run_b, produced_a, normed_seq)
    produced_b = exchange(list(run_b[3:]))
    hidden = [run_a[0], run_b[0]]
    tiles = ff_width // 256
    cuts = (0, (tiles + 1) // 2, tiles)
    g_args = after(grad_a + grad_b, run_b)
    down_1 = down_grad(ctx_arg, hidden, g_args, x_a + x_b, copies, 0, cuts[1])

    def sum_dp(half):
        return lax.psum_scatter(half, "dp", scatter_dimension=0, tiled=True)

    def to_ctx(half):
        return lax.ppermute(half, "ctx", [(0, 1), (1, 0)])

    came = to_ctx(down_1[1])
    g_args = after(grad_a + grad_b, down_1)
    down_2 = down_grad(ctx_arg, hidden, g_args, x_a + x_b, copies, cuts[1], tiles - cuts[1])
    undo_a = expert_bwd(
        after(grad_a, down_2), x_a, run_a[1], run_a[2], expert_in, expert_down
    )
    undo_a, came = lax.optimization_barrier((after(undo_a, produced_b), came))
    halves = [add_low((down_1[0], came))]
    grads_a = exchange(list(undo_a[1:]))
    came = to_ctx(after(down_2[1], undo_a))
    undo_b = expert_bwd(
        after(grad_b, undo_a), x_b, run_b[1], run_b[2], expert_in, expert_down
    )
    undo_b, came = lax.optimization_barrier((after(undo_b, grads_a), came))
    halves.append(add_low((down_2[0], came)))
    grads_b = exchange(list(undo_b[1:]))
    grads_in = [undo_a[0], undo_b[0]]
    total = 2 * tiles
    size_a, size_d = total * 3 // 22, total * 8 // 22
    xt = turn(ctx_arg, x_a + x_b, copies)
    part_a = in_grad(after(xt, undo_b), grads_in, 0, size_a)
    came_a = to_ctx(after(part_a[1], halves[1]))
    part_b = in_grad(after(xt, part_a), grads_in, size_a, size_a)
    part_d = in_grad(after(xt, part_b), grads_in, 2 * size_a, size_d)

    part_d, grads_b, came_a = lax.optimization_barrier((part_d, grads_b, came_a))
    came_b = to_ctx(after(part_b[1], came_a))
    layer_output, middle_grad, *outs = combine(
        exp_arg, place, expert_ids, probs, middle, cotangent, normed_moe, moe_gain,
        router_weight.T.astype(f32), out_weight, produced_a + produced_b, grads_a + grads_b, mixed,
        copies,
    )
    down_sums = [sum_dp(half) for half in halves]
    outs, came_b, down_sums[0] = lax.optimization_barrier((outs, came_b, down_sums[0]))
    half_a = jnp.concatenate(
        [add_low((part_a[0], came_a)), add_low((part_b[0], came_b))], axis=1
    )
    first = 2 * size_a + size_d
    part_c = in_grad(after(xt, outs), grads_in, first, total - first)
    early = outs[heads:]
    mixed_grad = [swap_blocks(part, pair) for part in outs[:heads]]

    last_own, last_other = [sum_dp(half) for half in part_d]
    sum_a = sum_dp(half_a)

    lanes = -(-(3 * HEAD_DIM + 1) // 128) * 128
    dp_arg = lax.axis_index("dp").astype(jnp.int32).reshape(1)
    backward, grads = [], []
    for h in range(heads):
        arg = after(mixed_grad[h], backward if h else (part_c, half_a))
        beside = [grads[h - 1]] if h else []
        if h == 0:
            came_c = to_ctx(after(part_c[1], arg))
            early_parts = exchange(after(early, arg))
            beside += [came_c, early_parts, last_own, last_other, down_sums[1]] + mixed_grad[1:2]
        else:
            arg = after(arg, half_c)
        if h == heads - 1:
            last_came = to_ctx(after(last_other, arg))
            beside += [last_came, sum_a]
        out = attention_bwd(
            order, chunks, table_dev[:, h], buck, kmask, hide, qkv[h], forward[h][0],
            arg, forward[h][1], step_k,
        )
        out, beside = lax.optimization_barrier((out, beside))
        if h == 0:
            half_c = add_low((part_c[0], beside[0]))
            sum_c = sum_dp(half_c)
            early_half = sum_dp(after(add_low(beside[1]), half_c))
        backward.append(out)
        grads.append(swap_blocks(out[0], pair))
    shares = sequence_grad(
        dp_arg, normed_seq, [out[0] for out in backward], [out[1] for out in backward], n_dp,
        n_exp, copies, lanes,
    )
    late = exchange(shares, "dp")
    in_sums = [sum_a, add_low((last_own, after(last_came, backward))), sum_c]
    input_grad = input_gradient(layer_input, attn_gain, middle_grad, qkv_weight, grads)
    late, input_grad = lax.optimization_barrier((late, input_grad))
    late = add_low(late)
    rows_out = swap_blocks(in_swap_order(late.reshape(groups, rows_dev, -1)), pair)
    early_half = after(early_half, backward).reshape(n_ctx, rows_dev, width + 128)
    early_own, early_other = [
        lax.dynamic_index_in_dim(early_half, at, 0, False) for at in (ctx_index, 1 - ctx_index)
    ]
    early_rows = early_own.astype(f32) + lax.ppermute(
        early_other, "ctx", [(0, 1), (1, 0)]
    ).astype(f32)
    expert_in_grad = jnp.concatenate(in_sums, axis=1).astype(f32)
    expert_down_grad = jnp.concatenate(after(down_sums, backward), axis=1).astype(f32)
    rows_out, input_grad, expert_in_grad, expert_down_grad, early_rows = (
        lax.optimization_barrier(
            (rows_out, input_grad, expert_in_grad, expert_down_grad, early_rows)
        )
    )
    qkv_grad, attn_gain_grad, bias_rows = finish(
        exp_arg,
        rows_out,
        weight_rows,
        gain_rows,
        heads,
        lanes,
        n_ctx,
    )
    router_grad = sum(
        early_rows[:, width + i * experts : width + (i + 1) * experts] for i in range(3)
    )
    return (
        layer_output,
        input_grad,
        attn_gain_grad.reshape(rows_dev),
        qkv_grad,
        early_rows[:, :width],
        bias_rows[: bias_table.shape[0] // copies],
        early_rows[:, width + 3 * experts],
        router_grad,
        expert_in_grad[None],
        expert_down_grad,
    )


def solution(mesh):
    rows = P(("dp", "ctx", "expert"), None)
    return jax.shard_map(
        shards,
        mesh=mesh,
        in_specs=(
            rows,
            P(),
            P(),
            P(),
            P(None, "expert"),
            P(),
            P(),
            P("expert", None, None),
            P("expert", None, None),
            rows,
            rows,
            P("dp", None),
            P(),
            rows,
        ),
        out_specs=(
            rows,
            rows,
            P(("dp", "ctx", "expert")),
            rows,
            rows,
            P(("dp", "ctx"), "expert"),
            P(("dp", "ctx", "expert")),
            rows,
            P("expert", ("dp", "ctx"), None),
            P("expert", None, ("dp", "ctx")),
        ),
        check_vma=False,
    )
```

```python
import functools

import jax
import jax.numpy as jnp
from jax import lax
from jax.experimental import pallas as pl
from jax.experimental.pallas import tpu as pltpu
from jax.sharding import PartitionSpec as P


HEAD_DIM = 64
TOP = 2
LOG2E = 1.4426950408889634
SCALE = 0.125 * LOG2E
HIDE = -(2.0**100)
f32 = jnp.float32
bf16 = jnp.bfloat16
highest = lax.Precision.HIGHEST
NN = (((1,), (0,)), ((), ()))
NT = (((1,), (1,)), ((), ()))
TN = (((0,), (0,)), ((), ()))


def mm(left, right, dims):
    return lax.dot_general(left, right, dims, preferred_element_type=f32)


def stack_refs(refs):
    return jnp.concatenate([ref[...] for ref in refs], axis=0)


def cost(flops, bytes_accessed, transcendentals=0):
    return pl.CostEstimate(
        flops=int(flops), bytes_accessed=int(bytes_accessed), transcendentals=int(transcendentals)
    )


def fill_table(tab_ref, buck_ref, tb_ref, width, mul):
    buck = buck_ref[...]
    row = jnp.zeros(buck.shape, f32)
    for b in range(tab_ref.shape[0]):
        row = jnp.where(buck == b, tab_ref[b] * mul, row)
    for m in range(16):
        rolled = pltpu.roll(row, 8 * m, 1, stride=1, stride_axis=0)
        for c in range(width // 128 - 1):
            lo = width - 128 - 128 * c
            tb_ref[16 * c + m] = rolled[:, lo : lo + 128]


def bias_tile(tb_ref, start, rows, cols):
    parts = [
        tb_ref[pl.ds(start - 16 * c, rows // 8)].reshape(rows, 128) for c in range(cols // 128)
    ]
    return jnp.concatenate(parts, axis=1)


def attention_fwd_kernel(
    bk, order, nch_ref, tab_ref, buck_ref, kmask_ref, qmask_ref, q_ref, k_ref, v_ref,
    o_ref, lse_ref, kaug, vaug, tb,
):
    qi = pl.program_id(0)
    blocks, _, _, tok = k_ref.shape
    length = blocks * tok

    @pl.when(qi == 0)
    def _():
        fill_table(tab_ref, buck_ref, tb, 2 * length, LOG2E)
        first = lax.broadcasted_iota(jnp.int32, (16, length), 0) == 0
        vaug[HEAD_DIM:, :] = first.astype(f32).astype(bf16)
        for p in range(blocks):
            rows = slice(p * tok, (p + 1) * tok)
            kaug[rows, :] = jnp.concatenate([k_ref[order(p), 0], kmask_ref[:, rows]], axis=0).T
            vaug[0:HEAD_DIM, rows] = v_ref[order(p), 0]

    qaug = jnp.concatenate([q_ref[0, 0], qmask_ref[...]], axis=0)
    base = (length - 128) // 8 - qi * (tok // 8)

    def step(j, carry):
        peak, acc = carry
        ks = pl.ds(pl.multiple_of(j * bk, bk), bk)
        scores = mm(kaug[ks, :], qaug, NN) * SCALE + bias_tile(tb, base + j * (bk // 8), bk, tok)
        now = jnp.maximum(peak, jnp.max(scores, axis=0, keepdims=True))
        weights = jnp.exp2(scores - now).astype(bf16)
        return now, acc * jnp.exp2(peak - now) + mm(vaug[:, ks], weights, NN)

    start = (jnp.full((1, tok), -1e37, f32), jnp.zeros((HEAD_DIM + 16, tok), f32))
    peak, acc = lax.fori_loop(0, nch_ref[qi], step, start)
    total = acc[HEAD_DIM : HEAD_DIM + 1]
    o_ref[0] = (acc[0:HEAD_DIM] / total).astype(bf16)
    lse_ref[0] = peak + jnp.log2(total)


def attention_fwd(order, chunks, table, buck, kmask, qmask, qkv, bk):
    blocks, _, dim, tok = qkv.shape
    length = blocks * tok
    return pl.pallas_call(
        functools.partial(attention_fwd_kernel, bk, order),
        grid_spec=pltpu.PrefetchScalarGridSpec(
            num_scalar_prefetch=2,
            grid=(blocks,),
            in_specs=[
                pl.BlockSpec((8, 2 * length), lambda i, *_: (0, 0)),
                pl.BlockSpec((64, length), lambda i, *_: (0, 0)),
                pl.BlockSpec((64, tok), lambda i, *_: (0, i)),
                pl.BlockSpec((1, 1, dim, tok), lambda i, *_: (order(i), 0, 0, 0)),
                pl.BlockSpec((blocks, 1, dim, tok), lambda i, *_: (0, 1, 0, 0)),
                pl.BlockSpec((blocks, 1, dim, tok), lambda i, *_: (0, 2, 0, 0)),
            ],
            out_specs=[
                pl.BlockSpec((1, dim, tok), lambda i, *_: (order(i), 0, 0)),
                pl.BlockSpec((1, 1, tok), lambda i, *_: (i, 0, 0)),
            ],
            scratch_shapes=[
                pltpu.VMEM((length, 128), bf16),
                pltpu.VMEM((dim + 16, length), bf16),
                pltpu.VMEM((2 * length // 8 - 16, 8, 128), f32),
            ],
        ),
        out_shape=[
            jax.ShapeDtypeStruct((blocks, dim, tok), bf16),
            jax.ShapeDtypeStruct((blocks, 1, tok), f32),
        ],
        compiler_params=pltpu.CompilerParams(vmem_limit_bytes=60 << 20),
        cost_estimate=cost(2000 * length * length // 2, 4 * length * 2 * dim, length * length // 2),
        name="attention_fwd",
    )(chunks, table, buck, kmask, qmask, qkv, qkv, qkv)


def three_rows(values, rows):
    high = values.astype(bf16).astype(f32)
    mid = (values - high).astype(bf16).astype(f32)
    row = lax.broadcasted_iota(jnp.int32, (rows, values.shape[1]), 0)
    out = jnp.where(row == 0, high, jnp.where(row == 1, mid, jnp.where(row == 2, values - high - mid, 0.0)))
    return out.astype(bf16)


def attention_bwd_kernel(
    bk, order, nch_ref, tab_ref, buck_ref, kmask_ref, qmask_ref, q_ref, k_ref, v_ref, o_ref,
    do_ref, lse_ref, out_ref, off_ref, knat, kaug, vaug, tb, gb, dkacc, dvacc,
):
    qi = pl.program_id(0)
    blocks, _, _, tok = k_ref.shape
    length = blocks * tok

    @pl.when(qi == 0)
    def _():
        fill_table(tab_ref, buck_ref, tb, 2 * length, LOG2E)
        gb[...] = jnp.zeros_like(gb)
        dkacc[...] = jnp.zeros_like(dkacc)
        dvacc[...] = jnp.zeros_like(dvacc)
        three = lax.broadcasted_iota(jnp.int32, (64, length), 0) < 3
        vaug[64:128, :] = three.astype(f32).astype(bf16)
        kaug[64:128, :] = kmask_ref[...]
        for p in range(blocks):
            rows = slice(p * tok, (p + 1) * tok)
            knat[rows, :] = k_ref[order(p), 0].T
            kaug[0:64, rows] = k_ref[order(p), 0]
            vaug[0:64, rows] = v_ref[order(p), 0]

    q_t = q_ref[0, 0]
    do_t = do_ref[0]
    delta = jnp.sum(do_t.astype(f32) * o_ref[0].astype(f32), axis=0, keepdims=True)
    lse = lse_ref[0] * (1.0 / SCALE)
    blank = jnp.zeros((32, tok), bf16)
    qaug = jnp.concatenate([q_t, qmask_ref[...], three_rows(-lse, 16), blank], axis=0).T
    doaug = jnp.concatenate([do_t, three_rows(-delta, 32), blank], axis=0).T
    base = (length - 128) // 8 + qi * (tok // 8)

    half = tok // 2

    def step(j, dq):
        ks = pl.ds(pl.multiple_of(j * bk, bk), bk)
        parts = []
        for i in range(2):
            rows = slice(i * half, (i + 1) * half)
            start = base + i * (half // 8) - j * (bk // 8)
            scores = mm(qaug[rows], kaug[:, ks], NN) * SCALE + bias_tile(tb, start, half, bk)
            probs = jnp.exp2(scores)
            ds = probs * mm(doaug[rows], vaug[:, ks], NN)
            for c in range(bk // 128):
                at = pl.ds(start - 16 * c, half // 8)
                gb[at] += ds[:, 128 * c : 128 * c + 128].reshape(half // 8, 8, 128)
            low = ds.astype(bf16)
            dvacc[:, ks] += mm(do_t[:, rows], probs.astype(bf16), NN)
            dkacc[:, ks] += mm(q_t[:, rows], low, NN)
            parts.append(mm(low, knat[ks, :], NN))
        return dq + jnp.concatenate(parts, axis=0)

    dq = lax.fori_loop(0, nch_ref[qi], step, jnp.zeros((tok, 64), f32))
    out_ref[order(qi), 0] = (dq * 0.125).T.astype(bf16)

    @pl.when(qi == blocks - 1)
    def _():
        for p in range(blocks):
            rows = slice(p * tok, (p + 1) * tok)
            out_ref[order(p), 1] = (dkacc[:, rows] * 0.125).astype(bf16)
            out_ref[order(p), 2] = dvacc[:, rows].astype(bf16)
        width = 2 * length
        total = jnp.zeros((8, width), f32)
        for m in range(16):
            tiles = [gb[16 * c + m] for c in range(width // 128 - 2, -1, -1)]
            skewed = jnp.concatenate([jnp.zeros((8, 128), f32)] + tiles, axis=1)
            total = total + (pltpu.roll(skewed, width - 8 * m, 1) if m else skewed)
        row = total[0:1]
        for s in range(1, 8):
            row = row + pltpu.roll(total[s : s + 1], width - s, 1)
        buck = buck_ref[0:1, :]
        for b in range(off_ref.shape[0]):
            mine = jnp.where(buck == b, row, 0.0)
            parts = [mine[:, 128 * c : 128 * c + 128] for c in range(width // 128)]
            while len(parts) > 1:
                parts = [x + y for x, y in zip(parts[::2], parts[1::2])]
            off_ref[b : b + 1, :] = parts[0]


def attention_bwd(order, chunks, table, buck, kmask, qmask, qkv, mixed, mixed_grad, lse, bk):
    blocks, _, dim, tok = qkv.shape
    length = blocks * tok
    one = pl.BlockSpec((1, dim, tok), lambda i, *_: (order(i), 0, 0))
    return pl.pallas_call(
        functools.partial(attention_bwd_kernel, bk, order),
        grid_spec=pltpu.PrefetchScalarGridSpec(
            num_scalar_prefetch=2,
            grid=(blocks,),
            in_specs=[
                pl.BlockSpec((8, 2 * length), lambda i, *_: (0, 0)),
                pl.BlockSpec((64, length), lambda i, *_: (0, 0)),
                pl.BlockSpec((16, tok), lambda i, *_: (0, i)),
                pl.BlockSpec((1, 1, dim, tok), lambda i, *_: (order(i), 0, 0, 0)),
                pl.BlockSpec((blocks, 1, dim, tok), lambda i, *_: (0, 1, 0, 0)),
                pl.BlockSpec((blocks, 1, dim, tok), lambda i, *_: (0, 2, 0, 0)),
                one,
                one,
                pl.BlockSpec((1, 1, tok), lambda i, *_: (i, 0, 0)),
            ],
            out_specs=[
                pl.BlockSpec((blocks, 3, dim, tok), lambda i, *_: (0, 0, 0, 0)),
                pl.BlockSpec((table.shape[0], 128), lambda i, *_: (0, 0)),
            ],
            scratch_shapes=[
                pltpu.VMEM((length, dim), bf16),
                pltpu.VMEM((128, length), bf16),
                pltpu.VMEM((128, length), bf16),
                pltpu.VMEM((2 * length // 8 - 16, 8, 128), f32),
                pltpu.VMEM((2 * length // 8 - 16, 8, 128), f32),
                pltpu.VMEM((dim, length), f32),
                pltpu.VMEM((dim, length), f32),
            ],
        ),
        out_shape=[
            jax.ShapeDtypeStruct((blocks, 3, dim, tok), bf16),
            jax.ShapeDtypeStruct((table.shape[0], 128), f32),
        ],
        compiler_params=pltpu.CompilerParams(vmem_limit_bytes=60 << 20),
        cost_estimate=cost(5000 * length * length // 2, 8 * length * 2 * dim, length * length // 2),
        name="attention_bwd",
    )(chunks, table, buck, kmask, qmask, qkv, qkv, qkv, mixed, mixed_grad, lse)


def write_groups(acc, refs):
    rows = refs[0].shape[0]
    for d, ref in enumerate(refs):
        ref[...] = acc[d * rows : (d + 1) * rows, :].astype(bf16)


def join_rows(refs, scratch):
    at = 0
    for ref in refs:
        scratch[at : at + ref.shape[0], :] = ref[:, : scratch.shape[1]]
        at += ref.shape[0]


def gate_column(refs):
    return jnp.concatenate(
        [jnp.sum(ref[...].astype(f32), axis=1, keepdims=True) for ref in refs], axis=0
    )


def expert_fwd_kernel(steps, groups, wg_ref, wu_ref, wd_ref, *refs):
    xs, refs = refs[:groups], refs[groups:]
    ht_ref, act_ref, slope_ref, *outs, rows, acc = refs
    f = pl.program_id(0)

    @pl.when(f == 0)
    def _():
        join_rows(xs, rows)
        acc[...] = jnp.zeros_like(acc)

    x = rows[...]
    gate = mm(x, wg_ref[0], NN)
    up = mm(x, wu_ref[0], NN)
    square = gate * gate
    t = jnp.tanh(gate * (0.7978845608028654 + 0.035677408136300125 * square))
    half = 0.5 + 0.5 * t
    act = gate * half
    slope = half + (gate * (0.5 - 0.5 * t * t)) * (
        0.7978845608028654 + 0.10703222440890037 * square
    )
    hidden = (act * up).astype(bf16)
    ht_ref[...] = hidden.T
    act_ref[...] = act.astype(bf16)
    slope_ref[...] = (slope * up).astype(bf16)
    acc[...] += mm(hidden, wd_ref[0], NN)

    @pl.when(f == steps - 1)
    def _():
        write_groups(acc, outs)


def expert_fwd(xs, w_in, w_down, tile=256):
    groups = len(xs)
    ff, width = w_down.shape[1:]
    rows = groups * xs[0].shape[0]
    steps = ff // tile
    part = pl.BlockSpec((rows, tile), lambda f: (0, f))
    inner = jax.ShapeDtypeStruct((rows, ff), bf16)
    one = pl.BlockSpec((rows // groups, width), lambda f: (0, 0))
    return pl.pallas_call(
        functools.partial(expert_fwd_kernel, steps, groups),
        grid=(steps,),
        in_specs=[
            pl.BlockSpec((1, width, tile), lambda f: (0, 0, f)),
            pl.BlockSpec((1, width, tile), lambda f: (0, 0, f + steps)),
            pl.BlockSpec((1, tile, width), lambda f: (0, f, 0)),
        ]
        + [pl.BlockSpec(xs[0].shape, lambda f: (0, 0))] * groups,
        out_specs=[pl.BlockSpec((tile, rows), lambda f: (f, 0)), part, part] + [one] * groups,
        out_shape=[jax.ShapeDtypeStruct((ff, rows), bf16), inner, inner]
        + [jax.ShapeDtypeStruct((rows // groups, width), bf16)] * groups,
        scratch_shapes=[pltpu.VMEM((rows, width), bf16), pltpu.VMEM((rows, width), f32)],
        compiler_params=pltpu.CompilerParams(vmem_limit_bytes=60 << 20),
        cost_estimate=cost(
            10 * rows * width * ff, 6 * width * ff + rows * (4 * width + 6 * ff), rows * ff
        ),
        name="expert_fwd",
    )(w_in, w_in, w_down, *xs)


def expert_bwd_kernel(steps, groups, act_ref, slope_ref, wg_ref, wu_ref, wd_ref, *refs):
    gs, gates, refs = refs[:groups], refs[groups : 2 * groups], refs[2 * groups :]
    grads_ref, *outs, pg, acc = refs
    f = pl.program_id(0)

    @pl.when(f == 0)
    def _():
        join_rows(gs, pg)
        pg[...] = (pg[...].astype(f32) * gate_column(gates)).astype(bf16)
        acc[...] = jnp.zeros_like(acc)

    hidden_grad = mm(pg[...], wd_ref[0], NT)
    dg = (slope_ref[...].astype(f32) * hidden_grad).astype(bf16)
    du = (act_ref[...].astype(f32) * hidden_grad).astype(bf16)
    grads_ref[0] = dg
    grads_ref[1] = du
    acc[...] += mm(dg, wg_ref[0], NT) + mm(du, wu_ref[0], NT)

    @pl.when(f == steps - 1)
    def _():
        write_groups(acc, outs)


def gate_block(x, width):
    return pl.BlockSpec((x.shape[0], 128), lambda f, *_: (0, width // 128))


def expert_bwd(gs, xs, act, slope, w_in, w_down, tile=256):
    groups = len(gs)
    rows, width = groups * gs[0].shape[0], gs[0].shape[1]
    ff = w_down.shape[1]
    steps = ff // tile
    part = pl.BlockSpec((rows, tile), lambda f: (0, f))
    one = pl.BlockSpec((rows // groups, width), lambda f: (0, 0))
    return pl.pallas_call(
        functools.partial(expert_bwd_kernel, steps, groups),
        grid=(steps,),
        in_specs=[
            part,
            part,
            pl.BlockSpec((1, width, tile), lambda f: (0, 0, f)),
            pl.BlockSpec((1, width, tile), lambda f: (0, 0, f + steps)),
            pl.BlockSpec((1, tile, width), lambda f: (0, f, 0)),
        ]
        + [one] * groups
        + [gate_block(x, width) for x in xs],
        out_specs=[pl.BlockSpec((2, rows, tile), lambda f: (0, 0, f))] + [one] * groups,
        out_shape=[jax.ShapeDtypeStruct((2, rows, ff), bf16)]
        + [jax.ShapeDtypeStruct((rows // groups, width), bf16)] * groups,
        scratch_shapes=[pltpu.VMEM((rows, width), bf16), pltpu.VMEM((rows, width), f32)],
        compiler_params=pltpu.CompilerParams(vmem_limit_bytes=60 << 20),
        cost_estimate=cost(
            10 * rows * width * ff, 6 * width * ff + rows * (4 * width + 8 * ff)
        ),
        name="expert_bwd",
    )(act, slope, w_in, w_in, w_down, *gs, *xs)


def column_block(ref, blk, ctx, flip, a):
    low = ref[:, 2 * a * blk : (2 * a + 1) * blk]
    high = ref[:, (2 * a + 1) * blk : (2 * a + 2) * blk]
    return jnp.where(lax.rem(ctx + flip, 2) == 0, low, high)


def turn_kernel(copies, ctx_ref, *refs):
    xs, xt_ref = refs[:-1], refs[-1]
    blk = xt_ref.shape[0] // copies
    at = 0
    for x_ref in xs:
        rows = x_ref.shape[0]
        for flip in range(2):
            for a in range(copies // 2):
                to = (flip * (copies // 2) + a) * blk
                block = column_block(x_ref, blk, ctx_ref[0], flip, a)
                xt_ref[to : to + blk, at : at + rows] = block.T
        at += rows


def turn(ctx, xs, copies):
    width = xs[0].shape[1] - 128
    total = sum(x.shape[0] for x in xs)
    return pl.pallas_call(
        functools.partial(turn_kernel, copies),
        in_specs=[pl.BlockSpec(memory_space=pltpu.SMEM)]
        + [pl.BlockSpec(memory_space=pltpu.VMEM)] * len(xs),
        out_specs=pl.BlockSpec(memory_space=pltpu.VMEM),
        out_shape=jax.ShapeDtypeStruct((width, total), bf16),
        compiler_params=pltpu.CompilerParams(vmem_limit_bytes=60 << 20),
        cost_estimate=cost(2 * total * width, 4 * total * width),
        name="turn",
    )(ctx, *xs)


def in_grad_kernel(*refs):
    x_refs, (*gs, own_ref, other_ref) = refs[:4], refs[4:]
    grads = jnp.concatenate([g[0] for g in gs], axis=0)
    half = own_ref.shape[0]
    grad = mm(stack_refs(x_refs), grads, NN).astype(bf16)
    own_ref[...] = grad[:half]
    other_ref[...] = grad[half:]


def in_grad(xt, grads, first, count, tile=256):
    width, total = xt.shape
    steps = grads[0].shape[2] // tile
    half = jax.ShapeDtypeStruct((width // 2, count * tile), bf16)
    out = pl.BlockSpec((width // 2, tile), lambda f: (0, f))

    def at(f):
        return ((f + first) // steps, 0, (f + first) % steps)

    return pl.pallas_call(
        in_grad_kernel,
        grid=(count,),
        in_specs=[pl.BlockSpec((width // 4, total), lambda f, i=i: (i, 0)) for i in range(4)]
        + [pl.BlockSpec((1, g.shape[1], tile), at) for g in grads],
        out_specs=[out, out],
        out_shape=[half, half],
        compiler_params=pltpu.CompilerParams(vmem_limit_bytes=60 << 20),
        cost_estimate=cost(
            4 * total * width * count * tile, 2 * (total + width) * count * tile + 2 * total * width
        ),
        name="in_grad",
    )(*[xt] * 4, *grads)


def down_grad_kernel(copies, n, ctx_ref, *refs):
    ps, gates, (*hs, own_ref, other_ref, pg) = refs[:n], refs[n : 2 * n], refs[2 * n :]
    blk = ps[0].shape[1] // copies

    @pl.when(pl.program_id(0) == 0)
    def _():
        at = 0
        for p_ref, gate_ref in zip(ps, gates):
            rows = p_ref.shape[0]
            gate = gate_column([gate_ref])
            for flip in range(2):
                for a in range(copies // 2):
                    to = (flip * (copies // 2) + a) * blk
                    block = column_block(p_ref, blk, ctx_ref[0], flip, a).astype(f32)
                    pg[at : at + rows, to : to + blk] = (block * gate).astype(bf16)
            at += rows

    grad = mm(jnp.concatenate([h[...] for h in hs], axis=1), pg[...], NN).astype(bf16)
    for a in range(copies // 2):
        own_ref[a] = grad[:, a * blk : (a + 1) * blk]
        to = (copies // 2 + a) * blk
        other_ref[a] = grad[:, to : to + blk]


def down_grad(ctx, hs, ps, xs, copies, first, count, tile=256):
    ff = count * tile
    width = ps[0].shape[1]
    total = sum(h.shape[1] for h in hs)
    blk = width // copies
    half = jax.ShapeDtypeStruct((copies // 2, ff, blk), bf16)
    out = pl.BlockSpec((copies // 2, tile, blk), lambda f, c: (0, f, 0))
    return pl.pallas_call(
        functools.partial(down_grad_kernel, copies, len(ps)),
        grid_spec=pltpu.PrefetchScalarGridSpec(
            num_scalar_prefetch=1,
            grid=(count,),
            in_specs=[pl.BlockSpec(p.shape, lambda f, c: (0, 0)) for p in ps]
            + [gate_block(x, width) for x in xs]
            + [pl.BlockSpec((tile, h.shape[1]), lambda f, c: (f + first, 0)) for h in hs],
            out_specs=[out, out],
            scratch_shapes=[pltpu.VMEM((total, width), bf16)],
        ),
        out_shape=[half, half],
        compiler_params=pltpu.CompilerParams(vmem_limit_bytes=60 << 20),
        cost_estimate=cost(4 * total * width * ff, 2 * (total * (width + ff) + width * ff)),
        name="down_grad",
    )(ctx, *ps, *xs, *hs)


def project_kernel(x_ref, gain_ref, *refs):
    w_refs, (normed_t, *outs) = refs[:4], refs[4:]
    heads = len(outs)

    @pl.when((pl.program_id(0) == 0) & (pl.program_id(1) == 0))
    def _():
        x = x_ref[...].astype(f32)
        scale = lax.rsqrt(jnp.mean(x * x, axis=1, keepdims=True) + 1e-06)
        normed = (x * scale * gain_ref[...]).astype(bf16)
        normed_t[...] = normed.T

    cols = w_refs[0].shape[1]
    tok = normed_t.shape[1]
    rows = mm(stack_refs(w_refs), normed_t[...], TN).astype(bf16)
    rows = rows.reshape(cols // (heads * HEAD_DIM), heads, HEAD_DIM, tok)
    for h in range(heads):
        outs[h][:, 0] = rows[:, h]


def project(x, gain, weight, groups, heads, cols=512):
    tok, width = x.shape
    per = cols // (heads * HEAD_DIM)
    blocks = width // cols
    return pl.pallas_call(
        project_kernel,
        grid=(3, blocks),
        in_specs=[
            pl.BlockSpec((tok, width), lambda p, j: (0, 0)),
            pl.BlockSpec((1, width), lambda p, j: (0, 0)),
        ]
        + [
            pl.BlockSpec((width // 4, cols), lambda p, j, i=i: (i, p * blocks + j))
            for i in range(4)
        ],
        out_specs=[pl.BlockSpec((width, tok), lambda p, j: (0, 0))]
        + [pl.BlockSpec((per, 1, HEAD_DIM, tok), lambda p, j: (j, p, 0, 0))] * heads,
        out_shape=[jax.ShapeDtypeStruct((width, tok), bf16)]
        + [jax.ShapeDtypeStruct((groups, 3, HEAD_DIM, tok), bf16)] * heads,
        compiler_params=pltpu.CompilerParams(vmem_limit_bytes=60 << 20),
        cost_estimate=cost(6 * tok * width * width, 6 * width * width + 10 * tok * width),
        name="project",
    )(x, gain.reshape(1, width), *[weight] * 4)


def input_grad_kernel(steps, x_ref, gain_ref, mid_ref, *refs):
    w_refs, (*grads, out_ref, acc) = refs[:4], refs[4:]
    step = pl.program_id(0)
    cols = w_refs[0].shape[1]
    tok = out_ref.shape[0]

    @pl.when(step == 0)
    def _():
        acc[...] = jnp.zeros_like(acc)

    rows = jnp.stack([g[:, 0] for g in grads], axis=1).reshape(cols, tok)
    acc[...] += mm(stack_refs(w_refs), rows, NN)

    @pl.when(step == steps - 1)
    def _():
        x = x_ref[...].astype(f32)
        scale = lax.rsqrt(jnp.mean(x * x, axis=1, keepdims=True) + 1e-06)
        dy = acc[...].T * gain_ref[...]
        pull = jnp.mean(x * dy, axis=1, keepdims=True)
        out_ref[...] = mid_ref[...] + scale * dy - x * (scale * scale * scale * pull)


def input_gradient(x, gain, middle_grad, weight, grads, cols=512):
    tok, width = x.shape
    heads = len(grads)
    per = cols // (heads * HEAD_DIM)
    blocks = width // cols
    whole = pl.BlockSpec((tok, width), lambda s: (0, 0))
    return pl.pallas_call(
        functools.partial(input_grad_kernel, 3 * blocks),
        grid=(3 * blocks,),
        in_specs=[
            whole,
            pl.BlockSpec((1, width), lambda s: (0, 0)),
            whole,
        ]
        + [pl.BlockSpec((width // 4, cols), lambda s, i=i: (i, s)) for i in range(4)]
        + [
            pl.BlockSpec((per, 1, HEAD_DIM, tok), lambda s: (s % blocks, s // blocks, 0, 0))
            for _ in grads
        ],
        out_specs=whole,
        out_shape=jax.ShapeDtypeStruct((tok, width), f32),
        scratch_shapes=[pltpu.VMEM((width, tok), f32)],
        compiler_params=pltpu.CompilerParams(vmem_limit_bytes=60 << 20),
        cost_estimate=cost(6 * tok * width * width, 6 * width * width + 16 * tok * width),
        name="input_grad",
    )(x, gain.reshape(1, width), middle_grad, *[weight] * 4, *grads)


def wide_thirds(values):
    high = values.astype(bf16)
    rest = values - high.astype(f32)
    mid = rest.astype(bf16)
    low = (rest - mid.astype(f32)).astype(bf16)
    rows, lanes = values.shape
    blank = jnp.zeros((rows, 128 - 3 * lanes), bf16)
    return jnp.concatenate([high, mid, low, blank], axis=1)


def combine_kernel(
    counts, exp_ref, place_ref, ids_ref, probs_ref, middle_ref, cot_ref, normed_ref, gain_ref,
    router_ref, weight_ref, *refs,
):
    blocks, heads, parts, copies = counts
    experts = probs_ref.shape[1]
    backs, refs = refs[:blocks], refs[blocks:]
    row_grads, refs = refs[:blocks], refs[blocks:]
    mixed, refs = refs[:heads], refs[heads:]
    out_ref, mid_ref, refs = refs[0], refs[1], refs[2:]
    mixed_grads, refs = refs[:heads], refs[heads:]
    early, (slot_rows, slot_grads, wide) = refs[:parts], refs[parts:]
    tok, width = middle_ref.shape
    total = slot_rows.shape[0]

    at = 0
    for back, row_grad in zip(backs, row_grads):
        rows = slice(at, at + back.shape[0])
        slot_rows[rows, :] = back[...]
        slot_grads[rows, :] = row_grad[...]
        at += back.shape[0]

    slot = lax.broadcasted_iota(jnp.int32, (tok, total), 1)
    one = (slot == place_ref[:, 0:1]).astype(f32).astype(bf16)
    two = (slot == place_ref[:, 1:2]).astype(f32).astype(bf16)
    first = mm(one, slot_rows[...], NN)
    second = mm(two, slot_rows[...], NN)
    dy = mm(one + two, slot_grads[...], NN)

    lane = lax.broadcasted_iota(jnp.int32, (tok, experts), 1)
    is_first, is_second = lane == ids_ref[:, 0:1], lane == ids_ref[:, 1:2]
    probs = probs_ref[...]
    gate_first = jnp.sum(jnp.where(is_first, probs, 0.0), axis=1, keepdims=True)
    gate_second = jnp.sum(jnp.where(is_second, probs, 0.0), axis=1, keepdims=True)
    middle = middle_ref[...]
    cot = cot_ref[...].astype(f32)
    out_ref[...] = (middle + gate_first * first + gate_second * second).astype(bf16)
    grad_first = jnp.sum(cot * first, axis=1, keepdims=True)
    grad_second = jnp.sum(cot * second, axis=1, keepdims=True)
    probs_grad = jnp.where(is_first, grad_first, 0.0) + jnp.where(is_second, grad_second, 0.0)
    logits_grad = probs * (probs_grad - jnp.sum(probs * probs_grad, axis=1, keepdims=True))
    for e in range(experts):
        dy = dy + logits_grad[:, e : e + 1] * router_ref[e : e + 1, :]

    scale = lax.rsqrt(jnp.mean(middle * middle, axis=1, keepdims=True) + 1e-06)
    unit = middle * scale
    gain_terms = unit * dy
    dy = dy * gain_ref[...]
    middle_grad = cot + scale * (dy - unit * jnp.mean(unit * dy, axis=1, keepdims=True))
    mid_ref[...] = middle_grad
    branch = middle_grad.astype(bf16)

    groups, dim, _ = mixed_grads[0].shape
    back = mm(weight_ref[...], branch, NT).astype(bf16).reshape(groups, heads, dim, tok)
    for h in range(heads):
        mixed_grads[h][...] = back[:, h]
    for h in range(heads):
        grad = mm(mixed[h][...], branch, NN)
        for g in range(groups):
            at = (g * heads + h) * dim
            wide[at : at + dim, 0:width] = grad[g * dim : (g + 1) * dim]
    mark = lax.broadcasted_iota(jnp.int32, (tok, 128), 1) == 3 * experts
    mark = mark.astype(f32).astype(bf16)
    high = gain_terms.astype(bf16)
    low = (gain_terms - high.astype(f32)).astype(bf16)
    wide[:, width:] = (
        mm(normed_ref[...], wide_thirds(logits_grad), TN) + mm(high, mark, TN) + mm(low, mark, TN)
    )
    per = wide.shape[0] // (parts * copies)
    for d in range(parts):
        e = jnp.bitwise_xor(exp_ref[0], d)
        rows = [
            wide[pl.ds(pl.multiple_of((k * parts + e) * per, per), per), :] for k in range(copies)
        ]
        early[d][...] = jnp.concatenate(rows, axis=0).astype(bf16)


def combine(
    exp, place, ids, probs, middle, cot, normed, gain, router, weight, backs, row_grads, mixed,
    copies,
):
    tok, width = middle.shape
    heads = len(mixed)
    parts = probs.shape[1]
    groups = width // (heads * HEAD_DIM)
    total = sum(b.shape[0] for b in backs)
    sds = jax.ShapeDtypeStruct
    return pl.pallas_call(
        functools.partial(combine_kernel, (len(backs), heads, parts, copies)),
        in_specs=[pl.BlockSpec(memory_space=pltpu.SMEM)]
        + [pl.BlockSpec(memory_space=pltpu.VMEM)] * (9 + 2 * len(backs) + heads),
        out_specs=[pl.BlockSpec(memory_space=pltpu.VMEM)] * (2 + heads + parts),
        out_shape=[sds((tok, width), bf16), sds((tok, width), f32)]
        + [sds((groups, HEAD_DIM, tok), bf16)] * heads
        + [sds((width // parts, width + 128), bf16)] * parts,
        scratch_shapes=[
            pltpu.VMEM((total, width), bf16),
            pltpu.VMEM((total, width), bf16),
            pltpu.VMEM((width, width + 128), f32),
        ],
        compiler_params=pltpu.CompilerParams(vmem_limit_bytes=60 << 20),
        cost_estimate=cost(
            6 * tok * total * width + 4 * tok * width * width,
            4 * total * width + 18 * tok * width + 4 * width * width,
        ),
        name="combine",
    )(exp, place, ids, probs, middle, cot, normed, gain.reshape(1, width), router, weight,
      *backs, *row_grads, *mixed)


def finish_kernel(heads, lanes, n_ctx, exp_ref, rows_ref, weight_ref, gain_ref, grad_ref, gain_grad_ref, bias_ref):
    groups = rows_ref.shape[0]
    width = weight_ref.shape[1] // 3
    for part in range(3):
        pieces = []
        for g in range(groups):
            for h in range(heads):
                lo = h * lanes + part * HEAD_DIM
                pieces.append(rows_ref[g][:, lo : lo + HEAD_DIM].astype(f32))
        grad_ref[:, part * width : (part + 1) * width] = jnp.concatenate(pieces, axis=1)
    terms = weight_ref[...].astype(f32) * grad_ref[...]
    gain_grad_ref[...] = jnp.sum(terms, axis=1, keepdims=True) / gain_ref[...]
    columns = []
    for c in range(n_ctx):
        mine = rows_ref[exp_ref[0] * n_ctx + c].astype(f32)
        for h in range(heads):
            lo = h * lanes + 3 * HEAD_DIM
            columns.append(mine[:, lo : lo + 1])
    bias_ref[...] = jnp.concatenate(columns, axis=1)


def finish(exp, rows, weight_rows, gain_rows, heads, lanes, n_ctx):
    count, columns = weight_rows.shape
    sds = jax.ShapeDtypeStruct
    vmem = pl.BlockSpec(memory_space=pltpu.VMEM)
    return pl.pallas_call(
        functools.partial(finish_kernel, heads, lanes, n_ctx),
        in_specs=[pl.BlockSpec(memory_space=pltpu.SMEM), vmem, vmem, vmem],
        out_specs=[vmem, vmem, vmem],
        out_shape=[
            sds((count, columns), f32), sds((count, 1), f32), sds((count, heads * n_ctx), f32)
        ],
        cost_estimate=cost(4 * count * columns, 8 * count * columns),
        name="finish",
    )(exp, rows, weight_rows, gain_rows)


def route_kernel(heads, x_ref, place_ref, ids_ref, gain_ref, router_ref, weight_ref, *refs):
    mixed, (middle_ref, normed_ref, probs_ref, *slots, joined) = refs[:heads], refs[heads:]
    tok, width = x_ref.shape
    experts = probs_ref.shape[1]
    for h in range(heads):
        for g in range(width // (heads * HEAD_DIM)):
            at = (g * heads + h) * HEAD_DIM
            joined[at : at + HEAD_DIM, :] = mixed[h][g * HEAD_DIM : (g + 1) * HEAD_DIM, :]
    middle = x_ref[...].astype(f32) + mm(joined[...], weight_ref[...], TN)
    middle_ref[...] = middle
    scale = lax.rsqrt(jnp.mean(middle * middle, axis=1, keepdims=True) + 1e-06)
    normed = (middle * scale * gain_ref[...]).astype(bf16)
    normed_ref[...] = normed
    logits = mm(normed, router_ref[...], NN)[:, :experts]
    weights = jnp.exp(logits - jnp.max(logits, axis=1, keepdims=True))
    probs = weights / jnp.sum(weights, axis=1, keepdims=True)
    probs_ref[...] = probs
    lane = lax.broadcasted_iota(jnp.int32, (tok, experts), 1)
    gates = [
        wide_thirds(jnp.sum(jnp.where(lane == ids_ref[:, j : j + 1], probs, 0.0), axis=1, keepdims=True))
        for j in range(2)
    ]
    at = 0
    for slot_ref in slots:
        rows = slot_ref.shape[0]
        slot = lax.broadcasted_iota(jnp.int32, (rows, tok), 0) + at
        one = (slot == place_ref[0:1, :]).astype(f32).astype(bf16)
        two = (slot == place_ref[1:2, :]).astype(f32).astype(bf16)
        slot_ref[:, 0:width] = mm(one + two, normed, NN).astype(bf16)
        slot_ref[:, width:] = (mm(one, gates[0], NN) + mm(two, gates[1], NN)).astype(bf16)
        at += rows


def route(x, place, ids, gain, router, weight, mixed, sizes):
    tok, width = x.shape
    experts = router.shape[1]
    heads = len(mixed)
    sds = jax.ShapeDtypeStruct
    vmem = pl.BlockSpec(memory_space=pltpu.VMEM)
    return pl.pallas_call(
        functools.partial(route_kernel, heads),
        in_specs=[vmem] * (6 + heads),
        out_specs=[vmem] * (3 + len(sizes)),
        out_shape=[sds((tok, width), f32), sds((tok, width), bf16), sds((tok, experts), f32)]
        + [sds((size, width + 128), bf16) for size in sizes],
        scratch_shapes=[pltpu.VMEM((width, tok), bf16)],
        compiler_params=pltpu.CompilerParams(vmem_limit_bytes=60 << 20),
        cost_estimate=cost(
            2 * tok * width * (width + sum(sizes)), 12 * tok * width + 2 * width * width
        ),
        name="route",
    )(x, place.T, ids, gain.reshape(1, width), jnp.pad(router, ((0, 0), (0, 128 - experts))),
      weight, *mixed)


def sequence_grad_kernel(heads, n_exp, copies, dp_ref, *refs):
    outs, offsets, refs = refs[:heads], refs[heads : 2 * heads], refs[2 * heads :]
    normed_refs, (*shares, acc) = refs[:4], refs[4:]
    step = pl.program_id(0)
    width, lanes = acc.shape[0], acc.shape[1] // heads
    own = 3 * HEAD_DIM

    @pl.when(step == 0)
    def _():
        acc[...] = jnp.zeros_like(acc)

    normed = jnp.concatenate([ref[0] for ref in normed_refs], axis=0)
    for h, out_ref in enumerate(outs):
        rows = out_ref[0].reshape(own, out_ref.shape[3])
        acc[:, h * lanes : h * lanes + own] += mm(normed, rows, NT)

    @pl.when(step == pl.num_programs(0) - 1)
    def _():
        count = offsets[0].shape[0]
        buckets, rows_dev = count // copies, width // (copies * n_exp)
        row = lax.broadcasted_iota(jnp.int32, (width, count), 0)
        bucket = lax.broadcasted_iota(jnp.int32, (width, count), 1)
        place = row // (n_exp * rows_dev) * buckets + row % rows_dev
        here = ((place == bucket) & (row % rows_dev < buckets)).astype(f32).astype(bf16)
        base = own // 128 * 128
        lane = lax.broadcasted_iota(jnp.int32, (width, 128), 1) + base
        for h, offsets_ref in enumerate(offsets):
            table = jnp.sum(offsets_ref[...], axis=1, keepdims=True)
            column = jnp.sum(mm(here, wide_thirds(table), NN), axis=1, keepdims=True)
            at = h * lanes + base
            acc[:, at : at + 128] += jnp.where(lane == own, column, 0.0)
        per = shares[0].shape[0]
        for d, share in enumerate(shares):
            start = pl.multiple_of(jnp.bitwise_xor(dp_ref[0], d) * per, per)
            share[...] = acc[pl.ds(start, per), :].astype(bf16)


def sequence_grad(dp, normed, outs, offsets, n_dp, n_exp, copies, lanes):
    groups, _, dim, tok = outs[0].shape
    width = normed.shape[1]
    heads = len(outs)
    columns = heads * lanes
    return pl.pallas_call(
        functools.partial(sequence_grad_kernel, heads, n_exp, copies),
        grid_spec=pltpu.PrefetchScalarGridSpec(
            num_scalar_prefetch=1,
            grid=(groups,),
            in_specs=[pl.BlockSpec((1, 3, dim, tok), lambda g, d: (g, 0, 0, 0)) for _ in outs]
            + [pl.BlockSpec(o.shape, lambda g, d: (0, 0)) for o in offsets]
            + [
                pl.BlockSpec((1, width // 4, tok), lambda g, d, i=i: (g, i, 0)) for i in range(4)
            ],
            out_specs=[pl.BlockSpec((width // n_dp, columns), lambda g, d: (0, 0))] * n_dp,
            scratch_shapes=[pltpu.VMEM((width, columns), f32)],
        ),
        out_shape=[jax.ShapeDtypeStruct((width // n_dp, columns), bf16)] * n_dp,
        compiler_params=pltpu.CompilerParams(vmem_limit_bytes=60 << 20),
        cost_estimate=cost(
            6 * heads * dim * groups * tok * width, 2 * groups * tok * (width + 3 * heads * dim)
        ),
        name="sequence_grad",
    )(dp, *outs, *offsets, *[normed] * 4)


def dot_f32(left, right, left_dim, right_dim):
    return mm(left, right, (((left_dim,), (right_dim,)), ((), ())))


def swap_blocks(blocks, axes):
    return lax.all_to_all(blocks, axes, split_axis=0, concat_axis=0, tiled=True)


def exchange(parts, axis="expert"):
    n = len(parts)
    return [parts[0]] + [
        lax.ppermute(parts[d], axis, [(i, i ^ d) for i in range(n)]) for d in range(1, n)
    ]


def scatter_dp(rows):
    n = lax.axis_size("dp")
    shares = rows.reshape((n, rows.shape[0] // n) + rows.shape[1:])
    mine = lax.axis_index("dp")
    return exchange(
        [
            lax.dynamic_index_in_dim(shares, jnp.bitwise_xor(mine, d), 0, False)
            for d in range(n)
        ],
        "dp",
    )


def add_low(parts):
    return sum(part.astype(f32) for part in parts).astype(bf16)


def after(value, *others):
    return lax.optimization_barrier((value, others))[0]


def attention_plan(block_row, bucket_ids, blocks, tok):
    length = blocks * tok
    pad = jnp.full((1,), -1, jnp.int32)
    buck_rev = jnp.broadcast_to(jnp.concatenate([pad, bucket_ids[::-1]])[None], (8, 2 * length))
    buck = jnp.broadcast_to(jnp.concatenate([pad, bucket_ids])[None], (8, 2 * length))
    ids = jnp.arange(16)
    hot = (block_row[None, :] == ids[:, None]).astype(bf16)
    hide = jnp.where(ids[:, None] > block_row[None, :], HIDE, 0.0).astype(bf16)
    kmask_t = jnp.concatenate(
        [hot, jnp.ones((3, length), bf16), jnp.zeros((45, length), bf16)], axis=0
    )
    qmask = jnp.concatenate([hide, jnp.zeros((48, length), bf16)], axis=0)
    last = block_row.reshape(blocks, tok)[:, -1]
    seen = jnp.sum((block_row[None, :] <= last[:, None]).astype(jnp.int32), axis=1)
    return buck_rev, buck, kmask_t, qmask, hide, seen


def shards(
    layer_input,
    attn_gain,
    qkv_weight,
    out_weight,
    bias_table,
    moe_gain,
    router_weight,
    expert_in,
    expert_down,
    expert_ids,
    fill_order,
    block_ids,
    bucket_ids,
    cotangent,
):
    tok, width = layer_input.shape
    n_dp, n_ctx, n_exp = lax.axis_size("dp"), lax.axis_size("ctx"), lax.axis_size("expert")
    groups = n_ctx * n_exp
    copies = n_dp * n_ctx
    head_exp = bias_table.shape[1]
    heads = head_exp // n_ctx
    experts = router_weight.shape[1]
    ff_width = expert_down.shape[1]
    capacity = 5 * TOP * tok // (4 * experts)
    cut = (capacity // 2 + 15) // 16 * 16
    spans = ((0, cut), (cut, capacity))
    ctx_index = lax.axis_index("ctx")
    exp_index = lax.axis_index("expert")
    ctx_arg = ctx_index.astype(jnp.int32).reshape(1)
    pair = ("expert", "ctx")
    step_k = 1024

    def order(p):
        return (p % n_exp) * n_ctx + p // n_exp

    def in_swap_order(blocks):
        shape = blocks.shape
        return jnp.swapaxes(blocks.reshape((n_ctx, n_exp) + shape[1:]), 0, 1).reshape(shape)

    exp_arg = exp_index.astype(jnp.int32).reshape(1)
    normed_t, *parts = project(layer_input, attn_gain, qkv_weight, groups, heads)
    qkv = [swap_blocks(part, pair) for part in parts]
    table_dev = lax.dynamic_slice_in_dim(bias_table, ctx_index * heads, heads, 1)
    buck_rev, buck, kmask, qmask, hide, seen = attention_plan(
        block_ids[0], bucket_ids, groups, tok
    )
    chunks = (seen + step_k - 1) // step_k

    flat_ids = expert_ids.reshape(TOP * tok)
    fill_rank = fill_order.reshape(TOP * tok)
    same_expert = flat_ids[:, None] == flat_ids[None, :]
    earlier = fill_rank[None, :] < fill_rank[:, None]
    slot_of = jnp.sum((same_expert & earlier).astype(jnp.int32), axis=1)
    slots = slot_of.reshape(tok, TOP)
    part_at = jnp.where(slots < cut, 0, experts * cut - cut)
    stride = jnp.where(slots < cut, cut, capacity - cut)
    place = jnp.where(
        slots < capacity,
        part_at + jnp.bitwise_xor(expert_ids, exp_index) * stride + slots,
        -1,
    )
    sizes = [high - low for low, high in spans for _ in range(experts)]

    def to_slots(rows):
        parts, at = [], 0
        for size in sizes:
            slot = jnp.arange(at, at + size)[:, None]
            hot = (slot == place[None, :, 0]) | (slot == place[None, :, 1])
            parts.append(dot_f32(hot.astype(bf16), rows, 1, 0).astype(bf16))
            at += size
        return parts

    forward, mixed = [], []
    cot_slots = to_slots(cotangent)
    slots_a, slots_b = cot_slots[:experts], cot_slots[experts:]
    rows_dev = width // (n_dp * groups)
    my_rows = ((lax.axis_index("dp") * n_ctx + ctx_index) * n_exp + exp_index) * rows_dev
    weight_rows = lax.dynamic_slice_in_dim(qkv_weight, my_rows, rows_dev, 0)
    gain_rows = lax.dynamic_slice_in_dim(attn_gain, my_rows, rows_dev, 0).reshape(rows_dev, 1)
    qkv[0], place, slots_a, slots_b, buck_rev, buck, kmask, qmask, hide, weight_rows, gain_rows = (
        lax.optimization_barrier(
            (
                qkv[0], place, slots_a, slots_b, buck_rev, buck, kmask, qmask, hide, weight_rows,
                gain_rows,
            )
        )
    )
    normed_seq = lax.all_gather(after(normed_t, qkv[0]), pair)
    for h in range(heads):
        arg = after(qkv[h], forward)
        if h == heads - 1:
            grad_a = exchange(after(slots_a, arg))
        out = attention_fwd(
            order, chunks, table_dev[:, h], buck_rev, kmask, qmask, arg, step_k
        )
        out = after(out, qkv[h + 1] if h < heads - 1 else grad_a, mixed)
        forward.append(out)
        mixed.append(swap_blocks(out[0], pair).reshape(groups * HEAD_DIM, tok))
    mixed = after(mixed, forward)
    middle, normed_moe, probs, *sent = route(
        layer_input, place, expert_ids, moe_gain, router_weight, out_weight, mixed, sizes
    )
    x_a, x_b = exchange(sent[:experts]), exchange(sent[experts:])

    grad_b = exchange(after(slots_b, x_a))
    run_a = after(expert_fwd(x_a, expert_in, expert_down), x_b, grad_b)
    produced_a = exchange(list(run_a[3:]))
    run_b = expert_fwd(after(x_b, run_a), expert_in, expert_down)
    run_b = after(run_b, produced_a, normed_seq)
    produced_b = exchange(list(run_b[3:]))
    hidden = [run_a[0], run_b[0]]
    tiles = ff_width // 256
    cuts = (0, (tiles + 1) // 2, tiles)
    g_args = after(grad_a + grad_b, run_b)
    down_1 = down_grad(ctx_arg, hidden, g_args, x_a + x_b, copies, 0, cuts[1])

    def sum_dp(half):
        return lax.psum_scatter(half, "dp", scatter_dimension=0, tiled=True)

    def to_ctx(half):
        return lax.ppermute(half, "ctx", [(0, 1), (1, 0)])

    came = to_ctx(down_1[1])
    g_args = after(grad_a + grad_b, down_1)
    down_2 = down_grad(ctx_arg, hidden, g_args, x_a + x_b, copies, cuts[1], tiles - cuts[1])
    undo_a = expert_bwd(
        after(grad_a, down_2), x_a, run_a[1], run_a[2], expert_in, expert_down
    )
    undo_a, came = lax.optimization_barrier((after(undo_a, produced_b), came))
    halves = [add_low((down_1[0], came))]
    grads_a = exchange(list(undo_a[1:]))
    came = to_ctx(after(down_2[1], undo_a))
    undo_b = expert_bwd(
        after(grad_b, undo_a), x_b, run_b[1], run_b[2], expert_in, expert_down
    )
    undo_b, came = lax.optimization_barrier((after(undo_b, grads_a), came))
    halves.append(add_low((down_2[0], came)))
    grads_b = exchange(list(undo_b[1:]))
    grads_in = [undo_a[0], undo_b[0]]
    total = 2 * tiles
    size_a, size_d = total * 3 // 22, total * 8 // 22
    xt = turn(ctx_arg, x_a + x_b, copies)
    part_a = in_grad(after(xt, undo_b), grads_in, 0, size_a)
    came_a = to_ctx(after(part_a[1], halves[1]))
    part_b = in_grad(after(xt, part_a), grads_in, size_a, size_a)
    part_d = in_grad(after(xt, part_b), grads_in, 2 * size_a, size_d)

    part_d, grads_b, came_a = lax.optimization_barrier((part_d, grads_b, came_a))
    came_b = to_ctx(after(part_b[1], came_a))
    layer_output, middle_grad, *outs = combine(
        exp_arg, place, expert_ids, probs, middle, cotangent, normed_moe, moe_gain,
        router_weight.T.astype(f32), out_weight, produced_a + produced_b, grads_a + grads_b, mixed,
        copies,
    )
    down_sums = [sum_dp(half) for half in halves]
    outs, came_b, down_sums[0] = lax.optimization_barrier((outs, came_b, down_sums[0]))
    half_a = jnp.concatenate(
        [add_low((part_a[0], came_a)), add_low((part_b[0], came_b))], axis=1
    )
    first = 2 * size_a + size_d
    part_c = in_grad(after(xt, outs), grads_in, first, total - first)
    early = outs[heads:]
    mixed_grad = [swap_blocks(part, pair) for part in outs[:heads]]

    last_own, last_other = [sum_dp(half) for half in part_d]
    sum_a = sum_dp(half_a)

    lanes = -(-(3 * HEAD_DIM + 1) // 128) * 128
    dp_arg = lax.axis_index("dp").astype(jnp.int32).reshape(1)
    backward, grads = [], []
    for h in range(heads):
        arg = after(mixed_grad[h], backward if h else (part_c, half_a))
        beside = [grads[h - 1]] if h else []
        if h == 0:
            came_c = to_ctx(after(part_c[1], arg))
            early_parts = exchange(after(early, arg))
            beside += [came_c, early_parts, last_own, last_other, down_sums[1]] + mixed_grad[1:2]
        else:
            arg = after(arg, half_c)
        if h == heads - 1:
            last_came = to_ctx(after(last_other, arg))
            beside += [last_came, sum_a] + ([early_sums] if h else [])
        out = attention_bwd(
            order, chunks, table_dev[:, h], buck, kmask, hide, qkv[h], forward[h][0],
            arg, forward[h][1], step_k,
        )
        out, beside = lax.optimization_barrier((out, beside))
        if h == 0:
            half_c = add_low((part_c[0], beside[0]))
            sum_c = sum_dp(half_c)
            early_sums = scatter_dp(add_low(beside[1]))
        elif h == heads - 1:
            early_sums = beside[-1]
        backward.append(out)
        grads.append(swap_blocks(out[0], pair))
    shares = sequence_grad(
        dp_arg, normed_seq, [out[0] for out in backward], [out[1] for out in backward], n_dp,
        n_exp, copies, lanes,
    )
    late = exchange(shares, "dp")
    in_sums = [sum_a, add_low((last_own, after(last_came, backward))), sum_c]
    input_grad = input_gradient(layer_input, attn_gain, middle_grad, qkv_weight, grads)
    late, input_grad = lax.optimization_barrier((late, input_grad))
    late = add_low(late)
    rows_out = swap_blocks(in_swap_order(late.reshape(groups, rows_dev, -1)), pair)
    early_half = add_low(after(early_sums, backward)).reshape(n_ctx, rows_dev, width + 128)
    early_own, early_other = [
        lax.dynamic_index_in_dim(early_half, at, 0, False) for at in (ctx_index, 1 - ctx_index)
    ]
    early_rows = early_own.astype(f32) + lax.ppermute(
        early_other, "ctx", [(0, 1), (1, 0)]
    ).astype(f32)
    expert_in_grad = jnp.concatenate(in_sums, axis=1).astype(f32)
    expert_down_grad = jnp.concatenate(after(down_sums, backward), axis=1).astype(f32)
    rows_out, input_grad, expert_in_grad, expert_down_grad, early_rows = (
        lax.optimization_barrier(
            (rows_out, input_grad, expert_in_grad, expert_down_grad, early_rows)
        )
    )
    qkv_grad, attn_gain_grad, bias_rows = finish(
        exp_arg,
        rows_out,
        weight_rows,
        gain_rows,
        heads,
        lanes,
        n_ctx,
    )
    router_grad = sum(
        early_rows[:, width + i * experts : width + (i + 1) * experts] for i in range(3)
    )
    return (
        layer_output,
        input_grad,
        attn_gain_grad.reshape(rows_dev),
        qkv_grad,
        early_rows[:, :width],
        bias_rows[: bias_table.shape[0] // copies],
        early_rows[:, width + 3 * experts],
        router_grad,
        expert_in_grad[None],
        expert_down_grad,
    )


def solution(mesh):
    rows = P(("dp", "ctx", "expert"), None)
    return jax.shard_map(
        shards,
        mesh=mesh,
        in_specs=(
            rows,
            P(),
            P(),
            P(),
            P(None, "expert"),
            P(),
            P(),
            P("expert", None, None),
            P("expert", None, None),
            rows,
            rows,
            P("dp", None),
            P(),
            rows,
        ),
        out_specs=(
            rows,
            rows,
            P(("dp", "ctx", "expert")),
            rows,
            rows,
            P(("dp", "ctx"), "expert"),
            P(("dp", "ctx", "expert")),
            rows,
            P("expert", ("dp", "ctx"), None),
            P("expert", None, ("dp", "ctx")),
        ),
        check_vma=False,
    )
```
